256 devices in a mesh: station: 16 (over z, y_hi), group: 8 (over x, core), bias: 2 (over y_lo).
Axes of the slice: x: 4, y: 4 (y_hi: 2, y_lo: 2; y = y_hi * 2 + y_lo), z: 8, core: 2. Of those that a mesh axis runs over, the one named last changes fastest.
Arguments:
- normal_mat: float32 [1024, 2304], P(('station', 'group')), may hold values from -16 to 18, as said below
- coupling: float32 [1024, 2, 8, 48, 128], P(('station', 'group'), 'bias'), may hold values from -0.13258252 to 0.13258252
- lengths: int32 [1024], P(('station', 'group')), may hold values from 12 to 48
- visible: int32 [1024, 2, 8], P(('station', 'group'), 'bias'), may hold values from 0 to 16, as said below
- bias_prior: float32 [2, 16, 128], P('bias', 'station'), may hold values from 0.1 to 1
- unimod: int32 [1024, 2304], P(('station', 'group')), may hold values from -1 to 2, as said below
Outputs:
- bias_cov: float32 [2, 16, 128, 128], P('bias', 'station')
- amb_cov: float32 [1024, 2304], P(('station', 'group'))
The draws below stay inside these ranges and needn't reach their ends.
Inputs may be any that keep to these rules, and one draw needn't show every extreme that they name: `normal_mat`: each station's matrix, read as 48 x 48 row by row, is symmetric with all eigenvalues 1 or more. Each list visible[s, h] holds distinct block numbers below 16 in its first slots and the value 16 in its unused slots; every list has at least one block; in every draw the stations of some devices use all 8 slots. `unimod`: each station's matrix, read as 48 x 48 row by row, is a unit lower triangular times a unit upper triangular integer matrix; each row of the lower factor and each column of the upper factor holds at most one entry off the diagonal, -1 or 1; so every leading square block has determinant 1.
All inputs are finite; a program needn't handle non-finite values.
Results may differ from the reference program's by a relative error of at most 0.0003.
Values sent between devices are 32-bit elements; how exact they have to be, the bound alone decides.
A program may use at most 64 MiB of HBM per device.

```python
import math
import jax
import jax.numpy as jnp
from jax import lax

A = 48
BS = 128
VH = 8
S_DEV = 8
NHALF = 16
STATIONS = 1024


def draw_normal_mat(key, part):
    first_key = jax.random.fold_in(jax.random.fold_in(key, 11), 0)
    base = jnp.clip(jax.random.normal(first_key, (STATIONS, A, A), jnp.float32), -4.0, 4.0)
    lift = jax.random.uniform(jax.random.fold_in(key, 12), (STATIONS, A), jnp.float32, 0.0, 1.0)
    light_mean = (1 + VH // 2) / 2.0
    per_half = 0.25 * VH + 0.75 * light_mean
    per_block = STATIONS * per_half / NHALF
    mean_len = (A // 4 + A) / 2.0
    coupling_var = 1.0 / (2.0 * BS * VH)
    target = min(0.5, 0.9 / (per_block * mean_len * coupling_var))
    strength = target / (1.5 * (1.0 - target))
    gram = jnp.einsum('sab,scb->sac', base, base, precision=lax.Precision.HIGHEST) / A
    matrix = strength * (gram + lift[:, :, None] * jnp.eye(A, dtype=jnp.float32)) + jnp.eye(A, dtype=jnp.float32)
    return matrix.reshape(STATIONS, A * A)


def draw_visible(key, part):
    keys = jax.random.split(jax.random.fold_in(key, 21), 4)
    owners = STATIONS // S_DEV
    heavy = (jax.random.randint(keys[0], (owners,), 0, 4) == 0) | (jnp.arange(owners, dtype=jnp.int32) == jax.random.randint(keys[3], (), 0, owners))
    heavy = jnp.repeat(heavy, S_DEV)
    light = jax.random.randint(keys[1], (STATIONS, 2), 1, VH // 2 + 1)
    filled = jnp.where(heavy[:, None], VH, light)
    scores = jax.random.randint(keys[2], (STATIONS, 2, NHALF), 0, 65536) * NHALF + jnp.arange(NHALF, dtype=jnp.int32)
    ordered = jnp.argsort(scores, axis=-1)[..., :VH].astype(jnp.int32)
    slots = jnp.arange(VH, dtype=jnp.int32)
    return jnp.where(slots < filled[..., None], ordered, NHALF).astype(jnp.int32)


def factor_entries(pick_key, sign_key, live_key, positions):
    reach = jnp.maximum(positions, 1)
    picked = jax.random.randint(pick_key, (STATIONS, A), 0, 1 << 20) % reach
    signs = 2 * jax.random.randint(sign_key, (STATIONS, A), 0, 2) - 1
    live = jax.random.randint(live_key, (STATIONS, A), 0, 2) * (positions >= 1).astype(jnp.int32)
    return (picked.astype(jnp.int32), (signs * live).astype(jnp.int32))


def draw_unimod(key, part):
    keys = jax.random.split(jax.random.fold_in(key, 31), 6)
    positions = jnp.arange(A, dtype=jnp.int32)
    lower_pick, lower_value = factor_entries(keys[0], keys[1], keys[2], positions)
    upper_pick, upper_value = factor_entries(keys[3], keys[4], keys[5], positions)
    first = jnp.arange(STATIONS, dtype=jnp.int32)[:, None] == 0
    lower_value = jnp.where(first & (positions == 1), 1, lower_value)
    lower_value = jnp.where(first & (positions == 2), -1, lower_value)
    lower_pick = jnp.where(first & (positions == 2), 0, lower_pick)
    upper_value = jnp.where(first & (positions == 1), 1, upper_value)
    identity = jnp.eye(A, dtype=jnp.int32)
    lower = identity + lower_value[:, :, None] * (lower_pick[:, :, None] == positions).astype(jnp.int32)
    upper = identity + upper_value[:, None, :] * (upper_pick[:, None, :] == positions[:, None]).astype(jnp.int32)
    product = jnp.einsum('sab,sbc->sac', lower, upper)
    return product.reshape(STATIONS, A * A).astype(jnp.int32)


def place_ends(entries, key, low, high):
    spot = [jax.random.randint(jax.random.fold_in(key, axis), (), 0, length) for axis, length in enumerate(entries.shape)]
    widest = entries.shape.index(max(entries.shape))
    next_to = spot[:widest] + [(spot[widest] + 1) % entries.shape[widest]] + spot[widest + 1:]
    return entries.at[tuple(spot)].set(low).at[tuple(next_to)].set(high)


def shard_levels(stream_key, dims, cuts, low, top_value):
    level, own = 1.0, jax.random.fold_in(stream_key, 6)
    for axis_at, shards_of in cuts:
        heights = jnp.exp(jax.random.uniform(jax.random.fold_in(own, axis_at), (shards_of,), jnp.float32, low / len(cuts), top_value / len(cuts)))
        level = level * jnp.repeat(heights, dims[axis_at] // shards_of).reshape([-1 if axis == axis_at else 1 for axis in range(len(dims))])
    return level


def bell_draw(own_key, shape, width, bound, cuts=(), held_as=jnp.bfloat16):
    gain = shard_levels(own_key, shape, cuts, -0.22, 0.18) if cuts else 1.0
    result = jax.random.normal(own_key, shape, jnp.float32) * width * gain
    return jnp.minimum(jnp.maximum(result, -bound), bound).astype(held_as)


def setup_inputs(seed: int = 0) -> dict:
    key_of = jax.random.split(jax.random.key(seed), 7)
    normal_mat = draw_normal_mat(jax.random.fold_in(key_of[6], 71), 0)
    coupling = bell_draw(key_of[1], (STATIONS, 2, VH, A, BS), ((2 * BS * VH) ** -0.5), 0.13258252, ((0, 128), (1, 2)), jnp.float32)
    lengths = place_ends(jax.random.randint(key_of[2], (STATIONS,), A // 4, A + 1), jax.random.fold_in(key_of[2], 1), A // 4, A).astype(jnp.int32)
    visible = draw_visible(jax.random.fold_in(key_of[6], 71), 0)
    bias_prior = jnp.clip(jnp.exp(math.log(1.0) - 2.3025851 * jax.random.uniform(key_of[4], (2, NHALF, BS), jnp.float32) ** shard_levels(key_of[4], (2, NHALF, BS), ((0, 2), (1, 16)), -0.2, 0.2)), 0.1, 1.0)
    unimod = draw_unimod(jax.random.fold_in(key_of[6], 71), 0)
    return {"normal_mat": normal_mat, "coupling": coupling, "lengths": lengths, "visible": visible, "bias_prior": bias_prior, "unimod": unimod}


precise = lax.Precision.HIGHEST

def spd_inverse(matrix):
    matrix_order = matrix.shape[-1]
    factor = jnp.linalg.cholesky(matrix)
    identity = jnp.broadcast_to(jnp.eye(matrix_order, dtype=matrix.dtype), matrix.shape)
    lower_inv = lax.linalg.triangular_solve(factor, identity, left_side=True, lower=True)
    return jnp.einsum('...ka,...kb->...ab', lower_inv, lower_inv, precision=precise)

def prepare(normal_mat, coupling, lengths):
    stations = coupling.shape[0]
    block_len = coupling.shape[3]
    positions = jnp.arange(block_len, dtype=jnp.int32)
    row_valid = (positions[None, :] < lengths[:, None]).astype(jnp.float32)
    keep_mask = row_valid[:, :, None] * row_valid[:, None, :]
    stacked = normal_mat.reshape(stations, block_len, block_len)
    effective = keep_mask * stacked + (1.0 - keep_mask) * jnp.eye(block_len, dtype=jnp.float32)
    inverse = spd_inverse(effective)
    weighted = coupling * row_valid[:, None, None, :, None]
    solved = jnp.einsum('sab,shjbc->shjac', inverse, weighted, precision=precise)
    return (keep_mask, inverse, weighted, solved)

def reduced_terms(weighted, solved):
    return jnp.einsum('shjac,shjad->shjcd', weighted, weighted - solved, precision=precise)

def bias_share(solved, chosen):
    lifted = jnp.einsum('shjac,shjcd->shjad', solved, chosen, precision=precise)
    return jnp.einsum('shjad,shjbd->sab', lifted, solved, precision=precise)

def finish_cov(keep_mask, inverse, bias_part, unimod):
    stations = keep_mask.shape[0]
    block_len = keep_mask.shape[1]
    covariance = keep_mask * (inverse + bias_part)
    integer_map = unimod.reshape(stations, block_len, block_len).astype(jnp.float32)
    mapped = jnp.einsum('sab,sbc,sdc->sad', integer_map, covariance, integer_map, precision=precise)
    return (keep_mask * mapped).reshape(stations, block_len * block_len)

def reference(normal_mat, coupling, lengths, visible, bias_prior, unimod):
    stations = coupling.shape[0]
    block_width = coupling.shape[4]
    group_rows = math.gcd(stations, 64)
    block_count = stations // group_rows

    def split_rows(array):
        return array.reshape((block_count, group_rows) + array.shape[1:])
    columns = jnp.arange(NHALF, dtype=jnp.int32)

    def accumulate(running, pieces):
        normal_blk, couple_blk, length_blk, visible_blk = pieces
        keep_mask, inverse, weighted, solved = prepare(normal_blk, couple_blk, length_blk)
        selector = (visible_blk[..., None] == columns).astype(jnp.float32)
        reduced = reduced_terms(weighted, solved)
        return (running + jnp.einsum('shjx,shjcd->hxcd', selector, reduced, precision=precise), None)
    empty_table = jnp.zeros((2, NHALF, block_width, block_width), jnp.float32)
    block_table = lax.scan(accumulate, empty_table, (split_rows(normal_mat), split_rows(coupling), split_rows(lengths), split_rows(visible)))[0]
    bias_cov = spd_inverse(block_table + bias_prior[..., :, None] * jnp.eye(block_width, dtype=jnp.float32))

    def finish_block(pieces):
        normal_blk, couple_blk, length_blk, visible_blk, unimod_blk = pieces
        keep_mask, inverse, weighted, solved = prepare(normal_blk, couple_blk, length_blk)
        selector = (visible_blk[..., None] == columns).astype(jnp.float32)
        chosen = jnp.einsum('shjx,hxcd->shjcd', selector, bias_cov, precision=precise)
        return finish_cov(keep_mask, inverse, bias_share(solved, chosen), unimod_blk)
    amb_cov = lax.map(finish_block, (split_rows(normal_mat), split_rows(coupling), split_rows(lengths), split_rows(visible), split_rows(unimod)))
    return (bias_cov, amb_cov.reshape(stations, -1))
```

```python
import jax
import jax.numpy as jnp
from jax import lax
from jax.experimental import pallas as pl
from jax.experimental.pallas import tpu as pltpu
from jax.sharding import PartitionSpec as P

A = 48
BS = 128
VH = 8
S = 8
NH = 16
NST = 16
NG = 8
HALF = A // 2
MESH = pl.DeviceIdType.MESH
F32 = jnp.float32
BF16 = jnp.bfloat16
I32 = jnp.int32
VMEM_LIMIT = 48 * 1024 * 1024


def lanes_of(shape=(8, 128)):
    return lax.broadcasted_iota(I32, shape, 1)


def subs_of(shape=(8, 128)):
    return lax.broadcasted_iota(I32, shape, 0)


def pick(x, idx):
    return jnp.take_along_axis(x, idx, axis=1, mode="promise_in_bounds")


def split2(x):
    hi = x.astype(BF16)
    lo = (x - hi.astype(F32)).astype(BF16)
    return hi, lo


def inv2(m):
    (a, b), (c, d) = m
    r = 1.0 / (a * d - b * c)
    return [[d * r, -(b * r)], [-(c * r), a * r]]


def mul2(m, n):
    return [[m[i][0] * n[0][j] + m[i][1] * n[1][j] for j in range(2)] for i in range(2)]


def inv4(p):
    a = [[p[i][j] for j in range(2)] for i in range(2)]
    b = [[p[i][j + 2] for j in range(2)] for i in range(2)]
    c = [[p[i + 2][j] for j in range(2)] for i in range(2)]
    d = [[p[i + 2][j + 2] for j in range(2)] for i in range(2)]
    ai = inv2(a)
    t = mul2(ai, b)
    u = mul2(c, ai)
    ct = mul2(c, t)
    si = inv2([[d[i][j] - ct[i][j] for j in range(2)] for i in range(2)])
    ts = mul2(t, si)
    su = mul2(si, u)
    tsu = mul2(ts, u)
    out = [[None] * 4 for _ in range(4)]
    for i in range(2):
        for j in range(2):
            out[i][j] = ai[i][j] + tsu[i][j]
            out[i][j + 2] = -ts[i][j]
            out[i + 2][j] = -su[i][j]
            out[i + 2][j + 2] = si[i][j]
    return out


def scaled_rows(pinv, rows, col, k):
    inside = (col >= k) & (col < k + 4)
    rows = [jnp.where(inside, (col == k + q).astype(F32), rows[q]) for q in range(4)]
    out = []
    for q in range(4):
        out.append((pinv[q][0] * rows[0] + pinv[q][1] * rows[1]) + (pinv[q][2] * rows[2] + pinv[q][3] * rows[3]))
    return inside, out


def unpack_rows(ref, base):
    lane = lanes_of()
    vregs = [ref[:, 128 * v : 128 * (v + 1)] for v in range(18)]
    out = []
    for r in range(HALF):
        v, o = divmod(A * r, 128)

        def part(first, shift):
            head = vregs[first] if shift == 0 else pltpu.roll(vregs[first], shift, 1)
            return head

        low = part(v, (128 - o) % 128)
        high = part(v + 9, (192 - o) % 128)
        if o + A > 128:
            low = jnp.where(lane < 128 - o, low, part(v + 1, (128 - o) % 128))
            high = jnp.where(lane < 192 - o, high, part(v + 10, (192 - o) % 128))
        out.append(jnp.where(lane < 64, low, high))
    return out


def len_column(len_ref):
    sub = subs_of()
    out = jnp.zeros((8, 128), I32)
    for s in range(S):
        out = jnp.where(sub == s, len_ref[s], out)
    return out


def invert48(rows, lens):
    lane = lanes_of()
    col = lane & 63
    side = lane & 64
    m = []
    for r in range(HALF):
        row_id = jnp.where(lane < 64, r, r + HALF)
        m.append(jnp.where((row_id < lens) & (col < lens), rows[r], (col == row_id).astype(F32)))
    for k in range(0, A, 4):
        high = k >= HALF
        r0 = k % HALF
        base = 64 if high else 0
        dup = col + base
        piv = [m[r0 + q] for q in range(4)]
        p = [[pick(piv[q], jnp.full((8, 128), base + k + r, I32)) for r in range(4)] for q in range(4)]
        pinv = inv4(p)
        inside, rh = scaled_rows(pinv, [pick(piv[q], dup) for q in range(4)], col, k)
        idx = [side + (k + q) for q in range(4)]
        own_half = (lane >= 64) if high else (lane < 64)
        new = []
        for r in range(HALF):
            c = [pick(m[r], idx[q]) for q in range(4)]
            upd = (c[0] * rh[0] + c[1] * rh[1]) + (c[2] * rh[2] + c[3] * rh[3])
            v = jnp.where(inside, 0.0, m[r]) - upd
            if r0 <= r < r0 + 4:
                v = jnp.where(own_half, rh[r - r0], v)
            new.append(v)
        m = new
    return m


def to_stations(m, buf):
    for r in range(HALF):
        buf[8 * r : 8 * r + 8, :] = m[r]
        buf[8 * (r + HALF) : 8 * (r + HALF) + 8, :] = pltpu.roll(m[r], 64, 1)


def station(buf, s):
    return buf[pl.ds(s, A, stride=S), :][:, :A]


def k1_body(len_ref, vis_ref, nm_ref, cp_ref, table_ref, s_ref, inv_ref, buf, w2, v2, slot):
    for s in range(S):
        for x in range(NH + 1):
            slot[s, x] = VH
        for j in range(VH):
            slot[s, vis_ref[s, j]] = j
    lens = len_column(len_ref)
    m = invert48(unpack_rows(nm_ref, 0), lens)
    to_stations(m, buf)
    zeros = jnp.zeros((A, 2 * BS), BF16)
    for s in range(S):
        inv = station(buf, s)
        inv_ref[s] = inv
        lhs = jnp.concatenate(split2(inv), axis=0)
        keep = lax.broadcasted_iota(I32, (A, BS), 0) < len_ref[s]
        for j in range(VH):
            w = jnp.where(keep, cp_ref[s, j], 0.0)
            wp = jnp.concatenate(split2(w), axis=1)
            w2[s, j] = wp
            out = jnp.dot(lhs, wp, preferred_element_type=F32)
            out = out[:A] + out[A:]
            sol = out[:, :BS] + out[:, BS:]
            s_ref[s, j] = jnp.concatenate(split2(sol), axis=1)
            v2[s, j] = jnp.concatenate(split2(w - sol), axis=1)
        w2[s, VH] = zeros
        v2[s, VH] = zeros
        s_ref[s, VH] = zeros

    def per_block(x, carry):
        wx = jnp.concatenate([w2[s, slot[s, x]] for s in range(S)], axis=0)
        vx = jnp.concatenate([v2[s, slot[s, x]] for s in range(S)], axis=0)
        out = lax.dot_general(wx, vx, (((0,), (0,)), ((), ())), preferred_element_type=F32)
        out = out[:BS] + out[BS:]
        out = out[:, :BS] + out[:, BS:]
        for g in range(NG):
            table_ref[g, x] = out[16 * g : 16 * g + 16]
        return carry

    lax.fori_loop(0, NH, per_block, 0)


def invert128(mat):
    lane = lanes_of()
    sub = subs_of()

    def tile_step(t, m):
        m = list(m)
        for half in range(2):
            k = 8 * t + 4 * half
            o = 4 * half
            piv = m[0]
            rows = [jnp.broadcast_to(piv[o + q : o + q + 1, :], (8, 128)) for q in range(4)]
            at = [jnp.full((8, 128), 1, I32) * (k + q) for q in range(4)]
            p = [[pick(rows[q], at[r]) for r in range(4)] for q in range(4)]
            pinv = inv4(p)
            inside, rh = scaled_rows(pinv, rows, lane, k)
            new = []
            for i in range(16):
                c = [pick(m[i], at[q]) for q in range(4)]
                upd = (c[0] * rh[0] + c[1] * rh[1]) + (c[2] * rh[2] + c[3] * rh[3])
                v = jnp.where(inside, 0.0, m[i]) - upd
                if i == 0:
                    for q in range(4):
                        v = jnp.where(sub == o + q, rh[q], v)
                new.append(v)
            m = new
        return tuple(m[1:] + m[:1])

    return lax.fori_loop(0, 16, tile_step, tuple(mat))


def peer(axis, index):
    return {axis: index}


def k2_body(table_ref, prior_ref, cov_ref, call_ref, r1, part, r2, piece, blk, seg, own, s1, q1, s2, q2, s3, q3, s4, q4, s5, q5):
    me_g = lax.axis_index("group")
    me_s = lax.axis_index("station")
    gp = [lax.rem(me_g + d, NG) for d in range(1, NG)]
    sp = [lax.rem(me_s + d, NST) for d in range(1, NST)]
    barrier = pltpu.get_barrier_semaphore()
    for g in gp:
        pl.semaphore_signal(barrier, inc=1, device_id=peer("group", g), device_id_type=MESH)
    for s in sp:
        pl.semaphore_signal(barrier, inc=1, device_id=peer("station", s), device_id_type=MESH)
    pl.semaphore_wait(barrier, NG - 1 + NST - 1)

    def send(src, dst, ss, rs, axis, index):
        copy = pltpu.make_async_remote_copy(src_ref=src, dst_ref=dst, send_sem=ss, recv_sem=rs, device_id=peer(axis, index), device_id_type=MESH)
        copy.start()
        return copy

    def arrived(src, dst, ss, rs, axis, index):
        pltpu.make_async_remote_copy(src_ref=src, dst_ref=dst, send_sem=ss, recv_sem=rs, device_id=peer(axis, index), device_id_type=MESH).wait_recv()

    sent = [send(table_ref.at[g], r1.at[me_g], s1.at[g], q1.at[me_g], "group", g) for g in gp]
    total = table_ref[me_g]
    for g in gp:
        arrived(table_ref.at[g], r1.at[g], s1.at[g], q1.at[g], "group", g)
    for g in gp:
        total = total + r1[g]
    part[...] = total
    sent += [send(part.at[s], r2.at[me_s], s2.at[s], q2.at[me_s], "station", s) for s in sp]
    total = part[me_s]
    for s in sp:
        arrived(part.at[s], r2.at[s], s2.at[s], q2.at[s], "station", s)
    for s in sp:
        total = total + r2[s]
    piece[...] = total
    sent += [send(piece, blk.at[me_g], s3.at[g], q3.at[me_g], "group", g) for g in gp]
    blk[me_g] = total
    for g in gp:
        arrived(piece, blk.at[g], s3.at[g], q3.at[g], "group", g)
    lane = lanes_of()
    sub = subs_of()
    prior = jnp.broadcast_to(prior_ref[...], (8, 128))
    mat = []
    for i in range(16):
        tile = blk[i // 2, 8 * (i % 2) : 8 * (i % 2) + 8, :]
        mat.append(tile + jnp.where(lane == sub + 8 * i, prior, 0.0))
    mat = invert128(mat)
    for i in range(16):
        own[i // 2, 8 * (i % 2) : 8 * (i % 2) + 8, :] = mat[i]
        cov_ref[8 * i : 8 * i + 8, :] = mat[i]
    sent += [send(own.at[me_g], seg.at[me_s], s4.at[s], q4.at[me_s], "station", s) for s in sp]
    seg[me_s] = own[me_g]
    for s in sp:
        arrived(own.at[me_g], seg.at[s], s4.at[s], q4.at[s], "station", s)
    sent += [send(seg, call_ref.at[me_g], s5.at[g], q5.at[me_g], "group", g) for g in gp]
    call_ref[me_g] = seg[...]
    for g in gp:
        arrived(seg, call_ref.at[g], s5.at[g], q5.at[g], "group", g)
    for copy in sent:
        copy.wait_send()


def k3_body(len_ref, vis_ref, slot_ref, s_ref, call_ref, inv_ref, um_ref, out_ref, sx, lx, buf, mine, theirs, ss, rs):
    other = 1 - lax.axis_index("bias")
    barrier = pltpu.get_barrier_semaphore()
    pl.semaphore_signal(barrier, inc=1, device_id=peer("bias", other), device_id_type=MESH)

    for x in range(NH):
        sg = [s_ref[s, slot_ref[s, x]] for s in range(S)]
        c = jnp.concatenate([call_ref[g, x] for g in range(NG)], axis=0)
        c2 = jnp.concatenate(split2(c), axis=1)
        c4 = jnp.concatenate([c2, c2], axis=0)
        out = jnp.dot(jnp.concatenate(sg, axis=0), c4, preferred_element_type=F32)
        lift = out[:, :BS] + out[:, BS:]
        hi, lo = split2(lift)
        at = slice(BS * x, BS * x + BS)
        for s in range(S):
            sx[s, :A, at] = sg[s][:, :BS]
            sx[s, A:, at] = sg[s][:, BS:]
            lx[s, :A, at] = hi[A * s : A * s + A]
            lx[s, A:, at] = lo[A * s : A * s + A]
    for s in range(S):
        out = lax.dot_general(lx[s], sx[s], (((1,), (1,)), ((), ())), preferred_element_type=F32)
        out = out[:A] + out[A:]
        mine[s] = out[:, :A] + out[:, A:]
    pl.semaphore_wait(barrier, 1)
    copy = pltpu.make_async_remote_copy(src_ref=mine, dst_ref=theirs, send_sem=ss, recv_sem=rs, device_id=peer("bias", other), device_id_type=MESH)
    copy.start()
    um = unpack_rows(um_ref, 0)
    to_stations([z.astype(F32) for z in um], buf)
    zs = [station(buf, s).astype(BF16) for s in range(S)]
    copy.wait()
    ri = lax.broadcasted_iota(I32, (A, A), 0)
    ci = lax.broadcasted_iota(I32, (A, A), 1)
    for s in range(S):
        keep = (ri < len_ref[s]) & (ci < len_ref[s])
        cov = jnp.where(keep, inv_ref[s] + (mine[s] + theirs[s]), 0.0)
        hi, lo = split2(cov)
        t = jnp.dot(zs[s], hi, preferred_element_type=F32) + jnp.dot(zs[s], lo, preferred_element_type=F32)
        hi, lo = split2(t)
        nt = (((1,), (1,)), ((), ()))
        o = lax.dot_general(hi, zs[s], nt, preferred_element_type=F32) + lax.dot_general(lo, zs[s], nt, preferred_element_type=F32)
        o = jnp.where(keep, o, 0.0)
        buf[pl.ds(s, A, stride=S), :] = jnp.concatenate([o, jnp.zeros((A, 128 - A), F32)], axis=1)
    lane = lanes_of()
    acc = [None] * 18
    for i in range(A):
        v, o = divmod(A * i, 128)
        row = buf[8 * i : 8 * i + 8, :]
        row = pltpu.roll(row, o, 1) if o else row
        if o + A > 128:
            acc[v] = row * (lane >= o) if acc[v] is None else jnp.where(lane >= o, row, acc[v])
            acc[v + 1] = jnp.where(lane < o, row, 0.0)
        else:
            acc[v] = row if acc[v] is None else jnp.where(lane >= o, row, acc[v])
    for v in range(18):
        out_ref[:, 128 * v : 128 * v + 128] = acc[v]


def local(normal_mat, coupling, lengths, visible, bias_prior, unimod):
    visible = visible.reshape(S, VH)
    coupling = coupling.reshape(S, VH, A, BS)
    vm = pl.BlockSpec(memory_space=pltpu.VMEM)
    sm = pl.BlockSpec(memory_space=pltpu.SMEM)
    table, solved, inv, slot = pl.pallas_call(
        lambda l, v, n, c, t, s, i, slot, b, w2, v2: k1_body(l, v, n, c, t, s, i, b, w2, v2, slot),
        out_shape=(
            jax.ShapeDtypeStruct((NG, NH, 16, BS), F32),
            jax.ShapeDtypeStruct((S, VH + 1, A, 2 * BS), BF16),
            jax.ShapeDtypeStruct((S, A, A), F32),
            jax.ShapeDtypeStruct((S, NH + 1), I32),
        ),
        in_specs=[sm, sm, vm, vm],
        out_specs=(vm, vm, vm, sm),
        scratch_shapes=[
            pltpu.VMEM((A * S, 128), F32),
            pltpu.VMEM((S, VH + 1, A, 2 * BS), BF16),
            pltpu.VMEM((S, VH + 1, A, 2 * BS), BF16),
        ],
        compiler_params=pltpu.CompilerParams(vmem_limit_bytes=VMEM_LIMIT),
        name="local_terms",
    )(lengths, visible, normal_mat, coupling)
    dma = pltpu.SemaphoreType.DMA
    cov, call = pl.pallas_call(
        k2_body,
        out_shape=(
            jax.ShapeDtypeStruct((BS, BS), F32),
            jax.ShapeDtypeStruct((NG, NH, 16, BS), F32),
        ),
        in_specs=[vm, vm],
        out_specs=(vm, vm),
        scratch_shapes=[
            pltpu.VMEM((NG, NH, 16, BS), F32),
            pltpu.VMEM((NH, 16, BS), F32),
            pltpu.VMEM((NH, 16, BS), F32),
            pltpu.VMEM((16, BS), F32),
            pltpu.VMEM((NG, 16, BS), F32),
            pltpu.VMEM((NH, 16, BS), F32),
            pltpu.VMEM((NG, 16, BS), F32),
            dma((NG,)), dma((NG,)), dma((NST,)), dma((NST,)), dma((NG,)), dma((NG,)), dma((NST,)), dma((NST,)), dma((NG,)), dma((NG,)),
        ],
        compiler_params=pltpu.CompilerParams(vmem_limit_bytes=VMEM_LIMIT, collective_id=0, has_side_effects=True),
        name="block_cov",
    )(table, bias_prior.reshape(1, BS))
    amb = pl.pallas_call(
        k3_body,
        out_shape=jax.ShapeDtypeStruct((S, A * A), F32),
        in_specs=[sm, sm, sm, vm, vm, vm, vm],
        out_specs=vm,
        scratch_shapes=[
            pltpu.VMEM((S, 2 * A, NH * BS), BF16),
            pltpu.VMEM((S, 2 * A, NH * BS), BF16),
            pltpu.VMEM((A * S, 128), F32),
            pltpu.VMEM((S, A, A), F32),
            pltpu.VMEM((S, A, A), F32),
            dma(()), dma(()),
        ],
        compiler_params=pltpu.CompilerParams(vmem_limit_bytes=VMEM_LIMIT, collective_id=1, has_side_effects=True),
        name="amb_cov",
    )(lengths, visible, slot, solved, call, inv, unimod)
    return (cov.reshape(1, 1, BS, BS), amb)


def solution(mesh):
    return jax.shard_map(
        local,
        mesh=mesh,
        in_specs=(
            P(("station", "group"), None),
            P(("station", "group"), "bias", None, None, None),
            P(("station", "group")),
            P(("station", "group"), "bias", None),
            P("bias", "station", None),
            P(("station", "group"), None),
        ),
        out_specs=(P("bias", "station", None, None), P(("station", "group"), None)),
        check_vma=False,
    )
```

```python
import jax
import jax.numpy as jnp
from jax import lax
from jax.experimental import pallas as pl
from jax.experimental.pallas import tpu as pltpu
from jax.sharding import PartitionSpec as P

A = 48
BS = 128
VH = 8
S = 8
NH = 16
NST = 16
NG = 8
HALF = A // 2
MESH = pl.DeviceIdType.MESH
F32 = jnp.float32
BF16 = jnp.bfloat16
I32 = jnp.int32
VMEM_LIMIT = 48 * 1024 * 1024


def lanes_of(shape=(8, 128)):
    return lax.broadcasted_iota(I32, shape, 1)


def subs_of(shape=(8, 128)):
    return lax.broadcasted_iota(I32, shape, 0)


def pick(x, idx):
    return jnp.take_along_axis(x, idx, axis=1, mode="promise_in_bounds")


def split2(x):
    hi = x.astype(BF16)
    lo = (x - hi.astype(F32)).astype(BF16)
    return hi, lo


def inv2(m):
    (a, b), (c, d) = m
    r = 1.0 / (a * d - b * c)
    return [[d * r, -(b * r)], [-(c * r), a * r]]


def mul2(m, n):
    return [[m[i][0] * n[0][j] + m[i][1] * n[1][j] for j in range(2)] for i in range(2)]


def inv4(p):
    a = [[p[i][j] for j in range(2)] for i in range(2)]
    b = [[p[i][j + 2] for j in range(2)] for i in range(2)]
    c = [[p[i + 2][j] for j in range(2)] for i in range(2)]
    d = [[p[i + 2][j + 2] for j in range(2)] for i in range(2)]
    ai = inv2(a)
    t = mul2(ai, b)
    u = mul2(c, ai)
    ct = mul2(c, t)
    si = inv2([[d[i][j] - ct[i][j] for j in range(2)] for i in range(2)])
    ts = mul2(t, si)
    su = mul2(si, u)
    tsu = mul2(ts, u)
    out = [[None] * 4 for _ in range(4)]
    for i in range(2):
        for j in range(2):
            out[i][j] = ai[i][j] + tsu[i][j]
            out[i][j + 2] = -ts[i][j]
            out[i + 2][j] = -su[i][j]
            out[i + 2][j + 2] = si[i][j]
    return out


def scaled_rows(pinv, rows, col, k):
    inside = (col >= k) & (col < k + 4)
    rows = [jnp.where(inside, (col == k + q).astype(F32), rows[q]) for q in range(4)]
    out = []
    for q in range(4):
        out.append((pinv[q][0] * rows[0] + pinv[q][1] * rows[1]) + (pinv[q][2] * rows[2] + pinv[q][3] * rows[3]))
    return inside, out


def unpack_rows(ref, base):
    lane = lanes_of()
    vregs = [ref[:, 128 * v : 128 * (v + 1)] for v in range(18)]
    out = []
    for r in range(HALF):
        v, o = divmod(A * r, 128)

        def part(first, shift):
            head = vregs[first] if shift == 0 else pltpu.roll(vregs[first], shift, 1)
            return head

        low = part(v, (128 - o) % 128)
        high = part(v + 9, (192 - o) % 128)
        if o + A > 128:
            low = jnp.where(lane < 128 - o, low, part(v + 1, (128 - o) % 128))
            high = jnp.where(lane < 192 - o, high, part(v + 10, (192 - o) % 128))
        out.append(jnp.where(lane < 64, low, high))
    return out


def len_column(len_ref):
    sub = subs_of()
    out = jnp.zeros((8, 128), I32)
    for s in range(S):
        out = jnp.where(sub == s, len_ref[s], out)
    return out


def invert48(rows, lens):
    lane = lanes_of()
    col = lane & 63
    side = lane & 64
    m = []
    for r in range(HALF):
        row_id = jnp.where(lane < 64, r, r + HALF)
        m.append(jnp.where((row_id < lens) & (col < lens), rows[r], (col == row_id).astype(F32)))
    for k in range(0, A, 4):
        high = k >= HALF
        r0 = k % HALF
        base = 64 if high else 0
        dup = col + base
        piv = [m[r0 + q] for q in range(4)]
        p = [[pick(piv[q], jnp.full((8, 128), base + k + r, I32)) for r in range(4)] for q in range(4)]
        pinv = inv4(p)
        inside, rh = scaled_rows(pinv, [pick(piv[q], dup) for q in range(4)], col, k)
        idx = [side + (k + q) for q in range(4)]
        own_half = (lane >= 64) if high else (lane < 64)
        new = []
        for r in range(HALF):
            c = [pick(m[r], idx[q]) for q in range(4)]
            upd = (c[0] * rh[0] + c[1] * rh[1]) + (c[2] * rh[2] + c[3] * rh[3])
            v = jnp.where(inside, 0.0, m[r]) - upd
            if r0 <= r < r0 + 4:
                v = jnp.where(own_half, rh[r - r0], v)
            new.append(v)
        m = new
    return m


def to_stations(m, buf):
    for r in range(HALF):
        buf[8 * r : 8 * r + 8, :] = m[r]
        buf[8 * (r + HALF) : 8 * (r + HALF) + 8, :] = pltpu.roll(m[r], 64, 1)


def station(buf, s):
    return buf[pl.ds(s, A, stride=S), :][:, :A]


def invert128(mat):
    lane = lanes_of()
    sub = subs_of()
    m = list(mat)
    for k in range(0, BS, 4):
        t, o = divmod(k, 8)
        rows = [jnp.broadcast_to(m[t][o + q : o + q + 1, :], (8, 128)) for q in range(4)]
        at = [jnp.full((8, 128), k + q, I32) for q in range(4)]
        p = [[pick(rows[q], at[r]) for r in range(4)] for q in range(4)]
        inside, rh = scaled_rows(inv4(p), rows, lane, k)
        new = []
        for i in range(16):
            c = [pick(m[i], at[q]) for q in range(4)]
            upd = (c[0] * rh[0] + c[1] * rh[1]) + (c[2] * rh[2] + c[3] * rh[3])
            v = jnp.where(inside, 0.0, m[i]) - upd
            if i == t:
                for q in range(4):
                    v = jnp.where(sub == o + q, rh[q], v)
            new.append(v)
        m = new
    return m


def peer(axis, index):
    return {axis: index}


CH = 4
XC = NH // CH


def body(len_ref, vis_ref, prior_ref, nm_hbm, cp_hbm, um_hbm, cov_ref, amb_ref,
         nm, cp, um, buf, w2, v2, s2, slot, invs, table, r1, part, r2, piece, blk, seg, own, call, sx, lx, mine, theirs,
         loc, s1, q1, s2s, q2, s3, q3, s4, q4, s5, q5, s6, q6):
    me_g = lax.axis_index("group")
    me_s = lax.axis_index("station")
    me_b = lax.axis_index("bias")
    gp = [lax.rem(me_g + d, NG) for d in (1, 7, 2, 6, 3, 5, 4)]
    sp = [lax.rem(me_s + d, NST) for d in (8, 9, 7, 6, 10, 5, 11, 4, 12, 3, 13, 2, 14, 1, 15)]
    nm_copy = pltpu.make_async_copy(nm_hbm, nm, loc.at[0])
    nm_copy.start()
    cp_copy = [pltpu.make_async_copy(cp_hbm.at[s], cp.at[s], loc.at[2 + s]) for s in range(S)]
    for c in cp_copy:
        c.start()
    um_copy = pltpu.make_async_copy(um_hbm, um, loc.at[1])
    um_copy.start()
    barrier = pltpu.get_barrier_semaphore()
    for g in gp:
        pl.semaphore_signal(barrier, inc=1, device_id=peer("group", g), device_id_type=MESH)
    for s in sp:
        pl.semaphore_signal(barrier, inc=1, device_id=peer("station", s), device_id_type=MESH)
    pl.semaphore_signal(barrier, inc=1, device_id=peer("bias", 1 - me_b), device_id_type=MESH)

    def remote(src, dst, ss, rs, axis, index):
        return pltpu.make_async_remote_copy(src_ref=src, dst_ref=dst, send_sem=ss, recv_sem=rs, device_id=peer(axis, index), device_id_type=MESH)

    sent = []

    def send(*args):
        copy = remote(*args)
        copy.start()
        sent.append(copy)

    def arrived(*args):
        remote(*args).wait_recv()

    lens = len_column(len_ref)
    nm_copy.wait()
    to_stations(invert48(unpack_rows(nm, 0), lens), buf)
    zeros = jnp.zeros((A, 2 * BS), BF16)
    for s in range(S):
        inv = station(buf, s)
        invs[s] = inv
        lhs = jnp.concatenate(split2(inv), axis=0)
        keep = lax.broadcasted_iota(I32, (A, BS), 0) < len_ref[s]
        cp_copy[s].wait()
        for j in range(VH):
            w = jnp.where(keep, cp[s, j], 0.0)
            wp = jnp.concatenate(split2(w), axis=1)
            w2[s, j] = wp
            out = jnp.dot(lhs, wp, preferred_element_type=F32)
            out = out[:A] + out[A:]
            sol = out[:, :BS] + out[:, BS:]
            s2[s, j] = jnp.concatenate(split2(sol), axis=1)
            v2[s, j] = jnp.concatenate(split2(w - sol), axis=1)
        w2[s, VH] = zeros
        v2[s, VH] = zeros
        s2[s, VH] = zeros

    for ch in range(CH):
        for x in range(XC * ch, XC * ch + XC):
            at = []
            for s in range(S):
                j = jnp.int32(VH)
                for jj in range(VH):
                    j = jnp.where(vis_ref[s, jj] == x, jj, j)
                slot[s, x] = j
                at.append(j)
            wx = jnp.concatenate([w2[s, at[s]] for s in range(S)], axis=0)
            vx = jnp.concatenate([v2[s, at[s]] for s in range(S)], axis=0)
            out = lax.dot_general(wx, vx, (((0,), (0,)), ((), ())), preferred_element_type=F32)
            out = out[:BS] + out[BS:]
            out = out[:, :BS] + out[:, BS:]
            for g in range(NG):
                table[g, x] = out[16 * g : 16 * g + 16]
        if ch == 0:
            pl.semaphore_wait(barrier, NG - 1 + NST - 1 + 1)
        xs = pl.ds(XC * ch, XC)
        for g in gp:
            send(table.at[g, xs], r1.at[me_g, xs], s1.at[ch, g], q1.at[ch, me_g], "group", g)
    for ch in range(CH):
        xs = pl.ds(XC * ch, XC)
        total = table[me_g, xs]
        for g in gp:
            arrived(table.at[g, xs], r1.at[g, xs], s1.at[ch, g], q1.at[ch, g], "group", g)
        for g in gp:
            total = total + r1[g, xs]
        part[xs] = total
    for s in sp:
        send(part.at[s], r2.at[me_s], s2s.at[s], q2.at[me_s], "station", s)
    total = part[me_s]
    for s in sp:
        arrived(part.at[s], r2.at[s], s2s.at[s], q2.at[s], "station", s)
    for s in sp:
        total = total + r2[s]
    piece[...] = total
    for g in gp:
        send(piece, blk.at[me_g], s3.at[g], q3.at[me_g], "group", g)
    blk[me_g] = total
    for g in gp:
        arrived(piece, blk.at[g], s3.at[g], q3.at[g], "group", g)
    lane = lanes_of()
    sub = subs_of()
    prior = jnp.broadcast_to(prior_ref[...], (8, 128))
    mat = []
    for i in range(16):
        tile = blk[i // 2, 8 * (i % 2) : 8 * (i % 2) + 8, :]
        mat.append(tile + jnp.where(lane == sub + 8 * i, prior, 0.0))
    mat = invert128(mat)
    for i in range(16):
        own[i // 2, 8 * (i % 2) : 8 * (i % 2) + 8, :] = mat[i]
        cov_ref[8 * i : 8 * i + 8, :] = mat[i]
    for s in sp:
        send(own.at[me_g], seg.at[me_s], s4.at[s], q4.at[me_s], "station", s)
    seg[me_s] = own[me_g]
    um_copy.wait()
    to_stations([z.astype(F32) for z in unpack_rows(um, 0)], buf)
    zs = [station(buf, s).astype(BF16) for s in range(S)]
    for s in sp:
        arrived(own.at[me_g], seg.at[s], s4.at[s], q4.at[s], "station", s)
    for ch in range(CH):
        xs = pl.ds(XC * ch, XC)
        for g in gp:
            send(seg.at[xs], call.at[me_g, xs], s5.at[ch, g], q5.at[ch, me_g], "group", g)
    call[me_g] = seg[...]
    for ch in range(CH):
        xs = pl.ds(XC * ch, XC)
        for g in gp:
            arrived(seg.at[xs], call.at[g, xs], s5.at[ch, g], q5.at[ch, g], "group", g)
        for x in range(XC * ch, XC * ch + XC):
            sg = [s2[s, slot[s, x]] for s in range(S)]
            c = jnp.concatenate([call[g, x] for g in range(NG)], axis=0)
            c2 = jnp.concatenate(split2(c), axis=1)
            c4 = jnp.concatenate([c2, c2], axis=0)
            out = jnp.dot(jnp.concatenate(sg, axis=0), c4, preferred_element_type=F32)
            hi, lo = split2(out[:, :BS] + out[:, BS:])
            at = slice(BS * x, BS * x + BS)
            for s in range(S):
                sx[s, :A, at] = sg[s][:, :BS]
                sx[s, A:, at] = sg[s][:, BS:]
                lx[s, :A, at] = hi[A * s : A * s + A]
                lx[s, A:, at] = lo[A * s : A * s + A]
    nt = (((1,), (1,)), ((), ()))
    for s in range(S):
        out = lax.dot_general(lx[s], sx[s], nt, preferred_element_type=F32)
        out = out[:A] + out[A:]
        mine[s] = out[:, :A] + out[:, A:]
    send(mine, theirs, s6, q6, "bias", 1 - me_b)
    arrived(mine, theirs, s6, q6, "bias", 1 - me_b)
    ri = lax.broadcasted_iota(I32, (A, A), 0)
    ci = lax.broadcasted_iota(I32, (A, A), 1)
    for s in range(S):
        keep = (ri < len_ref[s]) & (ci < len_ref[s])
        cov = jnp.where(keep, invs[s] + (mine[s] + theirs[s]), 0.0)
        hi, lo = split2(cov)
        t = jnp.dot(zs[s], hi, preferred_element_type=F32) + jnp.dot(zs[s], lo, preferred_element_type=F32)
        hi, lo = split2(t)
        o = lax.dot_general(hi, zs[s], nt, preferred_element_type=F32) + lax.dot_general(lo, zs[s], nt, preferred_element_type=F32)
        o = jnp.where(keep, o, 0.0)
        buf[pl.ds(s, A, stride=S), :] = jnp.concatenate([o, jnp.zeros((A, 128 - A), F32)], axis=1)
    acc = [None] * 18
    for i in range(A):
        v, o = divmod(A * i, 128)
        row = buf[8 * i : 8 * i + 8, :]
        row = pltpu.roll(row, o, 1) if o else row
        acc[v] = row if acc[v] is None else jnp.where(lane >= o, row, acc[v])
        if o + A > 128:
            acc[v + 1] = row
    for v in range(18):
        amb_ref[:, 128 * v : 128 * v + 128] = acc[v]
    for copy in sent:
        copy.wait_send()


def local(normal_mat, coupling, lengths, visible, bias_prior, unimod):
    vm = pl.BlockSpec(memory_space=pltpu.VMEM)
    sm = pl.BlockSpec(memory_space=pltpu.SMEM)
    hb = pl.BlockSpec(memory_space=pltpu.HBM)
    dma = pltpu.SemaphoreType.DMA
    vmem = pltpu.VMEM
    slots = vmem((S, VH + 1, A, 2 * BS), BF16)
    wide = vmem((S, 2 * A, NH * BS), BF16)
    full = vmem((NG, NH, 16, BS), F32)
    row = vmem((NH, 16, BS), F32)
    cov, amb = pl.pallas_call(
        body,
        out_shape=(jax.ShapeDtypeStruct((BS, BS), F32), jax.ShapeDtypeStruct((S, A * A), F32)),
        in_specs=[sm, sm, vm, hb, hb, hb],
        out_specs=(vm, vm),
        scratch_shapes=[
            vmem((S, A * A), F32),
            vmem((S, VH, A, BS), F32),
            vmem((S, A * A), I32),
            vmem((A * S, 128), F32),
            slots, slots, slots,
            pltpu.SMEM((S, NH), I32),
            vmem((S, A, A), F32),
            full, full,
            row, row,
            vmem((16, BS), F32),
            vmem((NG, 16, BS), F32),
            row,
            vmem((NG, 16, BS), F32),
            full,
            wide, wide,
            vmem((S, A, A), F32), vmem((S, A, A), F32),
            dma((2 + S,)),
            dma((CH, NG)), dma((CH, NG)), dma((NST,)), dma((NST,)), dma((NG,)), dma((NG,)),
            dma((NST,)), dma((NST,)), dma((CH, NG)), dma((CH, NG)), dma(()), dma(()),
        ],
        compiler_params=pltpu.CompilerParams(vmem_limit_bytes=VMEM_LIMIT, collective_id=0, has_side_effects=True),
        name="epoch",
    )(
        lengths,
        visible.reshape(S, VH),
        bias_prior.reshape(1, BS),
        normal_mat,
        coupling.reshape(S, VH, A, BS),
        unimod,
    )
    return (cov.reshape(1, 1, BS, BS), amb)


def solution(mesh):
    return jax.shard_map(
        local,
        mesh=mesh,
        in_specs=(
            P(("station", "group"), None),
            P(("station", "group"), "bias", None, None, None),
            P(("station", "group")),
            P(("station", "group"), "bias", None),
            P("bias", "station", None),
            P(("station", "group"), None),
        ),
        out_specs=(P("bias", "station", None, None), P(("station", "group"), None)),
        check_vma=False,
    )
```

```python
import jax
import jax.numpy as jnp
from jax import lax
from jax.experimental import pallas as pl
from jax.experimental.pallas import tpu as pltpu
from jax.sharding import PartitionSpec as P

A = 48
BS = 128
VH = 8
S = 8
NH = 16
NST = 16
NG = 8
HALF = A // 2
MESH = pl.DeviceIdType.MESH
F32 = jnp.float32
BF16 = jnp.bfloat16
I32 = jnp.int32
VMEM_LIMIT = 63 * 1024 * 1024


def lanes_of(shape=(8, 128)):
    return lax.broadcasted_iota(I32, shape, 1)


def subs_of(shape=(8, 128)):
    return lax.broadcasted_iota(I32, shape, 0)


def pick(x, idx):
    return jnp.take_along_axis(x, idx, axis=1, mode="promise_in_bounds")


def split2(x):
    hi = x.astype(BF16)
    lo = (x - hi.astype(F32)).astype(BF16)
    return hi, lo


def inv2(m):
    (a, b), (c, d) = m
    r = 1.0 / (a * d - b * c)
    return [[d * r, -(b * r)], [-(c * r), a * r]]


def mul2(m, n):
    return [[m[i][0] * n[0][j] + m[i][1] * n[1][j] for j in range(2)] for i in range(2)]


def inv4(p):
    a = [[p[i][j] for j in range(2)] for i in range(2)]
    b = [[p[i][j + 2] for j in range(2)] for i in range(2)]
    c = [[p[i + 2][j] for j in range(2)] for i in range(2)]
    d = [[p[i + 2][j + 2] for j in range(2)] for i in range(2)]
    ai = inv2(a)
    t = mul2(ai, b)
    u = mul2(c, ai)
    ct = mul2(c, t)
    si = inv2([[d[i][j] - ct[i][j] for j in range(2)] for i in range(2)])
    ts = mul2(t, si)
    su = mul2(si, u)
    tsu = mul2(ts, u)
    out = [[None] * 4 for _ in range(4)]
    for i in range(2):
        for j in range(2):
            out[i][j] = ai[i][j] + tsu[i][j]
            out[i][j + 2] = -ts[i][j]
            out[i + 2][j] = -su[i][j]
            out[i + 2][j + 2] = si[i][j]
    return out


def scaled_rows(pinv, rows, col, k):
    inside = (col >= k) & (col < k + 4)
    rows = [jnp.where(inside, (col == k + q).astype(F32), rows[q]) for q in range(4)]
    out = []
    for q in range(4):
        out.append((pinv[q][0] * rows[0] + pinv[q][1] * rows[1]) + (pinv[q][2] * rows[2] + pinv[q][3] * rows[3]))
    return inside, out


def unpack_rows(ref, base):
    lane = lanes_of()
    vregs = [ref[:, 128 * v : 128 * (v + 1)] for v in range(18)]
    out = []
    for r in range(HALF):
        v, o = divmod(A * r, 128)

        def part(first, shift):
            head = vregs[first] if shift == 0 else pltpu.roll(vregs[first], shift, 1)
            return head

        low = part(v, (128 - o) % 128)
        high = part(v + 9, (192 - o) % 128)
        if o + A > 128:
            low = jnp.where(lane < 128 - o, low, part(v + 1, (128 - o) % 128))
            high = jnp.where(lane < 192 - o, high, part(v + 10, (192 - o) % 128))
        out.append(jnp.where(lane < 64, low, high))
    return out


def len_column(len_ref):
    sub = subs_of()
    out = jnp.zeros((8, 128), I32)
    for s in range(S):
        out = jnp.where(sub == s, len_ref[s], out)
    return out


def invert48(rows, lens):
    lane = lanes_of()
    col = lane & 63
    side = lane & 64
    m = []
    for r in range(HALF):
        row_id = jnp.where(lane < 64, r, r + HALF)
        m.append(jnp.where((row_id < lens) & (col < lens), rows[r], (col == row_id).astype(F32)))
    for k in range(0, A, 4):
        high = k >= HALF
        r0 = k % HALF
        base = 64 if high else 0
        dup = col + base
        piv = [m[r0 + q] for q in range(4)]
        p = [[pick(piv[q], jnp.full((8, 128), base + k + r, I32)) for r in range(4)] for q in range(4)]
        pinv = inv4(p)
        inside, rh = scaled_rows(pinv, [pick(piv[q], dup) for q in range(4)], col, k)
        idx = [side + (k + q) for q in range(4)]
        own_half = (lane >= 64) if high else (lane < 64)
        new = []
        for r in range(HALF):
            c = [pick(m[r], idx[q]) for q in range(4)]
            upd = (c[0] * rh[0] + c[1] * rh[1]) + (c[2] * rh[2] + c[3] * rh[3])
            v = jnp.where(inside, 0.0, m[r]) - upd
            if r0 <= r < r0 + 4:
                v = jnp.where(own_half, rh[r - r0], v)
            new.append(v)
        m = new
    return m


def to_stations(m, buf):
    for r in range(HALF):
        buf[8 * r : 8 * r + 8, :] = m[r]
        buf[8 * (r + HALF) : 8 * (r + HALF) + 8, :] = pltpu.roll(m[r], 64, 1)


def station(buf, s):
    return buf[pl.ds(s, A, stride=S), :][:, :A]


def invert128(mat):
    lane = lanes_of()
    sub = subs_of()
    m = list(mat)
    for k in range(0, BS, 4):
        t, o = divmod(k, 8)
        rows = [jnp.broadcast_to(m[t][o + q : o + q + 1, :], (8, 128)) for q in range(4)]
        at = [jnp.full((8, 128), k + q, I32) for q in range(4)]
        p = [[pick(rows[q], at[r]) for r in range(4)] for q in range(4)]
        inside, rh = scaled_rows(inv4(p), rows, lane, k)
        new = []
        for i in range(16):
            c = [pick(m[i], at[q]) for q in range(4)]
            upd = (c[0] * rh[0] + c[1] * rh[1]) + (c[2] * rh[2] + c[3] * rh[3])
            v = jnp.where(inside, 0.0, m[i]) - upd
            if i == t:
                for q in range(4):
                    v = jnp.where(sub == o + q, rh[q], v)
            new.append(v)
        m = new
    return m


def peer(axis, index):
    return {axis: index}


CH = 4
XC = NH // CH
HB = BS // 2


def pack_half(top, bot):
    row = lax.broadcasted_iota(I32, (HB, BS), 0)
    lane = lax.broadcasted_iota(I32, (HB, BS), 1)
    return jnp.where((lane >= HB) | (row > lane), top, pltpu.roll(bot, HB, 1))


def diag_tile(top):
    lane = lanes_of()
    sub = subs_of()
    out = jnp.zeros((8, BS), F32)
    for t in range(8):
        out = jnp.where(lane == sub + 8 * t, top[8 * t : 8 * t + 8], out)
    return out


def unpack_half(p, e):
    row = lax.broadcasted_iota(I32, (HB, BS), 0)
    lane = lax.broadcasted_iota(I32, (HB, BS), 1)
    t = jnp.concatenate([p, jnp.zeros((HB, BS), F32)], axis=0).T
    e = jnp.concatenate([e] * 8, axis=0)
    top = jnp.where((lane >= HB) | (row > lane), p, jnp.where(row == lane, e, t[:HB]))
    low = pltpu.roll(jnp.where(row <= lane, p, t[:HB]), HB, 1)
    return jnp.concatenate([top, jnp.where(lane < HB, t[HB:], low)], axis=0)


def body(len_ref, vis_ref, prior_ref, nm_hbm, cp_hbm, um_hbm, cov_ref, amb_ref,
         nm, cp, um, buf, w2, v2, s2, slot, invs, table, ediag, r1, part, r2, rd2, piece, blk, eblk, own, seg, call, dall,
         sx, lx, mine, theirs,
         loc, s1, q1, s2s, q2, d2s, d2q, s3, q3, d3s, d3q, s4, q4, d4s, d4q, s5, q5, d5s, d5q, s6, q6):
    me_g = lax.axis_index("group")
    me_s = lax.axis_index("station")
    me_b = lax.axis_index("bias")
    gp = [lax.rem(me_g + d, NG) for d in (4, 3, 5, 2, 6, 1, 7)]
    sp = [lax.rem(me_s + d, NST) for d in (8, 9, 7, 6, 10, 5, 11, 4, 12, 3, 13, 2, 14, 1, 15)]
    nm_copy = pltpu.make_async_copy(nm_hbm, nm, loc.at[0])
    nm_copy.start()
    cp_copy = [pltpu.make_async_copy(cp_hbm.at[s], cp.at[s], loc.at[2 + s]) for s in range(S)]
    for c in cp_copy:
        c.start()
    um_copy = pltpu.make_async_copy(um_hbm, um, loc.at[1])
    um_copy.start()
    barrier = pltpu.get_barrier_semaphore()
    for s in sp:
        pl.semaphore_signal(barrier, inc=1, device_id=peer("station", s), device_id_type=MESH)
    for g in gp:
        pl.semaphore_signal(barrier, inc=1, device_id=peer("group", g), device_id_type=MESH)
    pl.semaphore_signal(barrier, inc=1, device_id=peer("bias", 1 - me_b), device_id_type=MESH)

    def remote(src, dst, ss, rs, axis, index):
        return pltpu.make_async_remote_copy(src_ref=src, dst_ref=dst, send_sem=ss, recv_sem=rs, device_id=peer(axis, index), device_id_type=MESH)

    sent = []

    def send(*args):
        copy = remote(*args)
        copy.start()
        sent.append(copy)

    def arrived(*args):
        remote(*args).wait_recv()

    lane = lanes_of()
    sub = subs_of()
    near = XC * (me_s // XC)
    far_first = [lax.rem(near + XC * d, NH) for d in (2, 1, 3, 0)]
    near_first = [lax.rem(near + XC * d, NH) for d in (0, 1, 3, 2)]
    diag_owner = me_g == me_s // 2

    lens = len_column(len_ref)
    nm_copy.wait()
    to_stations(invert48(unpack_rows(nm, 0), lens), buf)
    zeros = jnp.zeros((A, 2 * BS), BF16)
    for s in range(S):
        inv = station(buf, s)
        invs[s] = inv
        lhs = jnp.concatenate(split2(inv), axis=0)
        keep = lax.broadcasted_iota(I32, (A, BS), 0) < len_ref[s]
        cp_copy[s].wait()
        for j in range(VH):
            w = jnp.where(keep, cp[s, j], 0.0)
            wp = jnp.concatenate(split2(w), axis=1)
            w2[s, j] = wp
            out = jnp.dot(lhs, wp, preferred_element_type=F32)
            out = out[:A] + out[A:]
            sol = out[:, :BS] + out[:, BS:]
            s2[s, j] = jnp.concatenate(split2(sol), axis=1)
            v2[s, j] = jnp.concatenate(split2(w - sol), axis=1)
        w2[s, VH] = zeros
        v2[s, VH] = zeros
        s2[s, VH] = zeros

    for i, x0 in enumerate(far_first):
        for dx in range(XC):
            x = x0 + dx
            at = []
            for s in range(S):
                j = jnp.int32(VH)
                for jj in range(VH):
                    j = jnp.where(vis_ref[s, jj] == x, jj, j)
                slot[s, x] = j
                at.append(j)
            wx = jnp.concatenate([w2[s, at[s]] for s in range(S)], axis=0)
            vx = jnp.concatenate([v2[s, at[s]] for s in range(S)], axis=0)
            out = lax.dot_general(wx, vx, (((0,), (0,)), ((), ())), preferred_element_type=F32)
            out = out[:BS] + out[BS:]
            out = out[:, :BS] + out[:, BS:]
            packed = pack_half(out[:HB], out[HB:])
            for g in range(NG):
                table[g, x] = packed[8 * g : 8 * g + 8]
            ediag[x] = diag_tile(out[:HB])
        if i == 0:
            pl.semaphore_wait(barrier, NG - 1 + NST - 1 + 1)
        for g in gp:
            send(table.at[g, pl.ds(x0, XC)], r1.at[me_g, pl.ds(x0, XC)], s1.at[i, g], q1.at[i, me_g], "group", g)
    both = jnp.zeros((8, BS), F32)
    for x in range(NH):
        e = ediag[x]
        e = pltpu.roll(e, x % 8, 0) if x % 8 else e
        both = both + (pltpu.roll(e, HB, 1) if x >= 8 else e)
    ediag[NH] = both
    for g in gp:
        send(ediag.at[NH], r1.at[me_g, NH], s1.at[CH, g], q1.at[CH, me_g], "group", g)

    def to_owner(x):
        return remote(part.at[x], r2.at[me_s], s2s.at[x], q2.at[me_s], "station", x)

    for i, x0 in enumerate(far_first):
        xs = pl.ds(x0, XC)
        total = table[me_g, xs]
        for g in gp:
            arrived(table.at[g, xs], r1.at[g, xs], s1.at[i, g], q1.at[i, g], "group", g)
            total = total + r1[g, xs]
        part[xs] = total
        for dx in range(XC):
            x = x0 + dx

            @pl.when(x != me_s)
            def _():
                to_owner(x).start()

    total = both
    for g in gp:
        arrived(ediag.at[NH], r1.at[g, NH], s1.at[CH, g], q1.at[CH, g], "group", g)
        total = total + r1[g, NH]
    part[NH] = total

    def diag_to_owner(h):
        return remote(part.at[NH], rd2.at[me_s], d2s.at[h], d2q.at[me_s], "station", 2 * me_g + h)

    for h in range(2):

        @pl.when(2 * me_g + h != me_s)
        def _():
            diag_to_owner(h).start()

    total = part[me_s]
    for s in sp[::-1]:
        arrived(part.at[s], r2.at[s], s2s.at[s], q2.at[s], "station", s)
        total = total + r2[s]
    piece[...] = total
    for g in gp:
        send(piece, blk.at[me_g], s3.at[g], q3.at[me_g], "group", g)
    blk[me_g] = total

    def diag_to_peer(g):
        return remote(piece_e, eblk, d3s.at[g], d3q.at[0], "group", g)

    piece_e = part.at[NH + 1]

    @pl.when(diag_owner)
    def _():
        e = part[NH]
        for s in sp:
            arrived(part.at[NH], rd2.at[s], d2s.at[0], d2q.at[s], "station", s)
            e = e + rd2[s]
        e = pltpu.roll(e, lax.rem(8 - lax.rem(me_s, 8), 8), 0)
        e = pltpu.roll(e, HB * (me_s // 8), 1)
        part[NH + 1] = e
        for g in gp:
            diag_to_peer(g).start()
        eblk[...] = e

    for g in gp:
        arrived(piece, blk.at[g], s3.at[g], q3.at[g], "group", g)

    @pl.when(me_g != me_s // 2)
    def _():
        arrived(piece_e, eblk, d3s.at[0], d3q.at[0], "group", me_s // 2)

    prior = jnp.broadcast_to(prior_ref[...], (8, 128))
    full = unpack_half(jnp.concatenate([blk[g] for g in range(NG)], axis=0), eblk[...])
    mat = [full[8 * i : 8 * i + 8] + jnp.where(lane == sub + 8 * i, prior, 0.0) for i in range(16)]
    mat = invert128(mat)
    top = jnp.concatenate(mat[:8], axis=0)
    packed = pack_half(top, jnp.concatenate(mat[8:], axis=0))
    for g in range(NG):
        own[g] = packed[8 * g : 8 * g + 8]
    own[NG] = diag_tile(top)
    for s in sp:
        send(own.at[me_g], seg.at[me_s], s4.at[s], q4.at[me_s], "station", s)

    def diag_to_station(s):
        return remote(own.at[NG], dall.at[me_s], d4s.at[s], d4q.at[me_s], "station", s)

    @pl.when(diag_owner)
    def _():
        for s in sp:
            diag_to_station(s).start()
        dall[me_s] = own[NG]

    seg[me_s] = own[me_g]
    for i in range(16):
        cov_ref[8 * i : 8 * i + 8, :] = mat[i]
    um_copy.wait()
    to_stations([z.astype(F32) for z in unpack_rows(um, 0)], buf)
    zs = [station(buf, s).astype(BF16) for s in range(S)]
    for h in range(2):
        x = 2 * me_g + h

        @pl.when(x != me_s)
        def _():
            arrived(own.at[NG], dall.at[x], d4s.at[0], d4q.at[x], "station", x)

    pair = pl.ds(2 * me_g, 2)
    for i, x0 in enumerate(near_first):
        for dx in range(XC):
            x = x0 + dx

            @pl.when(x != me_s)
            def _():
                arrived(own.at[me_g], seg.at[x], s4.at[0], q4.at[x], "station", x)

        xs = pl.ds(x0, XC)
        for g in gp:
            send(seg.at[xs], call.at[me_g, xs], s5.at[i, g], q5.at[i, me_g], "group", g)
        if i == 0:
            for g in gp:
                send(dall.at[pair], dall.at[pair], d5s.at[g], d5q.at[me_g], "group", g)
    call[me_g] = seg[...]
    for g in gp:
        gpair = pl.ds(2 * g, 2)
        arrived(dall.at[gpair], dall.at[gpair], d5s.at[g], d5q.at[g], "group", g)
    for i, x0 in enumerate(near_first):
        xs = pl.ds(x0, XC)
        for g in gp:
            arrived(seg.at[xs], call.at[g, xs], s5.at[i, g], q5.at[i, g], "group", g)
        for dx in range(XC):
            x = x0 + dx
            sg = [s2[s, slot[s, x]] for s in range(S)]
            c = unpack_half(jnp.concatenate([call[g, x] for g in range(NG)], axis=0), dall[x])
            c2 = jnp.concatenate(split2(c), axis=1)
            c4 = jnp.concatenate([c2, c2], axis=0)
            out = jnp.dot(jnp.concatenate(sg, axis=0), c4, preferred_element_type=F32)
            hi, lo = split2(out[:, :BS] + out[:, BS:])
            n = XC * i + dx
            at = slice(BS * n, BS * n + BS)
            for s in range(S):
                sx[s, :A, at] = sg[s][:, :BS]
                sx[s, A:, at] = sg[s][:, BS:]
                lx[s, :A, at] = hi[A * s : A * s + A]
                lx[s, A:, at] = lo[A * s : A * s + A]
    nt = (((1,), (1,)), ((), ()))
    pad = jnp.zeros((HALF, 64 - A), F32)
    for s in range(S):
        out = lax.dot_general(lx[s], sx[s], nt, preferred_element_type=F32)
        out = out[:A] + out[A:]
        out = out[:, :A] + out[:, A:]
        mine[s] = jnp.concatenate([out[:HALF], pad, out[HALF:], pad], axis=1)
        if s % 4 == 3:
            ss = pl.ds(s - 3, 4)
            send(mine.at[ss], theirs.at[ss], s6.at[s // 4], q6.at[s // 4], "bias", 1 - me_b)
    ri = lax.broadcasted_iota(I32, (A, A), 0)
    ci = lax.broadcasted_iota(I32, (A, A), 1)
    for s in range(S):
        if s % 4 == 0:
            ss = pl.ds(s, 4)
            arrived(mine.at[ss], theirs.at[ss], s6.at[s // 4], q6.at[s // 4], "bias", 1 - me_b)
        keep = (ri < len_ref[s]) & (ci < len_ref[s])
        both = mine[s] + theirs[s]
        both = jnp.concatenate([both[:, :A], pltpu.roll(both, 64, 1)[:, :A]], axis=0)
        cov = jnp.where(keep, invs[s] + both, 0.0)
        hi, lo = split2(cov)
        t = jnp.dot(zs[s], hi, preferred_element_type=F32) + jnp.dot(zs[s], lo, preferred_element_type=F32)
        hi, lo = split2(t)
        o = lax.dot_general(hi, zs[s], nt, preferred_element_type=F32) + lax.dot_general(lo, zs[s], nt, preferred_element_type=F32)
        o = jnp.where(keep, o, 0.0)
        buf[pl.ds(s, A, stride=S), :] = jnp.concatenate([o, jnp.zeros((A, 128 - A), F32)], axis=1)
    acc = [None] * 18
    for i in range(A):
        v, o = divmod(A * i, 128)
        row = buf[8 * i : 8 * i + 8, :]
        row = pltpu.roll(row, o, 1) if o else row
        acc[v] = row if acc[v] is None else jnp.where(lane >= o, row, acc[v])
        if o + A > 128:
            acc[v + 1] = row
    for v in range(18):
        amb_ref[:, 128 * v : 128 * v + 128] = acc[v]
    for copy in sent:
        copy.wait_send()
    for s in sp:
        to_owner(s).wait_send()
    for h in range(2):

        @pl.when(2 * me_g + h != me_s)
        def _():
            diag_to_owner(h).wait_send()

    @pl.when(diag_owner)
    def _():
        for g in gp:
            diag_to_peer(g).wait_send()
        for s in sp:
            diag_to_station(s).wait_send()


def local(normal_mat, coupling, lengths, visible, bias_prior, unimod):
    vm = pl.BlockSpec(memory_space=pltpu.VMEM)
    sm = pl.BlockSpec(memory_space=pltpu.SMEM)
    hb = pl.BlockSpec(memory_space=pltpu.HBM)
    dma = pltpu.SemaphoreType.DMA
    vmem = pltpu.VMEM
    slots = vmem((S, VH + 1, A, 2 * BS), BF16)
    wide = vmem((S, 2 * A, NH * BS), BF16)
    rows = vmem((NH, 8, BS), F32)
    half = vmem((S, HALF, BS), F32)
    cov, amb = pl.pallas_call(
        body,
        out_shape=(jax.ShapeDtypeStruct((BS, BS), F32), jax.ShapeDtypeStruct((S, A * A), F32)),
        in_specs=[sm, sm, vm, hb, hb, hb],
        out_specs=(vm, vm),
        scratch_shapes=[
            vmem((S, A * A), F32),
            vmem((S, VH, A, BS), F32),
            vmem((S, A * A), I32),
            vmem((A * S, 128), F32),
            slots, slots, slots,
            pltpu.SMEM((S, NH), I32),
            vmem((S, A, A), F32),
            vmem((NG, NH, 8, BS), F32),
            vmem((NH + 1, 8, BS), F32),
            vmem((NG, NH + 1, 8, BS), F32),
            vmem((NH + 2, 8, BS), F32),
            rows, rows,
            vmem((8, BS), F32),
            vmem((NG, 8, BS), F32),
            vmem((8, BS), F32),
            vmem((NG + 1, 8, BS), F32),
            rows,
            vmem((NG, NH, 8, BS), F32),
            rows,
            wide, wide,
            half, half,
            dma((2 + S,)),
            dma((CH + 1, NG)), dma((CH + 1, NG)),
            dma((NST,)), dma((NST,)), dma((2,)), dma((NST,)),
            dma((NG,)), dma((NG,)), dma((NG,)), dma((1,)),
            dma((NST,)), dma((NST,)), dma((NST,)), dma((NST,)),
            dma((CH, NG)), dma((CH, NG)), dma((NG,)), dma((NG,)),
            dma((2,)), dma((2,)),
        ],
        compiler_params=pltpu.CompilerParams(vmem_limit_bytes=VMEM_LIMIT, collective_id=0, has_side_effects=True),
        name="epoch",
    )(
        lengths,
        visible.reshape(S, VH),
        bias_prior.reshape(1, BS),
        normal_mat,
        coupling.reshape(S, VH, A, BS),
        unimod,
    )
    return (cov.reshape(1, 1, BS, BS), amb)


def solution(mesh):
    return jax.shard_map(
        local,
        mesh=mesh,
        in_specs=(
            P(("station", "group"), None),
            P(("station", "group"), "bias", None, None, None),
            P(("station", "group")),
            P(("station", "group"), "bias", None),
            P("bias", "station", None),
            P(("station", "group"), None),
        ),
        out_specs=(P("bias", "station", None, None), P(("station", "group"), None)),
        check_vma=False,
    )
```

```python
import jax
import jax.numpy as jnp
from jax import lax
from jax.experimental import pallas as pl
from jax.experimental.pallas import tpu as pltpu
from jax.sharding import PartitionSpec as P

A = 48
BS = 128
VH = 8
S = 8
NH = 16
NST = 16
NG = 8
HALF = A // 2
MESH = pl.DeviceIdType.MESH
F32 = jnp.float32
BF16 = jnp.bfloat16
I32 = jnp.int32
VMEM_LIMIT = 48 * 1024 * 1024


def lanes_of(shape=(8, 128)):
    return lax.broadcasted_iota(I32, shape, 1)


def subs_of(shape=(8, 128)):
    return lax.broadcasted_iota(I32, shape, 0)


def pick(x, idx):
    return jnp.take_along_axis(x, idx, axis=1, mode="promise_in_bounds")


def split2(x):
    hi = x.astype(BF16)
    lo = (x - hi.astype(F32)).astype(BF16)
    return hi, lo


def inv2(m):
    (a, b), (c, d) = m
    r = 1.0 / (a * d - b * c)
    return [[d * r, -(b * r)], [-(c * r), a * r]]


def mul2(m, n):
    return [[m[i][0] * n[0][j] + m[i][1] * n[1][j] for j in range(2)] for i in range(2)]


def inv4(p):
    a = [[p[i][j] for j in range(2)] for i in range(2)]
    b = [[p[i][j + 2] for j in range(2)] for i in range(2)]
    c = [[p[i + 2][j] for j in range(2)] for i in range(2)]
    d = [[p[i + 2][j + 2] for j in range(2)] for i in range(2)]
    ai = inv2(a)
    t = mul2(ai, b)
    u = mul2(c, ai)
    ct = mul2(c, t)
    si = inv2([[d[i][j] - ct[i][j] for j in range(2)] for i in range(2)])
    ts = mul2(t, si)
    su = mul2(si, u)
    tsu = mul2(ts, u)
    out = [[None] * 4 for _ in range(4)]
    for i in range(2):
        for j in range(2):
            out[i][j] = ai[i][j] + tsu[i][j]
            out[i][j + 2] = -ts[i][j]
            out[i + 2][j] = -su[i][j]
            out[i + 2][j + 2] = si[i][j]
    return out


def scaled_rows(pinv, rows, col, k):
    inside = (col >= k) & (col < k + 4)
    rows = [jnp.where(inside, (col == k + q).astype(F32), rows[q]) for q in range(4)]
    out = []
    for q in range(4):
        out.append((pinv[q][0] * rows[0] + pinv[q][1] * rows[1]) + (pinv[q][2] * rows[2] + pinv[q][3] * rows[3]))
    return inside, out


def unpack_rows(ref, base):
    lane = lanes_of()
    vregs = [ref[:, 128 * v : 128 * (v + 1)] for v in range(18)]
    out = []
    for r in range(HALF):
        v, o = divmod(A * r, 128)

        def part(first, shift):
            head = vregs[first] if shift == 0 else pltpu.roll(vregs[first], shift, 1)
            return head

        low = part(v, (128 - o) % 128)
        high = part(v + 9, (192 - o) % 128)
        if o + A > 128:
            low = jnp.where(lane < 128 - o, low, part(v + 1, (128 - o) % 128))
            high = jnp.where(lane < 192 - o, high, part(v + 10, (192 - o) % 128))
        out.append(jnp.where(lane < 64, low, high))
    return out


def len_column(len_ref):
    sub = subs_of()
    out = jnp.zeros((8, 128), I32)
    for s in range(S):
        out = jnp.where(sub == s, len_ref[s], out)
    return out


def invert48(rows, lens):
    lane = lanes_of()
    col = lane & 63
    side = lane & 64
    m = []
    for r in range(HALF):
        row_id = jnp.where(lane < 64, r, r + HALF)
        m.append(jnp.where((row_id < lens) & (col < lens), rows[r], (col == row_id).astype(F32)))
    for k in range(0, A, 4):
        high = k >= HALF
        r0 = k % HALF
        base = 64 if high else 0
        dup = col + base
        piv = [m[r0 + q] for q in range(4)]
        p = [[pick(piv[q], jnp.full((8, 128), base + k + r, I32)) for r in range(4)] for q in range(4)]
        pinv = inv4(p)
        inside, rh = scaled_rows(pinv, [pick(piv[q], dup) for q in range(4)], col, k)
        idx = [side + (k + q) for q in range(4)]
        own_half = (lane >= 64) if high else (lane < 64)
        new = []
        for r in range(HALF):
            c = [pick(m[r], idx[q]) for q in range(4)]
            upd = (c[0] * rh[0] + c[1] * rh[1]) + (c[2] * rh[2] + c[3] * rh[3])
            v = jnp.where(inside, 0.0, m[r]) - upd
            if r0 <= r < r0 + 4:
                v = jnp.where(own_half, rh[r - r0], v)
            new.append(v)
        m = new
    return m


def to_stations(m, buf):
    for r in range(HALF):
        buf[8 * r : 8 * r + 8, :] = m[r]
        buf[8 * (r + HALF) : 8 * (r + HALF) + 8, :] = pltpu.roll(m[r], 64, 1)


def station(buf, s):
    return buf[pl.ds(s, A, stride=S), :][:, :A]


def invert128(mat):
    lane = lanes_of()
    sub = subs_of()
    m = list(mat)
    for k in range(0, BS, 4):
        t, o = divmod(k, 8)
        rows = [jnp.broadcast_to(m[t][o + q : o + q + 1, :], (8, 128)) for q in range(4)]
        at = [jnp.full((8, 128), k + q, I32) for q in range(4)]
        p = [[pick(rows[q], at[r]) for r in range(4)] for q in range(4)]
        inside, rh = scaled_rows(inv4(p), rows, lane, k)
        new = []
        for i in range(16):
            c = [pick(m[i], at[q]) for q in range(4)]
            upd = (c[0] * rh[0] + c[1] * rh[1]) + (c[2] * rh[2] + c[3] * rh[3])
            v = jnp.where(inside, 0.0, m[i]) - upd
            if i == t:
                for q in range(4):
                    v = jnp.where(sub == o + q, rh[q], v)
            new.append(v)
        m = new
    return m


def peer(axis, index):
    return {axis: index}


CH = 4
XC = NH // CH
HB = BS // 2


def pack_half(top, bot):
    row = lax.broadcasted_iota(I32, (HB, BS), 0)
    lane = lax.broadcasted_iota(I32, (HB, BS), 1)
    return jnp.where((lane >= HB) | (row > lane), top, pltpu.roll(bot, HB, 1))


def diag_tile(top):
    lane = lanes_of()
    sub = subs_of()
    out = jnp.zeros((8, BS), F32)
    for t in range(8):
        out = jnp.where(lane == sub + 8 * t, top[8 * t : 8 * t + 8], out)
    return out


def unpack_half(p, e):
    row = lax.broadcasted_iota(I32, (HB, BS), 0)
    lane = lax.broadcasted_iota(I32, (HB, BS), 1)
    t = jnp.concatenate([p, jnp.zeros((HB, BS), F32)], axis=0).T
    e = jnp.concatenate([e] * 8, axis=0)
    top = jnp.where((lane >= HB) | (row > lane), p, jnp.where(row == lane, e, t[:HB]))
    low = pltpu.roll(jnp.where(row <= lane, p, t[:HB]), HB, 1)
    return jnp.concatenate([top, jnp.where(lane < HB, t[HB:], low)], axis=0)


def body(len_ref, vis_ref, prior_ref, nm_hbm, cp_hbm, um_hbm, cov_ref, amb_ref,
         nm, cp, um, buf, w2, v2, s2, slot, invs, table, ediag, rc, tsum, r1, rd1, part, r2, rd2, piece, blk, eblk, own, seg, call, dall,
         sx, lx, mine, theirs,
         loc, sa, qa, s1, q1, d1s, d1q, s2s, q2, d2s, d2q, s3, q3, d3s, d3q, s4, q4, d4s, d4q, s5, q5, d5s, d5q, s7, q7, d7s, d7q, s6, q6):
    me_g = lax.axis_index("group")
    me_s = lax.axis_index("station")
    me_b = lax.axis_index("bias")
    gp = [lax.rem(me_g + d, NG) for d in (4, 3, 5, 2, 6, 1, 7)]
    sp = [lax.rem(me_s + d, NST) for d in (8, 9, 7, 6, 10, 5, 11, 4, 12, 3, 13, 2, 14, 1, 15)]
    me_c = lax.rem(me_g, 2)
    me_x = me_g // 2
    mate = me_g + 1 - 2 * me_c
    xp = [lax.rem(me_x + d, 4) for d in (2, 1, 3)]
    nm_copy = pltpu.make_async_copy(nm_hbm, nm, loc.at[0])
    nm_copy.start()
    cp_copy = [pltpu.make_async_copy(cp_hbm.at[s], cp.at[s], loc.at[2 + s]) for s in range(S)]
    for c in cp_copy:
        c.start()
    um_copy = pltpu.make_async_copy(um_hbm, um, loc.at[1])
    um_copy.start()
    barrier = pltpu.get_barrier_semaphore()
    for s in sp:
        pl.semaphore_signal(barrier, inc=1, device_id=peer("station", s), device_id_type=MESH)
    for g in gp:
        pl.semaphore_signal(barrier, inc=1, device_id=peer("group", g), device_id_type=MESH)
    pl.semaphore_signal(barrier, inc=1, device_id=peer("bias", 1 - me_b), device_id_type=MESH)

    def remote(src, dst, ss, rs, axis, index):
        return pltpu.make_async_remote_copy(src_ref=src, dst_ref=dst, send_sem=ss, recv_sem=rs, device_id=peer(axis, index), device_id_type=MESH)

    sent = []

    def send(*args):
        copy = remote(*args)
        copy.start()
        sent.append(copy)

    def arrived(*args):
        remote(*args).wait_recv()

    lane = lanes_of()
    sub = subs_of()
    near = XC * (me_s // XC)
    far_first = [lax.rem(near + XC * d, NH) for d in (2, 1, 3, 0)]
    near_first = [lax.rem(near + XC * d, NH) for d in (0, 1, 3, 2)]
    diag_owner = me_g == me_s // 2

    lens = len_column(len_ref)

    nm_copy.wait()
    to_stations(invert48(unpack_rows(nm, 0), lens), buf)
    zeros = jnp.zeros((A, 2 * BS), BF16)
    for s in range(S):
        inv = station(buf, s)
        invs[s] = inv
        lhs = jnp.concatenate(split2(inv), axis=0)
        keep = lax.broadcasted_iota(I32, (A, BS), 0) < len_ref[s]
        cp_copy[s].wait()
        for j in range(VH):
            w = jnp.where(keep, cp[s, j], 0.0)
            wp = jnp.concatenate(split2(w), axis=1)
            w2[s, j] = wp
            out = jnp.dot(lhs, wp, preferred_element_type=F32)
            out = out[:A] + out[A:]
            sol = out[:, :BS] + out[:, BS:]
            s2[s, j] = jnp.concatenate(split2(sol), axis=1)
            v2[s, j] = jnp.concatenate(split2(w - sol), axis=1)
        w2[s, VH] = zeros
        v2[s, VH] = zeros
        s2[s, VH] = zeros

    def pass_on(i):
        xs = pl.ds(far_first[i], XC)
        arrived(table.at[me_c, :, xs], rc.at[:, xs], sa.at[i], qa.at[i], "group", mate)
        tsum[:, xs] = table[me_c, :, xs] + rc[:, xs]
        for p in xp:
            send(tsum.at[p, xs], r1.at[me_x, xs], s1.at[i, p], q1.at[i, me_x], "group", 2 * p + me_c)

    for i, x0 in enumerate(far_first):
        for dx in range(XC):
            x = x0 + dx
            at = []
            for s in range(S):
                j = jnp.int32(VH)
                for jj in range(VH):
                    j = jnp.where(vis_ref[s, jj] == x, jj, j)
                slot[s, x] = j
                at.append(j)
            wx = jnp.concatenate([w2[s, at[s]] for s in range(S)], axis=0)
            vx = jnp.concatenate([v2[s, at[s]] for s in range(S)], axis=0)
            out = lax.dot_general(wx, vx, (((0,), (0,)), ((), ())), preferred_element_type=F32)
            out = out[:BS] + out[BS:]
            out = out[:, :BS] + out[:, BS:]
            packed = pack_half(out[:HB], out[HB:])
            for g in range(NG):
                table[g % 2, g // 2, x] = packed[8 * g : 8 * g + 8]
            ediag[x] = diag_tile(out[:HB])
        if i == 0:
            pl.semaphore_wait(barrier, NG - 1 + NST - 1 + 1)
        xs = pl.ds(x0, XC)
        send(table.at[1 - me_c, :, xs], rc.at[:, xs], sa.at[i], qa.at[i], "group", mate)
        if i > 0:
            pass_on(i - 1)
    both = jnp.zeros((8, BS), F32)
    for x in range(NH):
        e = ediag[x]
        e = pltpu.roll(e, x % 8, 0) if x % 8 else e
        both = both + (pltpu.roll(e, HB, 1) if x >= 8 else e)
    ediag[NH] = both
    for g in gp:
        send(ediag.at[NH], rd1.at[me_g], d1s.at[g], d1q.at[me_g], "group", g)
    pass_on(CH - 1)

    def to_owner(x):
        return remote(part.at[x], r2.at[me_s], s2s.at[x], q2.at[me_s], "station", x)

    for i, x0 in enumerate(far_first):
        xs = pl.ds(x0, XC)
        total = tsum[me_x, xs]
        for p in xp:
            arrived(tsum.at[p, xs], r1.at[p, xs], s1.at[i, p], q1.at[i, p], "group", 2 * p + me_c)
            total = total + r1[p, xs]
        part[xs] = total
        for dx in range(XC):
            x = x0 + dx

            @pl.when(x != me_s)
            def _():
                to_owner(x).start()

    total = both
    for g in gp:
        arrived(ediag.at[NH], rd1.at[g], d1s.at[g], d1q.at[g], "group", g)
        total = total + rd1[g]
    part[NH] = total

    def diag_to_owner(h):
        return remote(part.at[NH], rd2.at[me_s], d2s.at[h], d2q.at[me_s], "station", 2 * me_g + h)

    for h in range(2):

        @pl.when(2 * me_g + h != me_s)
        def _():
            diag_to_owner(h).start()

    total = part[me_s]
    for s in sp[::-1]:
        arrived(part.at[s], r2.at[s], s2s.at[s], q2.at[s], "station", s)
        total = total + r2[s]
    piece[...] = total
    for g in gp:
        send(piece, blk.at[me_g], s3.at[g], q3.at[me_g], "group", g)
    blk[me_g] = total

    def diag_to_peer(g):
        return remote(piece_e, eblk, d3s.at[g], d3q.at[0], "group", g)

    piece_e = part.at[NH + 1]

    @pl.when(diag_owner)
    def _():
        e = part[NH]
        for s in sp:
            arrived(part.at[NH], rd2.at[s], d2s.at[0], d2q.at[s], "station", s)
            e = e + rd2[s]
        e = pltpu.roll(e, lax.rem(8 - lax.rem(me_s, 8), 8), 0)
        e = pltpu.roll(e, HB * (me_s // 8), 1)
        part[NH + 1] = e
        for g in gp:
            diag_to_peer(g).start()
        eblk[...] = e

    for g in gp:
        arrived(piece, blk.at[g], s3.at[g], q3.at[g], "group", g)

    @pl.when(me_g != me_s // 2)
    def _():
        arrived(piece_e, eblk, d3s.at[0], d3q.at[0], "group", me_s // 2)

    prior = jnp.broadcast_to(prior_ref[...], (8, 128))
    full = unpack_half(jnp.concatenate([blk[g] for g in range(NG)], axis=0), eblk[...])
    mat = [full[8 * i : 8 * i + 8] + jnp.where(lane == sub + 8 * i, prior, 0.0) for i in range(16)]
    mat = invert128(mat)
    top = jnp.concatenate(mat[:8], axis=0)
    packed = pack_half(top, jnp.concatenate(mat[8:], axis=0))
    for g in range(NG):
        own[g] = packed[8 * g : 8 * g + 8]
    own[NG] = diag_tile(top)
    for s in sp:
        send(own.at[me_g], seg.at[me_s], s4.at[s], q4.at[me_s], "station", s)

    def diag_to_station(s):
        return remote(own.at[NG], dall.at[me_x, me_c, lax.rem(me_s, 2)], d4s.at[s], d4q.at[me_s], "station", s)

    @pl.when(diag_owner)
    def _():
        for s in sp:
            diag_to_station(s).start()
        dall[me_x, me_c, lax.rem(me_s, 2)] = own[NG]

    seg[me_s] = own[me_g]
    for i in range(16):
        cov_ref[8 * i : 8 * i + 8, :] = mat[i]
    um_copy.wait()
    to_stations([z.astype(F32) for z in unpack_rows(um, 0)], buf)
    zs = [station(buf, s).astype(BF16) for s in range(S)]
    for h in range(2):
        x = 2 * me_g + h

        @pl.when(x != me_s)
        def _():
            arrived(own.at[NG], dall.at[me_x, me_c, h], d4s.at[0], d4q.at[x], "station", x)

    for i, x0 in enumerate(near_first):
        for dx in range(XC):
            x = x0 + dx

            @pl.when(x != me_s)
            def _():
                arrived(own.at[me_g], seg.at[x], s4.at[0], q4.at[x], "station", x)

        xs = pl.ds(x0, XC)
        for p in xp:
            send(seg.at[xs], call.at[me_c, me_x, xs], s5.at[i, p], q5.at[i, me_x], "group", 2 * p + me_c)
        if i == 0:
            for p in xp:
                send(dall.at[me_x, me_c], dall.at[me_x, me_c], d5s.at[p], d5q.at[me_x], "group", 2 * p + me_c)
    call[me_c, me_x] = seg[...]

    def forward(i):
        xs = pl.ds(near_first[i], XC)
        for p in xp:
            arrived(seg.at[xs], call.at[me_c, p, xs], s5.at[i, p], q5.at[i, p], "group", 2 * p + me_c)
        send(call.at[me_c, :, xs], call.at[me_c, :, xs], s7.at[i], q7.at[i], "group", mate)

    for p in xp:
        arrived(dall.at[p, me_c], dall.at[p, me_c], d5s.at[p], d5q.at[p], "group", 2 * p + me_c)
    send(dall.at[:, me_c], dall.at[:, me_c], d7s, d7q, "group", mate)
    forward(0)
    arrived(dall.at[:, 1 - me_c], dall.at[:, 1 - me_c], d7s, d7q, "group", mate)
    for i, x0 in enumerate(near_first):
        xs = pl.ds(x0, XC)
        if i + 1 < CH:
            forward(i + 1)
        arrived(call.at[1 - me_c, :, xs], call.at[1 - me_c, :, xs], s7.at[i], q7.at[i], "group", mate)
        for dx in range(XC):
            x = x0 + dx
            sg = [s2[s, slot[s, x]] for s in range(S)]
            c = unpack_half(jnp.concatenate([call[g % 2, g // 2, x] for g in range(NG)], axis=0), dall[x // 4, lax.rem(x // 2, 2), lax.rem(x, 2)])
            c2 = jnp.concatenate(split2(c), axis=1)
            c4 = jnp.concatenate([c2, c2], axis=0)
            out = jnp.dot(jnp.concatenate(sg, axis=0), c4, preferred_element_type=F32)
            hi, lo = split2(out[:, :BS] + out[:, BS:])
            n = XC * i + dx
            at = slice(BS * n, BS * n + BS)
            for s in range(S):
                sx[s, :A, at] = sg[s][:, :BS]
                sx[s, A:, at] = sg[s][:, BS:]
                lx[s, :A, at] = hi[A * s : A * s + A]
                lx[s, A:, at] = lo[A * s : A * s + A]
    nt = (((1,), (1,)), ((), ()))
    pad = jnp.zeros((HALF, 64 - A), F32)
    for s in range(S):
        out = lax.dot_general(lx[s], sx[s], nt, preferred_element_type=F32)
        out = out[:A] + out[A:]
        out = out[:, :A] + out[:, A:]
        mine[s] = jnp.concatenate([out[:HALF], pad, out[HALF:], pad], axis=1)
        if s % 4 == 3:
            ss = pl.ds(s - 3, 4)
            send(mine.at[ss], theirs.at[ss], s6.at[s // 4], q6.at[s // 4], "bias", 1 - me_b)
    ri = lax.broadcasted_iota(I32, (A, A), 0)
    ci = lax.broadcasted_iota(I32, (A, A), 1)
    for s in range(S):
        if s % 4 == 0:
            ss = pl.ds(s, 4)
            arrived(mine.at[ss], theirs.at[ss], s6.at[s // 4], q6.at[s // 4], "bias", 1 - me_b)
        keep = (ri < len_ref[s]) & (ci < len_ref[s])
        both = mine[s] + theirs[s]
        both = jnp.concatenate([both[:, :A], pltpu.roll(both, 64, 1)[:, :A]], axis=0)
        cov = jnp.where(keep, invs[s] + both, 0.0)
        hi, lo = split2(cov)
        t = jnp.dot(zs[s], hi, preferred_element_type=F32) + jnp.dot(zs[s], lo, preferred_element_type=F32)
        hi, lo = split2(t)
        o = lax.dot_general(hi, zs[s], nt, preferred_element_type=F32) + lax.dot_general(lo, zs[s], nt, preferred_element_type=F32)
        o = jnp.where(keep, o, 0.0)
        buf[pl.ds(s, A, stride=S), :] = jnp.concatenate([o, jnp.zeros((A, 128 - A), F32)], axis=1)
    acc = [None] * 18
    for i in range(A):
        v, o = divmod(A * i, 128)
        row = buf[8 * i : 8 * i + 8, :]
        row = pltpu.roll(row, o, 1) if o else row
        acc[v] = row if acc[v] is None else jnp.where(lane >= o, row, acc[v])
        if o + A > 128:
            acc[v + 1] = row
    for v in range(18):
        amb_ref[:, 128 * v : 128 * v + 128] = acc[v]
    for copy in sent:
        copy.wait_send()
    for s in sp:
        to_owner(s).wait_send()
    for h in range(2):

        @pl.when(2 * me_g + h != me_s)
        def _():
            diag_to_owner(h).wait_send()

    @pl.when(diag_owner)
    def _():
        for g in gp:
            diag_to_peer(g).wait_send()
        for s in sp:
            diag_to_station(s).wait_send()


def hbm(x):
    return pltpu.with_memory_space_constraint(x, pltpu.HBM)


def local(normal_mat, coupling, lengths, visible, bias_prior, unimod):
    vm = pl.BlockSpec(memory_space=pltpu.VMEM)
    sm = pl.BlockSpec(memory_space=pltpu.SMEM)
    hb = pl.BlockSpec(memory_space=pltpu.HBM)
    dma = pltpu.SemaphoreType.DMA
    vmem = pltpu.VMEM
    slots = vmem((S, VH + 1, A, 2 * BS), BF16)
    wide = vmem((S, 2 * A, NH * BS), BF16)
    rows = vmem((NH, 8, BS), F32)
    quart = vmem((4, NH, 8, BS), F32)
    half = vmem((S, HALF, BS), F32)
    cov, amb = pl.pallas_call(
        body,
        out_shape=(jax.ShapeDtypeStruct((BS, BS), F32), jax.ShapeDtypeStruct((S, A * A), F32)),
        in_specs=[sm, sm, vm, hb, hb, hb],
        out_specs=(vm, vm),
        scratch_shapes=[
            vmem((S, A * A), F32),
            vmem((S, VH, A, BS), F32),
            vmem((S, A * A), I32),
            vmem((A * S, 128), F32),
            slots, slots, slots,
            pltpu.SMEM((S, NH), I32),
            vmem((S, A, A), F32),
            vmem((2, 4, NH, 8, BS), F32),
            vmem((NH + 1, 8, BS), F32),
            quart, quart, quart,
            vmem((NG, 8, BS), F32),
            vmem((NH + 2, 8, BS), F32),
            rows, rows,
            vmem((8, BS), F32),
            vmem((NG, 8, BS), F32),
            vmem((8, BS), F32),
            vmem((NG + 1, 8, BS), F32),
            rows,
            vmem((2, 4, NH, 8, BS), F32),
            vmem((4, 2, 2, 8, BS), F32),
            wide, wide,
            half, half,
            dma((2 + S,)),
            dma((CH,)), dma((CH,)), dma((CH, 4)), dma((CH, 4)), dma((NG,)), dma((NG,)),
            dma((NST,)), dma((NST,)), dma((2,)), dma((NST,)),
            dma((NG,)), dma((NG,)), dma((NG,)), dma((1,)),
            dma((NST,)), dma((NST,)), dma((NST,)), dma((NST,)),
            dma((CH, 4)), dma((CH, 4)), dma((4,)), dma((4,)),
            dma((CH,)), dma((CH,)), dma(()), dma(()),
            dma((2,)), dma((2,)),
        ],
        compiler_params=pltpu.CompilerParams(vmem_limit_bytes=VMEM_LIMIT, collective_id=0, has_side_effects=True),
        name="epoch",
    )(
        hbm(lengths),
        hbm(visible.reshape(S, VH)),
        hbm(bias_prior.reshape(1, BS)),
        hbm(normal_mat),
        hbm(coupling.reshape(S, VH, A, BS)),
        hbm(unimod),
    )
    return (cov.reshape(1, 1, BS, BS), amb)


def solution(mesh):
    return jax.shard_map(
        local,
        mesh=mesh,
        in_specs=(
            P(("station", "group"), None),
            P(("station", "group"), "bias", None, None, None),
            P(("station", "group")),
            P(("station", "group"), "bias", None),
            P("bias", "station", None),
            P(("station", "group"), None),
        ),
        out_specs=(P("bias", "station", None, None), P(("station", "group"), None)),
        check_vma=False,
    )
```

```python
import jax
import jax.numpy as jnp
from jax import lax
from jax.experimental import pallas as pl
from jax.experimental.pallas import tpu as pltpu
from jax.sharding import PartitionSpec as P

A = 48
BS = 128
VH = 8
S = 8
NH = 16
NST = 16
NG = 8
HALF = A // 2
MESH = pl.DeviceIdType.MESH
F32 = jnp.float32
BF16 = jnp.bfloat16
I32 = jnp.int32
VMEM_LIMIT = 48 * 1024 * 1024


def lanes_of(shape=(8, 128)):
    return lax.broadcasted_iota(I32, shape, 1)


def subs_of(shape=(8, 128)):
    return lax.broadcasted_iota(I32, shape, 0)


def pick(x, idx):
    return jnp.take_along_axis(x, idx, axis=1, mode="promise_in_bounds")


def split2(x):
    hi = x.astype(BF16)
    lo = (x - hi.astype(F32)).astype(BF16)
    return hi, lo


def inv2(m):
    (a, b), (c, d) = m
    r = 1.0 / (a * d - b * c)
    return [[d * r, -(b * r)], [-(c * r), a * r]]


def mul2(m, n):
    return [[m[i][0] * n[0][j] + m[i][1] * n[1][j] for j in range(2)] for i in range(2)]


def inv4(p):
    a = [[p[i][j] for j in range(2)] for i in range(2)]
    b = [[p[i][j + 2] for j in range(2)] for i in range(2)]
    c = [[p[i + 2][j] for j in range(2)] for i in range(2)]
    d = [[p[i + 2][j + 2] for j in range(2)] for i in range(2)]
    ai = inv2(a)
    t = mul2(ai, b)
    u = mul2(c, ai)
    ct = mul2(c, t)
    si = inv2([[d[i][j] - ct[i][j] for j in range(2)] for i in range(2)])
    ts = mul2(t, si)
    su = mul2(si, u)
    tsu = mul2(ts, u)
    out = [[None] * 4 for _ in range(4)]
    for i in range(2):
        for j in range(2):
            out[i][j] = ai[i][j] + tsu[i][j]
            out[i][j + 2] = -ts[i][j]
            out[i + 2][j] = -su[i][j]
            out[i + 2][j + 2] = si[i][j]
    return out


def unpack_rows(ref, base):
    lane = lanes_of()
    vregs = [ref[:, 128 * v : 128 * (v + 1)] for v in range(18)]
    out = []
    for r in range(HALF):
        v, o = divmod(A * r, 128)

        def part(first, shift):
            head = vregs[first] if shift == 0 else pltpu.roll(vregs[first], shift, 1)
            return head

        low = part(v, (128 - o) % 128)
        high = part(v + 9, (192 - o) % 128)
        if o + A > 128:
            low = jnp.where(lane < 128 - o, low, part(v + 1, (128 - o) % 128))
            high = jnp.where(lane < 192 - o, high, part(v + 10, (192 - o) % 128))
        out.append(jnp.where(lane < 64, low, high))
    return out


def to_stations(m, buf):
    for r in range(HALF):
        buf[8 * r : 8 * r + 8, :] = m[r]
        buf[8 * (r + HALF) : 8 * (r + HALF) + 8, :] = pltpu.roll(m[r], 64, 1)


def station(buf, s):
    return buf[pl.ds(s, A, stride=S), :][:, :A]


def block_rows(pinv, rows):
    return [(pinv[q][0] * rows[0] + pinv[q][1] * rows[1]) + (pinv[q][2] * rows[2] + pinv[q][3] * rows[3]) for q in range(4)]


def regroup(tiles, shifts, width):
    lane = lanes_of()
    out = None
    for h, (tile, shift) in enumerate(zip(tiles, shifts)):
        shift = shift % 128
        tile = pltpu.roll(tile, shift, 1) if shift else tile
        out = tile if out is None else jnp.where(lane >= width * h, tile, out)
    return out


def eliminate(m, order, group, row_tile, row_lanes):
    lane = lanes_of()
    sub = subs_of()
    jj = lane & (group - 1)
    base = lane - jj
    for k in range(0, order, 4):
        u0, o = row_tile(k)
        c0, j0 = divmod(k, group)
        at = [base + (j0 + q) for q in range(4)]
        inside = (jj >= j0) & (jj < j0 + 4)
        wide = [[jnp.broadcast_to(t[o + q : o + q + 1, :], (8, 128)) for t in m[u0]] for q in range(4)]
        h0 = row_lanes(k)
        if h0 is None:
            own = None
            p = [[pick(wide[q][c0], at[r]) for r in range(4)] for q in range(4)]
        else:
            own = base == h0
            p = [[pick(wide[q][c0], jnp.full((8, 128), h0 + j0 + r, I32)) for r in range(4)] for q in range(4)]
            wide = [[pick(t, jj + h0) for t in row] for row in wide]
        pinv = inv4(p)
        rh = []
        for c in range(len(m[0])):
            rows = [wide[q][c] for q in range(4)]
            if c == c0:
                rows = [jnp.where(inside, (jj == j0 + q).astype(F32), rows[q]) for q in range(4)]
            rh.append(block_rows(pinv, rows))
        new = []
        for u in range(len(m)):
            col = [pick(m[u][c0], at[q]) for q in range(4)]
            line = []
            for c in range(len(m[0])):
                r = rh[c]
                upd = (col[0] * r[0] + col[1] * r[1]) + (col[2] * r[2] + col[3] * r[3])
                v = (jnp.where(inside, 0.0, m[u][c]) if c == c0 else m[u][c]) - upd
                if u == u0:
                    for q in range(4):
                        hit = sub == o + q
                        v = jnp.where(hit if own is None else hit & own, r[q], v)
                line.append(v)
            new.append(line)
        m = new
    return m


def invert48(buf, len_ref):
    lane = lanes_of()
    sub = subs_of()
    lens = jnp.zeros((8, 128), I32)
    for s in range(S):
        lens = jnp.where(lane >= 16 * s, len_ref[s], lens)
    nat = [buf[pl.ds(s, A, stride=S), :] for s in range(S)]
    m = []
    for t in range(6):
        line = []
        for c in range(3):
            v = regroup([nat[s][8 * t : 8 * t + 8] for s in range(S)], [16 * s - 16 * c for s in range(S)], 16)
            row, col = sub + 8 * t, (lane & 15) + 16 * c
            line.append(jnp.where((row < lens) & (col < lens), v, (row == col).astype(F32)))
        m.append(line)
    m = eliminate(m, A, 16, lambda k: (k // 8, k % 8), lambda k: None)
    out = []
    for s in range(S):
        tiles = []
        for t in range(6):
            v = regroup(m[t], [16 * c - 16 * s for c in range(3)], 16)
            tiles.append(jnp.where(lane < A, v, 0.0))
        out.append(jnp.concatenate(tiles, axis=0))
    return out


def invert128(mat):
    m = [[regroup([mat[4 * u + h] for h in range(4)], [32 * h - 32 * c for h in range(4)], 32) for c in range(4)] for u in range(4)]
    m = eliminate(m, BS, 32, lambda k: (k // 32, k % 8), lambda k: 32 * ((k // 8) % 4))
    return [regroup(m[i // 4], [32 * c - 32 * (i % 4) for c in range(4)], 32) for i in range(16)]


def peer(axis, index):
    return {axis: index}


CH = 4
XC = NH // CH
HB = BS // 2


def pack_half(top, bot):
    row = lax.broadcasted_iota(I32, (HB, BS), 0)
    lane = lax.broadcasted_iota(I32, (HB, BS), 1)
    return jnp.where((lane >= HB) | (row > lane), top, pltpu.roll(bot, HB, 1))


def diag_tile(top):
    lane = lanes_of()
    sub = subs_of()
    out = jnp.zeros((8, BS), F32)
    for t in range(8):
        out = jnp.where(lane == sub + 8 * t, top[8 * t : 8 * t + 8], out)
    return out


def unpack_half(p, e):
    row = lax.broadcasted_iota(I32, (HB, BS), 0)
    lane = lax.broadcasted_iota(I32, (HB, BS), 1)
    t = jnp.concatenate([p, jnp.zeros((HB, BS), F32)], axis=0).T
    e = jnp.concatenate([e] * 8, axis=0)
    top = jnp.where((lane >= HB) | (row > lane), p, jnp.where(row == lane, e, t[:HB]))
    low = pltpu.roll(jnp.where(row <= lane, p, t[:HB]), HB, 1)
    return jnp.concatenate([top, jnp.where(lane < HB, t[HB:], low)], axis=0)


def body(len_ref, vis_ref, prior_ref, nm_hbm, cp_hbm, um_hbm, cov_ref, amb_ref,
         nm, cp, um, buf, w2, v2, s2, slot, invs, table, ediag, rc, tsum, r1, rd1, part, r2, rd2, piece, blk, eblk, own, seg, call, dall,
         sx, lx, mine, theirs,
         loc, sa, qa, s1, q1, d1s, d1q, s2s, q2, d2s, d2q, s3, q3, d3s, d3q, s4, q4, d4s, d4q, s5, q5, d5s, d5q, s7, q7, d7s, d7q, s6, q6):
    me_g = lax.axis_index("group")
    me_s = lax.axis_index("station")
    me_b = lax.axis_index("bias")
    gp = [lax.rem(me_g + d, NG) for d in (4, 3, 5, 2, 6, 1, 7)]
    sp = [lax.rem(me_s + d, NST) for d in (8, 9, 7, 6, 10, 5, 11, 4, 12, 3, 13, 2, 14, 1, 15)]
    me_c = lax.rem(me_g, 2)
    me_x = me_g // 2
    mate = me_g + 1 - 2 * me_c
    xp = [lax.rem(me_x + d, 4) for d in (2, 1, 3)]
    nm_copy = pltpu.make_async_copy(nm_hbm, nm, loc.at[0])
    nm_copy.start()
    cp_copy = [pltpu.make_async_copy(cp_hbm.at[s], cp.at[s], loc.at[2 + s]) for s in range(S)]
    for c in cp_copy:
        c.start()
    um_copy = pltpu.make_async_copy(um_hbm, um, loc.at[1])
    um_copy.start()
    barrier = pltpu.get_barrier_semaphore()
    for s in sp:
        pl.semaphore_signal(barrier, inc=1, device_id=peer("station", s), device_id_type=MESH)
    for g in gp:
        pl.semaphore_signal(barrier, inc=1, device_id=peer("group", g), device_id_type=MESH)
    pl.semaphore_signal(barrier, inc=1, device_id=peer("bias", 1 - me_b), device_id_type=MESH)

    def remote(src, dst, ss, rs, axis, index):
        return pltpu.make_async_remote_copy(src_ref=src, dst_ref=dst, send_sem=ss, recv_sem=rs, device_id=peer(axis, index), device_id_type=MESH)

    sent = []

    def send(*args):
        copy = remote(*args)
        copy.start()
        sent.append(copy)

    def arrived(*args):
        remote(*args).wait_recv()

    lane = lanes_of()
    sub = subs_of()
    near = XC * (me_s // XC)
    far_first = [lax.rem(near + XC * d, NH) for d in (2, 1, 3, 0)]
    near_first = [lax.rem(near + XC * d, NH) for d in (0, 1, 3, 2)]
    diag_owner = me_g == me_s // 2


    nm_copy.wait()
    to_stations(unpack_rows(nm, 0), buf)
    inverses = invert48(buf, len_ref)
    zeros = jnp.zeros((A, 2 * BS), BF16)
    for s in range(S):
        inv = inverses[s][:, :A]
        invs[s] = inv
        lhs = jnp.concatenate(split2(inv), axis=0)
        keep = lax.broadcasted_iota(I32, (A, BS), 0) < len_ref[s]
        cp_copy[s].wait()
        for j in range(VH):
            w = jnp.where(keep, cp[s, j], 0.0)
            wp = jnp.concatenate(split2(w), axis=1)
            w2[s, j] = wp
            out = jnp.dot(lhs, wp, preferred_element_type=F32)
            out = out[:A] + out[A:]
            sol = out[:, :BS] + out[:, BS:]
            s2[s, j] = jnp.concatenate(split2(sol), axis=1)
            v2[s, j] = jnp.concatenate(split2(w - sol), axis=1)
        w2[s, VH] = zeros
        v2[s, VH] = zeros
        s2[s, VH] = zeros

    def pass_on(i):
        xs = pl.ds(far_first[i], XC)
        arrived(table.at[me_c, :, xs], rc.at[:, xs], sa.at[i], qa.at[i], "group", mate)
        tsum[:, xs] = table[me_c, :, xs] + rc[:, xs]
        for p in xp:
            send(tsum.at[p, xs], r1.at[me_x, xs], s1.at[i, p], q1.at[i, me_x], "group", 2 * p + me_c)

    for i, x0 in enumerate(far_first):
        for dx in range(XC):
            x = x0 + dx
            at = []
            for s in range(S):
                j = jnp.int32(VH)
                for jj in range(VH):
                    j = jnp.where(vis_ref[s, jj] == x, jj, j)
                slot[s, x] = j
                at.append(j)
            wx = jnp.concatenate([w2[s, at[s]] for s in range(S)], axis=0)
            vx = jnp.concatenate([v2[s, at[s]] for s in range(S)], axis=0)
            out = lax.dot_general(wx, vx, (((0,), (0,)), ((), ())), preferred_element_type=F32)
            out = out[:BS] + out[BS:]
            out = out[:, :BS] + out[:, BS:]
            packed = pack_half(out[:HB], out[HB:])
            for g in range(NG):
                table[g % 2, g // 2, x] = packed[8 * g : 8 * g + 8]
            ediag[x] = diag_tile(out[:HB])
        if i == 0:
            pl.semaphore_wait(barrier, NG - 1 + NST - 1 + 1)
        xs = pl.ds(x0, XC)
        send(table.at[1 - me_c, :, xs], rc.at[:, xs], sa.at[i], qa.at[i], "group", mate)
        if i > 0:
            pass_on(i - 1)
    both = jnp.zeros((8, BS), F32)
    for x in range(NH):
        e = ediag[x]
        e = pltpu.roll(e, x % 8, 0) if x % 8 else e
        both = both + (pltpu.roll(e, HB, 1) if x >= 8 else e)
    ediag[NH] = both
    for g in gp:
        send(ediag.at[NH], rd1.at[me_g], d1s.at[g], d1q.at[me_g], "group", g)
    pass_on(CH - 1)

    def to_owner(x):
        return remote(part.at[x], r2.at[me_s], s2s.at[x], q2.at[me_s], "station", x)

    for i, x0 in enumerate(far_first):
        xs = pl.ds(x0, XC)
        total = tsum[me_x, xs]
        for p in xp:
            arrived(tsum.at[p, xs], r1.at[p, xs], s1.at[i, p], q1.at[i, p], "group", 2 * p + me_c)
            total = total + r1[p, xs]
        part[xs] = total
        for dx in range(XC):
            x = x0 + dx

            @pl.when(x != me_s)
            def _():
                to_owner(x).start()

    total = both
    for g in gp:
        arrived(ediag.at[NH], rd1.at[g], d1s.at[g], d1q.at[g], "group", g)
        total = total + rd1[g]
    part[NH] = total

    def diag_to_owner(h):
        return remote(part.at[NH], rd2.at[me_s], d2s.at[h], d2q.at[me_s], "station", 2 * me_g + h)

    for h in range(2):

        @pl.when(2 * me_g + h != me_s)
        def _():
            diag_to_owner(h).start()

    total = part[me_s]
    for s in sp[::-1]:
        arrived(part.at[s], r2.at[s], s2s.at[s], q2.at[s], "station", s)
        total = total + r2[s]
    piece[...] = total
    for g in gp:
        send(piece, blk.at[me_g], s3.at[g], q3.at[me_g], "group", g)
    blk[me_g] = total

    def diag_to_peer(g):
        return remote(piece_e, eblk, d3s.at[g], d3q.at[0], "group", g)

    piece_e = part.at[NH + 1]

    @pl.when(diag_owner)
    def _():
        e = part[NH]
        for s in sp:
            arrived(part.at[NH], rd2.at[s], d2s.at[0], d2q.at[s], "station", s)
            e = e + rd2[s]
        e = pltpu.roll(e, lax.rem(8 - lax.rem(me_s, 8), 8), 0)
        e = pltpu.roll(e, HB * (me_s // 8), 1)
        part[NH + 1] = e
        for g in gp:
            diag_to_peer(g).start()
        eblk[...] = e

    for g in gp:
        arrived(piece, blk.at[g], s3.at[g], q3.at[g], "group", g)

    @pl.when(me_g != me_s // 2)
    def _():
        arrived(piece_e, eblk, d3s.at[0], d3q.at[0], "group", me_s // 2)

    prior = jnp.broadcast_to(prior_ref[...], (8, 128))
    full = unpack_half(jnp.concatenate([blk[g] for g in range(NG)], axis=0), eblk[...])
    mat = [full[8 * i : 8 * i + 8] + jnp.where(lane == sub + 8 * i, prior, 0.0) for i in range(16)]
    mat = invert128(mat)
    top = jnp.concatenate(mat[:8], axis=0)
    packed = pack_half(top, jnp.concatenate(mat[8:], axis=0))
    for g in range(NG):
        own[g] = packed[8 * g : 8 * g + 8]
    own[NG] = diag_tile(top)
    for s in sp:
        send(own.at[me_g], seg.at[me_s], s4.at[s], q4.at[me_s], "station", s)

    def diag_to_station(s):
        return remote(own.at[NG], dall.at[me_x, me_c, lax.rem(me_s, 2)], d4s.at[s], d4q.at[me_s], "station", s)

    @pl.when(diag_owner)
    def _():
        for s in sp:
            diag_to_station(s).start()
        dall[me_x, me_c, lax.rem(me_s, 2)] = own[NG]

    seg[me_s] = own[me_g]
    for i in range(16):
        cov_ref[8 * i : 8 * i + 8, :] = mat[i]
    um_copy.wait()
    to_stations([z.astype(F32) for z in unpack_rows(um, 0)], buf)
    zs = [station(buf, s).astype(BF16) for s in range(S)]
    for h in range(2):
        x = 2 * me_g + h

        @pl.when(x != me_s)
        def _():
            arrived(own.at[NG], dall.at[me_x, me_c, h], d4s.at[0], d4q.at[x], "station", x)

    for i, x0 in enumerate(near_first):
        for dx in range(XC):
            x = x0 + dx

            @pl.when(x != me_s)
            def _():
                arrived(own.at[me_g], seg.at[x], s4.at[0], q4.at[x], "station", x)

        xs = pl.ds(x0, XC)
        for p in xp:
            send(seg.at[xs], call.at[me_c, me_x, xs], s5.at[i, p], q5.at[i, me_x], "group", 2 * p + me_c)
        if i == 0:
            for p in xp:
                send(dall.at[me_x, me_c], dall.at[me_x, me_c], d5s.at[p], d5q.at[me_x], "group", 2 * p + me_c)
    call[me_c, me_x] = seg[...]

    def forward(i):
        xs = pl.ds(near_first[i], XC)
        for p in xp:
            arrived(seg.at[xs], call.at[me_c, p, xs], s5.at[i, p], q5.at[i, p], "group", 2 * p + me_c)
        send(call.at[me_c, :, xs], call.at[me_c, :, xs], s7.at[i], q7.at[i], "group", mate)

    for p in xp:
        arrived(dall.at[p, me_c], dall.at[p, me_c], d5s.at[p], d5q.at[p], "group", 2 * p + me_c)
    send(dall.at[:, me_c], dall.at[:, me_c], d7s, d7q, "group", mate)
    forward(0)
    arrived(dall.at[:, 1 - me_c], dall.at[:, 1 - me_c], d7s, d7q, "group", mate)
    for i, x0 in enumerate(near_first):
        xs = pl.ds(x0, XC)
        if i + 1 < CH:
            forward(i + 1)
        arrived(call.at[1 - me_c, :, xs], call.at[1 - me_c, :, xs], s7.at[i], q7.at[i], "group", mate)
        for dx in range(XC):
            x = x0 + dx
            sg = [s2[s, slot[s, x]] for s in range(S)]
            c = unpack_half(jnp.concatenate([call[g % 2, g // 2, x] for g in range(NG)], axis=0), dall[x // 4, lax.rem(x // 2, 2), lax.rem(x, 2)])
            c2 = jnp.concatenate(split2(c), axis=1)
            c4 = jnp.concatenate([c2, c2], axis=0)
            out = jnp.dot(jnp.concatenate(sg, axis=0), c4, preferred_element_type=F32)
            hi, lo = split2(out[:, :BS] + out[:, BS:])
            n = XC * i + dx
            at = slice(BS * n, BS * n + BS)
            for s in range(S):
                sx[s, :A, at] = sg[s][:, :BS]
                sx[s, A:, at] = sg[s][:, BS:]
                lx[s, :A, at] = hi[A * s : A * s + A]
                lx[s, A:, at] = lo[A * s : A * s + A]
    nt = (((1,), (1,)), ((), ()))
    pad = jnp.zeros((HALF, 64 - A), F32)
    for s in range(S):
        out = lax.dot_general(lx[s], sx[s], nt, preferred_element_type=F32)
        out = out[:A] + out[A:]
        out = out[:, :A] + out[:, A:]
        mine[s] = jnp.concatenate([out[:HALF], pad, out[HALF:], pad], axis=1)
        if s % 4 == 3:
            ss = pl.ds(s - 3, 4)
            send(mine.at[ss], theirs.at[ss], s6.at[s // 4], q6.at[s // 4], "bias", 1 - me_b)
    ri = lax.broadcasted_iota(I32, (A, A), 0)
    ci = lax.broadcasted_iota(I32, (A, A), 1)
    for s in range(S):
        if s % 4 == 0:
            ss = pl.ds(s, 4)
            arrived(mine.at[ss], theirs.at[ss], s6.at[s // 4], q6.at[s // 4], "bias", 1 - me_b)
        keep = (ri < len_ref[s]) & (ci < len_ref[s])
        both = mine[s] + theirs[s]
        both = jnp.concatenate([both[:, :A], pltpu.roll(both, 64, 1)[:, :A]], axis=0)
        cov = jnp.where(keep, invs[s] + both, 0.0)
        hi, lo = split2(cov)
        t = jnp.dot(zs[s], hi, preferred_element_type=F32) + jnp.dot(zs[s], lo, preferred_element_type=F32)
        hi, lo = split2(t)
        o = lax.dot_general(hi, zs[s], nt, preferred_element_type=F32) + lax.dot_general(lo, zs[s], nt, preferred_element_type=F32)
        o = jnp.where(keep, o, 0.0)
        buf[pl.ds(s, A, stride=S), :] = jnp.concatenate([o, jnp.zeros((A, 128 - A), F32)], axis=1)
    acc = [None] * 18
    for i in range(A):
        v, o = divmod(A * i, 128)
        row = buf[8 * i : 8 * i + 8, :]
        row = pltpu.roll(row, o, 1) if o else row
        acc[v] = row if acc[v] is None else jnp.where(lane >= o, row, acc[v])
        if o + A > 128:
            acc[v + 1] = row
    for v in range(18):
        amb_ref[:, 128 * v : 128 * v + 128] = acc[v]
    for copy in sent:
        copy.wait_send()
    for s in sp:
        to_owner(s).wait_send()
    for h in range(2):

        @pl.when(2 * me_g + h != me_s)
        def _():
            diag_to_owner(h).wait_send()

    @pl.when(diag_owner)
    def _():
        for g in gp:
            diag_to_peer(g).wait_send()
        for s in sp:
            diag_to_station(s).wait_send()


def hbm(x):
    return pltpu.with_memory_space_constraint(x, pltpu.HBM)


def local(normal_mat, coupling, lengths, visible, bias_prior, unimod):
    vm = pl.BlockSpec(memory_space=pltpu.VMEM)
    sm = pl.BlockSpec(memory_space=pltpu.SMEM)
    hb = pl.BlockSpec(memory_space=pltpu.HBM)
    dma = pltpu.SemaphoreType.DMA
    vmem = pltpu.VMEM
    slots = vmem((S, VH + 1, A, 2 * BS), BF16)
    wide = vmem((S, 2 * A, NH * BS), BF16)
    rows = vmem((NH, 8, BS), F32)
    quart = vmem((4, NH, 8, BS), F32)
    half = vmem((S, HALF, BS), F32)
    cov, amb = pl.pallas_call(
        body,
        out_shape=(jax.ShapeDtypeStruct((BS, BS), F32), jax.ShapeDtypeStruct((S, A * A), F32)),
        in_specs=[sm, sm, vm, hb, hb, hb],
        out_specs=(vm, vm),
        scratch_shapes=[
            vmem((S, A * A), F32),
            vmem((S, VH, A, BS), F32),
            vmem((S, A * A), I32),
            vmem((A * S, 128), F32),
            slots, slots, slots,
            pltpu.SMEM((S, NH), I32),
            vmem((S, A, A), F32),
            vmem((2, 4, NH, 8, BS), F32),
            vmem((NH + 1, 8, BS), F32),
            quart, quart, quart,
            vmem((NG, 8, BS), F32),
            vmem((NH + 2, 8, BS), F32),
            rows, rows,
            vmem((8, BS), F32),
            vmem((NG, 8, BS), F32),
            vmem((8, BS), F32),
            vmem((NG + 1, 8, BS), F32),
            rows,
            vmem((2, 4, NH, 8, BS), F32),
            vmem((4, 2, 2, 8, BS), F32),
            wide, wide,
            half, half,
            dma((2 + S,)),
            dma((CH,)), dma((CH,)), dma((CH, 4)), dma((CH, 4)), dma((NG,)), dma((NG,)),
            dma((NST,)), dma((NST,)), dma((2,)), dma((NST,)),
            dma((NG,)), dma((NG,)), dma((NG,)), dma((1,)),
            dma((NST,)), dma((NST,)), dma((NST,)), dma((NST,)),
            dma((CH, 4)), dma((CH, 4)), dma((4,)), dma((4,)),
            dma((CH,)), dma((CH,)), dma(()), dma(()),
            dma((2,)), dma((2,)),
        ],
        compiler_params=pltpu.CompilerParams(vmem_limit_bytes=VMEM_LIMIT, collective_id=0, has_side_effects=True),
        name="epoch",
    )(
        hbm(lengths),
        hbm(visible.reshape(S, VH)),
        hbm(bias_prior.reshape(1, BS)),
        hbm(normal_mat),
        hbm(coupling.reshape(S, VH, A, BS)),
        hbm(unimod),
    )
    return (cov.reshape(1, 1, BS, BS), amb)


def solution(mesh):
    return jax.shard_map(
        local,
        mesh=mesh,
        in_specs=(
            P(("station", "group"), None),
            P(("station", "group"), "bias", None, None, None),
            P(("station", "group")),
            P(("station", "group"), "bias", None),
            P("bias", "station", None),
            P(("station", "group"), None),
        ),
        out_specs=(P("bias", "station", None, None), P(("station", "group"), None)),
        check_vma=False,
    )
```

```python
import jax
import jax.numpy as jnp
from jax import lax
from jax.experimental import pallas as pl
from jax.experimental.pallas import tpu as pltpu
from jax.sharding import PartitionSpec as P

A = 48
BS = 128
VH = 8
S = 8
NH = 16
NST = 16
NG = 8
HALF = A // 2
MESH = pl.DeviceIdType.MESH
F32 = jnp.float32
BF16 = jnp.bfloat16
I32 = jnp.int32
VMEM_LIMIT = 48 * 1024 * 1024


def lanes_of(shape=(8, 128)):
    return lax.broadcasted_iota(I32, shape, 1)


def subs_of(shape=(8, 128)):
    return lax.broadcasted_iota(I32, shape, 0)


def pick(x, idx):
    return jnp.take_along_axis(x, idx, axis=1, mode="promise_in_bounds")


def split2(x):
    hi = x.astype(BF16)
    lo = (x - hi.astype(F32)).astype(BF16)
    return hi, lo


def unpack_rows(ref, base):
    lane = lanes_of()
    vregs = [ref[:, 128 * v : 128 * (v + 1)] for v in range(18)]
    out = []
    for r in range(HALF):
        v, o = divmod(A * r, 128)

        def part(first, shift):
            head = vregs[first] if shift == 0 else pltpu.roll(vregs[first], shift, 1)
            return head

        low = part(v, (128 - o) % 128)
        high = part(v + 9, (192 - o) % 128)
        if o + A > 128:
            low = jnp.where(lane < 128 - o, low, part(v + 1, (128 - o) % 128))
            high = jnp.where(lane < 192 - o, high, part(v + 10, (192 - o) % 128))
        out.append(jnp.where(lane < 64, low, high))
    return out


def to_stations(m, buf):
    for r in range(HALF):
        buf[8 * r : 8 * r + 8, :] = m[r]
        buf[8 * (r + HALF) : 8 * (r + HALF) + 8, :] = pltpu.roll(m[r], 64, 1)


def station(buf, s):
    return buf[pl.ds(s, A, stride=S), :][:, :A]


def pivot_terms(p):
    a, b, d = p[0][0], p[0][1], p[1][1]
    det = a * d - b * b
    u = [[d * p[0][j] - b * p[1][j] for j in (2, 3)], [a * p[1][j] - b * p[0][j] for j in (2, 3)]]
    s00 = det * p[2][2] - (p[0][2] * u[0][0] + p[1][2] * u[1][0])
    s01 = det * p[2][3] - (p[0][2] * u[0][1] + p[1][2] * u[1][1])
    s11 = det * p[3][3] - (p[0][3] * u[0][1] + p[1][3] * u[1][1])
    r = 1.0 / det
    q = det * (1.0 / (s00 * s11 - s01 * s01))
    t = [[v * r for v in row] for row in u]
    return (a * r, b * r, d * r), t, (s00, s01, s11), q


def pivot_rows(terms, rows):
    (ar, br, dr), t, (s00, s01, s11), q = terms
    w = [rows[2 + j] - (t[0][j] * rows[0] + t[1][j] * rows[1]) for j in range(2)]
    y2 = [q * (s11 * w[0] - s01 * w[1]), q * (s00 * w[1] - s01 * w[0])]
    v = [dr * rows[0] - br * rows[1], ar * rows[1] - br * rows[0]]
    y1 = [v[i] - (t[i][0] * y2[0] + t[i][1] * y2[1]) for i in range(2)]
    return y1 + y2


def regroup(tiles, shifts, width):
    lane = lanes_of()
    out = None
    for h, (tile, shift) in enumerate(zip(tiles, shifts)):
        shift = shift % 128
        tile = pltpu.roll(tile, shift, 1) if shift else tile
        out = tile if out is None else jnp.where(lane >= width * h, tile, out)
    return out


def eliminate(m, order, group, row_tile, row_lanes):
    lane = lanes_of()
    sub = subs_of()
    jj = lane & (group - 1)
    base = lane - jj
    for k in range(0, order, 4):
        u0, o = row_tile(k)
        c0, j0 = divmod(k, group)
        at = [base + (j0 + q) for q in range(4)]
        inside = (jj >= j0) & (jj < j0 + 4)
        wide = [[jnp.broadcast_to(t[o + q : o + q + 1, :], (8, 128)) for t in m[u0]] for q in range(4)]
        h0 = row_lanes(k)
        own = None if h0 is None else base == h0
        p = [[None] * 4 for _ in range(4)]
        for q in range(4):
            for r in range(q, 4):
                to = at[r] if h0 is None else jnp.full((8, 128), h0 + j0 + r, I32)
                p[q][r] = p[r][q] = pick(wide[q][c0], to)
        if h0 is not None:
            wide = [[pick(t, jj + h0) for t in row] for row in wide]
        terms = pivot_terms(p)
        rh = []
        for c in range(len(m[0])):
            rows = [wide[q][c] for q in range(4)]
            if c == c0:
                rows = [jnp.where(inside, (jj == j0 + q).astype(F32), rows[q]) for q in range(4)]
            rh.append(pivot_rows(terms, rows))
        new = []
        for u in range(len(m)):
            col = [pick(m[u][c0], at[q]) for q in range(4)]
            line = []
            for c in range(len(m[0])):
                r = rh[c]
                v = jnp.where(inside, 0.0, m[u][c]) if c == c0 else m[u][c]
                v = (v - (col[2] * r[2] + col[3] * r[3])) - (col[0] * r[0] + col[1] * r[1])
                if u == u0:
                    for q in range(4):
                        hit = sub == o + q
                        v = jnp.where(hit if own is None else hit & own, r[q], v)
                line.append(v)
            new.append(line)
        m = new
    return m


def invert48(buf, len_ref):
    lane = lanes_of()
    sub = subs_of()
    lens = jnp.zeros((8, 128), I32)
    for s in range(S):
        lens = jnp.where(lane >= 16 * s, len_ref[s], lens)
    nat = [buf[pl.ds(s, A, stride=S), :] for s in range(S)]
    m = []
    for t in range(6):
        line = []
        for c in range(3):
            v = regroup([nat[s][8 * t : 8 * t + 8] for s in range(S)], [16 * s - 16 * c for s in range(S)], 16)
            row, col = sub + 8 * t, (lane & 15) + 16 * c
            line.append(jnp.where((row < lens) & (col < lens), v, (row == col).astype(F32)))
        m.append(line)
    m = eliminate(m, A, 16, lambda k: (k // 8, k % 8), lambda k: None)
    out = []
    for s in range(S):
        tiles = []
        for t in range(6):
            v = regroup(m[t], [16 * c - 16 * s for c in range(3)], 16)
            tiles.append(jnp.where(lane < A, v, 0.0))
        out.append(jnp.concatenate(tiles, axis=0))
    return out


def invert128(mat):
    m = [[regroup([mat[4 * u + h] for h in range(4)], [32 * h - 32 * c for h in range(4)], 32) for c in range(4)] for u in range(4)]
    m = eliminate(m, BS, 32, lambda k: (k // 32, k % 8), lambda k: 32 * ((k // 8) % 4))
    return [regroup(m[i // 4], [32 * c - 32 * (i % 4) for c in range(4)], 32) for i in range(16)]


def peer(axis, index):
    return {axis: index}


CH = 4
XC = NH // CH
HB = BS // 2


def pack_half(top, bot):
    row = lax.broadcasted_iota(I32, (HB, BS), 0)
    lane = lax.broadcasted_iota(I32, (HB, BS), 1)
    return jnp.where((lane >= HB) | (row > lane), top, pltpu.roll(bot, HB, 1))


def diag_tile(top):
    lane = lanes_of()
    sub = subs_of()
    out = jnp.zeros((8, BS), F32)
    for t in range(8):
        out = jnp.where(lane == sub + 8 * t, top[8 * t : 8 * t + 8], out)
    return out


def unpack_half(p, e):
    row = lax.broadcasted_iota(I32, (HB, BS), 0)
    lane = lax.broadcasted_iota(I32, (HB, BS), 1)
    t = jnp.concatenate([p, jnp.zeros((HB, BS), F32)], axis=0).T
    e = jnp.concatenate([e] * 8, axis=0)
    top = jnp.where((lane >= HB) | (row > lane), p, jnp.where(row == lane, e, t[:HB]))
    low = pltpu.roll(jnp.where(row <= lane, p, t[:HB]), HB, 1)
    return jnp.concatenate([top, jnp.where(lane < HB, t[HB:], low)], axis=0)


def body(len_ref, vis_ref, prior_ref, nm_hbm, cp_hbm, um_hbm, cov_ref, amb_ref,
         nm, cp, um, buf, w2, v2, s2, slot, invs, table, ediag, rc, tsum, r1, rd1, part, r2, rd2, piece, blk, eblk, own, seg, call, dall,
         sx, lx, mine, theirs,
         loc, sa, qa, s1, q1, d1s, d1q, s2s, q2, d2s, d2q, s3, q3, d3s, d3q, s4, q4, d4s, d4q, s5, q5, d5s, d5q, s7, q7, d7s, d7q, s6, q6):
    me_g = lax.axis_index("group")
    me_s = lax.axis_index("station")
    me_b = lax.axis_index("bias")
    gp = [lax.rem(me_g + d, NG) for d in (4, 3, 5, 2, 6, 1, 7)]
    sp = [lax.rem(me_s + d, NST) for d in (8, 9, 7, 6, 10, 5, 11, 4, 12, 3, 13, 2, 14, 1, 15)]
    me_c = lax.rem(me_g, 2)
    me_x = me_g // 2
    mate = me_g + 1 - 2 * me_c
    xp = [lax.rem(me_x + d, 4) for d in (2, 1, 3)]
    nm_copy = pltpu.make_async_copy(nm_hbm, nm, loc.at[0])
    nm_copy.start()
    cp_copy = [pltpu.make_async_copy(cp_hbm.at[s], cp.at[s], loc.at[2 + s]) for s in range(S)]
    for c in cp_copy:
        c.start()
    um_copy = pltpu.make_async_copy(um_hbm, um, loc.at[1])
    um_copy.start()
    barrier = pltpu.get_barrier_semaphore()
    for s in sp:
        pl.semaphore_signal(barrier, inc=1, device_id=peer("station", s), device_id_type=MESH)
    for g in gp:
        pl.semaphore_signal(barrier, inc=1, device_id=peer("group", g), device_id_type=MESH)
    pl.semaphore_signal(barrier, inc=1, device_id=peer("bias", 1 - me_b), device_id_type=MESH)

    def remote(src, dst, ss, rs, axis, index):
        return pltpu.make_async_remote_copy(src_ref=src, dst_ref=dst, send_sem=ss, recv_sem=rs, device_id=peer(axis, index), device_id_type=MESH)

    sent = []

    def send(*args):
        copy = remote(*args)
        copy.start()
        sent.append(copy)

    def arrived(*args):
        remote(*args).wait_recv()

    lane = lanes_of()
    sub = subs_of()
    near = XC * (me_s // XC)
    far_first = [lax.rem(near + XC * d, NH) for d in (2, 1, 3, 0)]
    near_first = [lax.rem(near + XC * d, NH) for d in (0, 1, 3, 2)]
    diag_owner = me_g == me_s // 2


    nm_copy.wait()
    to_stations(unpack_rows(nm, 0), buf)
    inverses = invert48(buf, len_ref)
    zeros = jnp.zeros((A, 2 * BS), BF16)
    for s in range(S):
        inv = inverses[s][:, :A]
        invs[s] = inv
        lhs = jnp.concatenate(split2(inv), axis=0)
        keep = lax.broadcasted_iota(I32, (A, BS), 0) < len_ref[s]
        cp_copy[s].wait()
        for j in range(VH):
            w = jnp.where(keep, cp[s, j], 0.0)
            wp = jnp.concatenate(split2(w), axis=1)
            w2[s, j] = wp
            out = jnp.dot(lhs, wp, preferred_element_type=F32)
            out = out[:A] + out[A:]
            sol = out[:, :BS] + out[:, BS:]
            s2[s, j] = jnp.concatenate(split2(sol), axis=1)
            v2[s, j] = jnp.concatenate(split2(w - sol), axis=1)
        w2[s, VH] = zeros
        v2[s, VH] = zeros
        s2[s, VH] = zeros

    def pass_on(i):
        xs = pl.ds(far_first[i], XC)
        arrived(table.at[me_c, :, xs], rc.at[:, xs], sa.at[i], qa.at[i], "group", mate)
        tsum[:, xs] = table[me_c, :, xs] + rc[:, xs]
        for p in xp:
            send(tsum.at[p, xs], r1.at[me_x, xs], s1.at[i, p], q1.at[i, me_x], "group", 2 * p + me_c)

    for i, x0 in enumerate(far_first):
        for dx in range(XC):
            x = x0 + dx
            at = []
            for s in range(S):
                j = jnp.int32(VH)
                for jj in range(VH):
                    j = jnp.where(vis_ref[s, jj] == x, jj, j)
                slot[s, x] = j
                at.append(j)
            wx = jnp.concatenate([w2[s, at[s]] for s in range(S)], axis=0)
            vx = jnp.concatenate([v2[s, at[s]] for s in range(S)], axis=0)
            out = lax.dot_general(wx, vx, (((0,), (0,)), ((), ())), preferred_element_type=F32)
            out = out[:BS] + out[BS:]
            out = out[:, :BS] + out[:, BS:]
            packed = pack_half(out[:HB], out[HB:])
            for g in range(NG):
                table[g % 2, g // 2, x] = packed[8 * g : 8 * g + 8]
            ediag[x] = diag_tile(out[:HB])
        if i == 0:
            pl.semaphore_wait(barrier, NG - 1 + NST - 1 + 1)
        xs = pl.ds(x0, XC)
        send(table.at[1 - me_c, :, xs], rc.at[:, xs], sa.at[i], qa.at[i], "group", mate)
        if i > 0:
            pass_on(i - 1)
    both = jnp.zeros((8, BS), F32)
    for x in range(NH):
        e = ediag[x]
        e = pltpu.roll(e, x % 8, 0) if x % 8 else e
        both = both + (pltpu.roll(e, HB, 1) if x >= 8 else e)
    ediag[NH] = both
    for g in gp:
        send(ediag.at[NH], rd1.at[me_g], d1s.at[g], d1q.at[me_g], "group", g)
    pass_on(CH - 1)

    def to_owner(x):
        return remote(part.at[x], r2.at[me_s], s2s.at[x], q2.at[me_s], "station", x)

    for i, x0 in enumerate(far_first):
        xs = pl.ds(x0, XC)
        total = tsum[me_x, xs]
        for p in xp:
            arrived(tsum.at[p, xs], r1.at[p, xs], s1.at[i, p], q1.at[i, p], "group", 2 * p + me_c)
            total = total + r1[p, xs]
        part[xs] = total
        for dx in range(XC):
            x = x0 + dx

            @pl.when(x != me_s)
            def _():
                to_owner(x).start()

    total = both
    for g in gp:
        arrived(ediag.at[NH], rd1.at[g], d1s.at[g], d1q.at[g], "group", g)
        total = total + rd1[g]
    part[NH] = total

    def diag_to_owner(h):
        return remote(part.at[NH], rd2.at[me_s], d2s.at[h], d2q.at[me_s], "station", 2 * me_g + h)

    for h in range(2):

        @pl.when(2 * me_g + h != me_s)
        def _():
            diag_to_owner(h).start()

    total = part[me_s]
    for s in sp[::-1]:
        arrived(part.at[s], r2.at[s], s2s.at[s], q2.at[s], "station", s)
        total = total + r2[s]
    piece[...] = total
    for g in gp:
        send(piece, blk.at[me_g], s3.at[g], q3.at[me_g], "group", g)
    blk[me_g] = total

    def diag_to_peer(g):
        return remote(piece_e, eblk, d3s.at[g], d3q.at[0], "group", g)

    piece_e = part.at[NH + 1]

    @pl.when(diag_owner)
    def _():
        e = part[NH]
        for s in sp:
            arrived(part.at[NH], rd2.at[s], d2s.at[0], d2q.at[s], "station", s)
            e = e + rd2[s]
        e = pltpu.roll(e, lax.rem(8 - lax.rem(me_s, 8), 8), 0)
        e = pltpu.roll(e, HB * (me_s // 8), 1)
        part[NH + 1] = e
        for g in gp:
            diag_to_peer(g).start()
        eblk[...] = e

    for g in gp:
        arrived(piece, blk.at[g], s3.at[g], q3.at[g], "group", g)

    @pl.when(me_g != me_s // 2)
    def _():
        arrived(piece_e, eblk, d3s.at[0], d3q.at[0], "group", me_s // 2)

    prior = jnp.broadcast_to(prior_ref[...], (8, 128))
    full = unpack_half(jnp.concatenate([blk[g] for g in range(NG)], axis=0), eblk[...])
    mat = [full[8 * i : 8 * i + 8] + jnp.where(lane == sub + 8 * i, prior, 0.0) for i in range(16)]
    mat = invert128(mat)
    top = jnp.concatenate(mat[:8], axis=0)
    packed = pack_half(top, jnp.concatenate(mat[8:], axis=0))
    for g in range(NG):
        own[g] = packed[8 * g : 8 * g + 8]
    own[NG] = diag_tile(top)
    for s in sp:
        send(own.at[me_g], seg.at[me_s], s4.at[s], q4.at[me_s], "station", s)

    def diag_to_station(s):
        return remote(own.at[NG], dall.at[me_x, me_c, lax.rem(me_s, 2)], d4s.at[s], d4q.at[me_s], "station", s)

    @pl.when(diag_owner)
    def _():
        for s in sp:
            diag_to_station(s).start()
        dall[me_x, me_c, lax.rem(me_s, 2)] = own[NG]

    seg[me_s] = own[me_g]
    for i in range(16):
        cov_ref[8 * i : 8 * i + 8, :] = mat[i]
    um_copy.wait()
    to_stations([z.astype(F32) for z in unpack_rows(um, 0)], buf)
    zs = [station(buf, s).astype(BF16) for s in range(S)]
    for h in range(2):
        x = 2 * me_g + h

        @pl.when(x != me_s)
        def _():
            arrived(own.at[NG], dall.at[me_x, me_c, h], d4s.at[0], d4q.at[x], "station", x)

    for i, x0 in enumerate(near_first):
        for dx in range(XC):
            x = x0 + dx

            @pl.when(x != me_s)
            def _():
                arrived(own.at[me_g], seg.at[x], s4.at[0], q4.at[x], "station", x)

        xs = pl.ds(x0, XC)
        for p in xp:
            send(seg.at[xs], call.at[me_c, me_x, xs], s5.at[i, p], q5.at[i, me_x], "group", 2 * p + me_c)
        if i == 0:
            for p in xp:
                send(dall.at[me_x, me_c], dall.at[me_x, me_c], d5s.at[p], d5q.at[me_x], "group", 2 * p + me_c)
    call[me_c, me_x] = seg[...]

    def forward(i):
        xs = pl.ds(near_first[i], XC)
        for p in xp:
            arrived(seg.at[xs], call.at[me_c, p, xs], s5.at[i, p], q5.at[i, p], "group", 2 * p + me_c)
        send(call.at[me_c, :, xs], call.at[me_c, :, xs], s7.at[i], q7.at[i], "group", mate)

    for p in xp:
        arrived(dall.at[p, me_c], dall.at[p, me_c], d5s.at[p], d5q.at[p], "group", 2 * p + me_c)
    send(dall.at[:, me_c], dall.at[:, me_c], d7s, d7q, "group", mate)
    forward(0)
    arrived(dall.at[:, 1 - me_c], dall.at[:, 1 - me_c], d7s, d7q, "group", mate)
    for i, x0 in enumerate(near_first):
        xs = pl.ds(x0, XC)
        if i + 1 < CH:
            forward(i + 1)
        arrived(call.at[1 - me_c, :, xs], call.at[1 - me_c, :, xs], s7.at[i], q7.at[i], "group", mate)
        for dx in range(XC):
            x = x0 + dx
            sg = [s2[s, slot[s, x]] for s in range(S)]
            c = unpack_half(jnp.concatenate([call[g % 2, g // 2, x] for g in range(NG)], axis=0), dall[x // 4, lax.rem(x // 2, 2), lax.rem(x, 2)])
            c2 = jnp.concatenate(split2(c), axis=1)
            c4 = jnp.concatenate([c2, c2], axis=0)
            out = jnp.dot(jnp.concatenate(sg, axis=0), c4, preferred_element_type=F32)
            hi, lo = split2(out[:, :BS] + out[:, BS:])
            n = XC * i + dx
            at = slice(BS * n, BS * n + BS)
            for s in range(S):
                sx[s, :A, at] = sg[s][:, :BS]
                sx[s, A:, at] = sg[s][:, BS:]
                lx[s, :A, at] = hi[A * s : A * s + A]
                lx[s, A:, at] = lo[A * s : A * s + A]
    nt = (((1,), (1,)), ((), ()))
    pad = jnp.zeros((HALF, 64 - A), F32)
    for s in range(S):
        out = lax.dot_general(lx[s], sx[s], nt, preferred_element_type=F32)
        out = out[:A] + out[A:]
        out = out[:, :A] + out[:, A:]
        mine[s] = jnp.concatenate([out[:HALF], pad, out[HALF:], pad], axis=1)
        if s % 4 == 3:
            ss = pl.ds(s - 3, 4)
            send(mine.at[ss], theirs.at[ss], s6.at[s // 4], q6.at[s // 4], "bias", 1 - me_b)
    ri = lax.broadcasted_iota(I32, (A, A), 0)
    ci = lax.broadcasted_iota(I32, (A, A), 1)
    for s in range(S):
        if s % 4 == 0:
            ss = pl.ds(s, 4)
            arrived(mine.at[ss], theirs.at[ss], s6.at[s // 4], q6.at[s // 4], "bias", 1 - me_b)
        keep = (ri < len_ref[s]) & (ci < len_ref[s])
        both = mine[s] + theirs[s]
        both = jnp.concatenate([both[:, :A], pltpu.roll(both, 64, 1)[:, :A]], axis=0)
        cov = jnp.where(keep, invs[s] + both, 0.0)
        hi, lo = split2(cov)
        t = jnp.dot(zs[s], hi, preferred_element_type=F32) + jnp.dot(zs[s], lo, preferred_element_type=F32)
        hi, lo = split2(t)
        o = lax.dot_general(hi, zs[s], nt, preferred_element_type=F32) + lax.dot_general(lo, zs[s], nt, preferred_element_type=F32)
        o = jnp.where(keep, o, 0.0)
        buf[pl.ds(s, A, stride=S), :] = jnp.concatenate([o, jnp.zeros((A, 128 - A), F32)], axis=1)
    acc = [None] * 18
    for i in range(A):
        v, o = divmod(A * i, 128)
        row = buf[8 * i : 8 * i + 8, :]
        row = pltpu.roll(row, o, 1) if o else row
        acc[v] = row if acc[v] is None else jnp.where(lane >= o, row, acc[v])
        if o + A > 128:
            acc[v + 1] = row
    for v in range(18):
        amb_ref[:, 128 * v : 128 * v + 128] = acc[v]
    for copy in sent:
        copy.wait_send()
    for s in sp:
        to_owner(s).wait_send()
    for h in range(2):

        @pl.when(2 * me_g + h != me_s)
        def _():
            diag_to_owner(h).wait_send()

    @pl.when(diag_owner)
    def _():
        for g in gp:
            diag_to_peer(g).wait_send()
        for s in sp:
            diag_to_station(s).wait_send()


def hbm(x):
    return pltpu.with_memory_space_constraint(x, pltpu.HBM)


def local(normal_mat, coupling, lengths, visible, bias_prior, unimod):
    vm = pl.BlockSpec(memory_space=pltpu.VMEM)
    sm = pl.BlockSpec(memory_space=pltpu.SMEM)
    hb = pl.BlockSpec(memory_space=pltpu.HBM)
    dma = pltpu.SemaphoreType.DMA
    vmem = pltpu.VMEM
    slots = vmem((S, VH + 1, A, 2 * BS), BF16)
    wide = vmem((S, 2 * A, NH * BS), BF16)
    rows = vmem((NH, 8, BS), F32)
    quart = vmem((4, NH, 8, BS), F32)
    half = vmem((S, HALF, BS), F32)
    cov, amb = pl.pallas_call(
        body,
        out_shape=(jax.ShapeDtypeStruct((BS, BS), F32), jax.ShapeDtypeStruct((S, A * A), F32)),
        in_specs=[sm, sm, vm, hb, hb, hb],
        out_specs=(vm, vm),
        scratch_shapes=[
            vmem((S, A * A), F32),
            vmem((S, VH, A, BS), F32),
            vmem((S, A * A), I32),
            vmem((A * S, 128), F32),
            slots, slots, slots,
            pltpu.SMEM((S, NH), I32),
            vmem((S, A, A), F32),
            vmem((2, 4, NH, 8, BS), F32),
            vmem((NH + 1, 8, BS), F32),
            quart, quart, quart,
            vmem((NG, 8, BS), F32),
            vmem((NH + 2, 8, BS), F32),
            rows, rows,
            vmem((8, BS), F32),
            vmem((NG, 8, BS), F32),
            vmem((8, BS), F32),
            vmem((NG + 1, 8, BS), F32),
            rows,
            vmem((2, 4, NH, 8, BS), F32),
            vmem((4, 2, 2, 8, BS), F32),
            wide, wide,
            half, half,
            dma((2 + S,)),
            dma((CH,)), dma((CH,)), dma((CH, 4)), dma((CH, 4)), dma((NG,)), dma((NG,)),
            dma((NST,)), dma((NST,)), dma((2,)), dma((NST,)),
            dma((NG,)), dma((NG,)), dma((NG,)), dma((1,)),
            dma((NST,)), dma((NST,)), dma((NST,)), dma((NST,)),
            dma((CH, 4)), dma((CH, 4)), dma((4,)), dma((4,)),
            dma((CH,)), dma((CH,)), dma(()), dma(()),
            dma((2,)), dma((2,)),
        ],
        compiler_params=pltpu.CompilerParams(vmem_limit_bytes=VMEM_LIMIT, collective_id=0, has_side_effects=True),
        name="epoch",
    )(
        hbm(lengths),
        hbm(visible.reshape(S, VH)),
        hbm(bias_prior.reshape(1, BS)),
        hbm(normal_mat),
        hbm(coupling.reshape(S, VH, A, BS)),
        hbm(unimod),
    )
    return (cov.reshape(1, 1, BS, BS), amb)


def solution(mesh):
    return jax.shard_map(
        local,
        mesh=mesh,
        in_specs=(
            P(("station", "group"), None),
            P(("station", "group"), "bias", None, None, None),
            P(("station", "group")),
            P(("station", "group"), "bias", None),
            P("bias", "station", None),
            P(("station", "group"), None),
        ),
        out_specs=(P("bias", "station", None, None), P(("station", "group"), None)),
        check_vma=False,
    )
```

```python
import jax
import jax.numpy as jnp
from jax import lax
from jax.experimental import pallas as pl
from jax.experimental.pallas import tpu as pltpu
from jax.sharding import PartitionSpec as P

A = 48
BS = 128
VH = 8
S = 8
NH = 16
NST = 16
NG = 8
HALF = A // 2
MESH = pl.DeviceIdType.MESH
F32 = jnp.float32
BF16 = jnp.bfloat16
I32 = jnp.int32
VMEM_LIMIT = 48 * 1024 * 1024


def lanes_of(shape=(8, 128)):
    return lax.broadcasted_iota(I32, shape, 1)


def subs_of(shape=(8, 128)):
    return lax.broadcasted_iota(I32, shape, 0)


def pick(x, idx):
    return jnp.take_along_axis(x, idx, axis=1, mode="promise_in_bounds")


def split2(x):
    hi = x.astype(BF16)
    lo = (x - hi.astype(F32)).astype(BF16)
    return hi, lo


def unpack_rows(ref, base):
    lane = lanes_of()
    vregs = [ref[:, 128 * v : 128 * (v + 1)] for v in range(18)]
    out = []
    for r in range(HALF):
        v, o = divmod(A * r, 128)

        def part(first, shift):
            head = vregs[first] if shift == 0 else pltpu.roll(vregs[first], shift, 1)
            return head

        low = part(v, (128 - o) % 128)
        high = part(v + 9, (192 - o) % 128)
        if o + A > 128:
            low = jnp.where(lane < 128 - o, low, part(v + 1, (128 - o) % 128))
            high = jnp.where(lane < 192 - o, high, part(v + 10, (192 - o) % 128))
        out.append(jnp.where(lane < 64, low, high))
    return out


def to_stations(m, buf):
    for r in range(HALF):
        buf[8 * r : 8 * r + 8, :] = m[r]
        buf[8 * (r + HALF) : 8 * (r + HALF) + 8, :] = pltpu.roll(m[r], 64, 1)


def station(buf, s):
    return buf[pl.ds(s, A, stride=S), :][:, :A]


def pivot_terms(p):
    a, b, d = p[0][0], p[0][1], p[1][1]
    det = a * d - b * b
    u = [[d * p[0][j] - b * p[1][j] for j in (2, 3)], [a * p[1][j] - b * p[0][j] for j in (2, 3)]]
    s00 = det * p[2][2] - (p[0][2] * u[0][0] + p[1][2] * u[1][0])
    s01 = det * p[2][3] - (p[0][2] * u[0][1] + p[1][2] * u[1][1])
    s11 = det * p[3][3] - (p[0][3] * u[0][1] + p[1][3] * u[1][1])
    r = 1.0 / det
    q = det * (1.0 / (s00 * s11 - s01 * s01))
    t = [[v * r for v in row] for row in u]
    return (a * r, b * r, d * r), t, (s00, s01, s11), q


def pivot_rows(terms, rows):
    (ar, br, dr), t, (s00, s01, s11), q = terms
    w = [rows[2 + j] - (t[0][j] * rows[0] + t[1][j] * rows[1]) for j in range(2)]
    y2 = [q * (s11 * w[0] - s01 * w[1]), q * (s00 * w[1] - s01 * w[0])]
    v = [dr * rows[0] - br * rows[1], ar * rows[1] - br * rows[0]]
    y1 = [v[i] - (t[i][0] * y2[0] + t[i][1] * y2[1]) for i in range(2)]
    return y1 + y2


def regroup(tiles, shifts, width):
    lane = lanes_of()
    out = None
    for h, (tile, shift) in enumerate(zip(tiles, shifts)):
        shift = shift % 128
        tile = pltpu.roll(tile, shift, 1) if shift else tile
        out = tile if out is None else jnp.where(lane >= width * h, tile, out)
    return out


def eliminate(m, order, group, row_tile, row_lanes):
    lane = lanes_of()
    sub = subs_of()
    jj = lane & (group - 1)
    base = lane - jj
    for k in range(0, order, 4):
        u0, o = row_tile(k)
        c0, j0 = divmod(k, group)
        at = [base + (j0 + q) for q in range(4)]
        inside = (jj >= j0) & (jj < j0 + 4)
        wide = [[jnp.broadcast_to(t[o + q : o + q + 1, :], (8, 128)) for t in m[u0]] for q in range(4)]
        h0 = row_lanes(k)
        own = None if h0 is None else base == h0
        p = [[None] * 4 for _ in range(4)]
        for q in range(4):
            for r in range(q, 4):
                to = at[r] if h0 is None else jnp.full((8, 128), h0 + j0 + r, I32)
                p[q][r] = p[r][q] = pick(wide[q][c0], to)
        if h0 is not None:
            wide = [[pick(t, jj + h0) for t in row] for row in wide]
        terms = pivot_terms(p)
        rh = []
        for c in range(len(m[0])):
            rows = [wide[q][c] for q in range(4)]
            if c == c0:
                rows = [jnp.where(inside, (jj == j0 + q).astype(F32), rows[q]) for q in range(4)]
            rh.append(pivot_rows(terms, rows))
        new = []
        for u in range(len(m)):
            col = [pick(m[u][c0], at[q]) for q in range(4)]
            line = []
            for c in range(len(m[0])):
                r = rh[c]
                v = jnp.where(inside, 0.0, m[u][c]) if c == c0 else m[u][c]
                v = (v - (col[2] * r[2] + col[3] * r[3])) - (col[0] * r[0] + col[1] * r[1])
                if u == u0:
                    for q in range(4):
                        hit = sub == o + q
                        v = jnp.where(hit if own is None else hit & own, r[q], v)
                line.append(v)
            new.append(line)
        m = new
    return m


def invert48(buf, len_ref):
    lane = lanes_of()
    sub = subs_of()
    lens = jnp.zeros((8, 128), I32)
    for s in range(S):
        lens = jnp.where(lane >= 16 * s, len_ref[s], lens)
    nat = [buf[pl.ds(s, A, stride=S), :] for s in range(S)]
    m = []
    for t in range(6):
        line = []
        for c in range(3):
            v = regroup([nat[s][8 * t : 8 * t + 8] for s in range(S)], [16 * s - 16 * c for s in range(S)], 16)
            row, col = sub + 8 * t, (lane & 15) + 16 * c
            line.append(jnp.where((row < lens) & (col < lens), v, (row == col).astype(F32)))
        m.append(line)
    m = eliminate(m, A, 16, lambda k: (k // 8, k % 8), lambda k: None)
    out = []
    for s in range(S):
        tiles = []
        for t in range(6):
            v = regroup(m[t], [16 * c - 16 * s for c in range(3)], 16)
            tiles.append(jnp.where(lane < A, v, 0.0))
        out.append(jnp.concatenate(tiles, axis=0))
    return out


def invert128(mat):
    m = [[regroup([mat[4 * u + h] for h in range(4)], [32 * h - 32 * c for h in range(4)], 32) for c in range(4)] for u in range(4)]
    m = eliminate(m, BS, 32, lambda k: (k // 32, k % 8), lambda k: 32 * ((k // 8) % 4))
    return [regroup(m[i // 4], [32 * c - 32 * (i % 4) for c in range(4)], 32) for i in range(16)]


def peer(axis, index):
    return {axis: index}


CR = 2
XR = NH // CR
CG = 2
XG = NH // CG
HB = BS // 2


def pack_half(top, bot):
    row = lax.broadcasted_iota(I32, (HB, BS), 0)
    lane = lax.broadcasted_iota(I32, (HB, BS), 1)
    return jnp.where((lane >= HB) | (row > lane), top, pltpu.roll(bot, HB, 1))


def diag_tile(top):
    lane = lanes_of()
    sub = subs_of()
    out = jnp.zeros((8, BS), F32)
    for t in range(8):
        out = jnp.where(lane == sub + 8 * t, top[8 * t : 8 * t + 8], out)
    return out


def unpack_half(p, e):
    row = lax.broadcasted_iota(I32, (HB, BS), 0)
    lane = lax.broadcasted_iota(I32, (HB, BS), 1)
    t = jnp.concatenate([p, jnp.zeros((HB, BS), F32)], axis=0).T
    e = jnp.concatenate([e] * 8, axis=0)
    top = jnp.where((lane >= HB) | (row > lane), p, jnp.where(row == lane, e, t[:HB]))
    low = pltpu.roll(jnp.where(row <= lane, p, t[:HB]), HB, 1)
    return jnp.concatenate([top, jnp.where(lane < HB, t[HB:], low)], axis=0)


def body(len_ref, vis_ref, prior_ref, nm_hbm, cp_hbm, um_hbm, cov_ref, amb_ref,
         nm, cp, um, buf, w2, v2, s2, slot, invs, table, ediag, rc, tsum, r1, rd1, part, r2, rd2, piece, blk, eblk, own, seg, call, dall,
         sx, lx, mine, theirs,
         loc, sa, qa, s1, q1, d1s, d1q, s2s, q2, d2s, d2q, s3, q3, d3s, d3q, s4, q4, d4s, d4q, s5, q5, d5s, d5q, s7, q7, d7s, d7q, s6, q6):
    me_g = lax.axis_index("group")
    me_s = lax.axis_index("station")
    me_b = lax.axis_index("bias")
    gp = [lax.rem(me_g + d, NG) for d in (4, 3, 5, 2, 6, 1, 7)]
    sp = [lax.rem(me_s + d, NST) for d in (8, 9, 7, 6, 10, 5, 11, 4, 12, 3, 13, 2, 14, 1, 15)]
    me_c = lax.rem(me_g, 2)
    me_x = me_g // 2
    mate = me_g + 1 - 2 * me_c
    xp = [lax.rem(me_x + d, 4) for d in (2, 1, 3)]
    nm_copy = pltpu.make_async_copy(nm_hbm, nm, loc.at[0])
    nm_copy.start()
    cp_copy = [pltpu.make_async_copy(cp_hbm.at[s], cp.at[s], loc.at[2 + s]) for s in range(S)]
    for c in cp_copy:
        c.start()
    um_copy = pltpu.make_async_copy(um_hbm, um, loc.at[1])
    um_copy.start()
    barrier = pltpu.get_barrier_semaphore()
    for s in sp:
        pl.semaphore_signal(barrier, inc=1, device_id=peer("station", s), device_id_type=MESH)
    for g in gp:
        pl.semaphore_signal(barrier, inc=1, device_id=peer("group", g), device_id_type=MESH)
    pl.semaphore_signal(barrier, inc=1, device_id=peer("bias", 1 - me_b), device_id_type=MESH)

    def remote(src, dst, ss, rs, axis, index):
        return pltpu.make_async_remote_copy(src_ref=src, dst_ref=dst, send_sem=ss, recv_sem=rs, device_id=peer(axis, index), device_id_type=MESH)

    sent = []

    def send(*args):
        copy = remote(*args)
        copy.start()
        sent.append(copy)

    def arrived(*args):
        remote(*args).wait_recv()

    lane = lanes_of()
    sub = subs_of()
    far_first = [lax.rem(XR * (me_s // XR) + XR * d, NH) for d in range(CR - 1, -1, -1)]
    near_first = [lax.rem(XG * (me_s // XG) + XG * d, NH) for d in range(CG)]
    diag_owner = me_g == me_s // 2


    nm_copy.wait()
    to_stations(unpack_rows(nm, 0), buf)
    inverses = invert48(buf, len_ref)
    zeros = jnp.zeros((A, 2 * BS), BF16)
    for s in range(S):
        inv = inverses[s][:, :A]
        invs[s] = inv
        lhs = jnp.concatenate(split2(inv), axis=0)
        keep = lax.broadcasted_iota(I32, (A, BS), 0) < len_ref[s]
        cp_copy[s].wait()
        for j in range(VH):
            w = jnp.where(keep, cp[s, j], 0.0)
            wp = jnp.concatenate(split2(w), axis=1)
            w2[s, j] = wp
            out = jnp.dot(lhs, wp, preferred_element_type=F32)
            out = out[:A] + out[A:]
            sol = out[:, :BS] + out[:, BS:]
            s2[s, j] = jnp.concatenate(split2(sol), axis=1)
            v2[s, j] = jnp.concatenate(split2(w - sol), axis=1)
        w2[s, VH] = zeros
        v2[s, VH] = zeros
        s2[s, VH] = zeros

    def pass_on(i):
        xs = pl.ds(far_first[i], XR)
        arrived(table.at[me_c, :, xs], rc.at[:, xs], sa.at[i], qa.at[i], "group", mate)
        tsum[:, xs] = table[me_c, :, xs] + rc[:, xs]
        for p in xp:
            send(tsum.at[p, xs], r1.at[me_x, xs], s1.at[i, p], q1.at[i, me_x], "group", 2 * p + me_c)

    for i, x0 in enumerate(far_first):
        for dx in range(XR):
            x = x0 + dx
            at = []
            for s in range(S):
                j = jnp.int32(VH)
                for jj in range(VH):
                    j = jnp.where(vis_ref[s, jj] == x, jj, j)
                slot[s, x] = j
                at.append(j)
            wx = jnp.concatenate([w2[s, at[s]] for s in range(S)], axis=0)
            vx = jnp.concatenate([v2[s, at[s]] for s in range(S)], axis=0)
            out = lax.dot_general(wx, vx, (((0,), (0,)), ((), ())), preferred_element_type=F32)
            out = out[:BS] + out[BS:]
            out = out[:, :BS] + out[:, BS:]
            packed = pack_half(out[:HB], out[HB:])
            for g in range(NG):
                table[g % 2, g // 2, x] = packed[8 * g : 8 * g + 8]
            ediag[x] = diag_tile(out[:HB])
        if i == 0:
            pl.semaphore_wait(barrier, NG - 1 + NST - 1 + 1)
        xs = pl.ds(x0, XR)
        send(table.at[1 - me_c, :, xs], rc.at[:, xs], sa.at[i], qa.at[i], "group", mate)
        if i > 0:
            pass_on(i - 1)
    both = jnp.zeros((8, BS), F32)
    for x in range(NH):
        e = ediag[x]
        e = pltpu.roll(e, x % 8, 0) if x % 8 else e
        both = both + (pltpu.roll(e, HB, 1) if x >= 8 else e)
    ediag[NH] = both
    for g in gp:
        send(ediag.at[NH], rd1.at[me_g], d1s.at[g], d1q.at[me_g], "group", g)
    pass_on(CR - 1)

    def to_owner(x):
        return remote(part.at[x], r2.at[me_s], s2s.at[x], q2.at[me_s], "station", x)

    for i, x0 in enumerate(far_first):
        xs = pl.ds(x0, XR)
        total = tsum[me_x, xs]
        for p in xp:
            arrived(tsum.at[p, xs], r1.at[p, xs], s1.at[i, p], q1.at[i, p], "group", 2 * p + me_c)
            total = total + r1[p, xs]
        part[xs] = total
        for dx in range(XR):
            x = x0 + dx

            @pl.when(x != me_s)
            def _():
                to_owner(x).start()

    total = both
    for g in gp:
        arrived(ediag.at[NH], rd1.at[g], d1s.at[g], d1q.at[g], "group", g)
        total = total + rd1[g]
    part[NH] = total

    def diag_to_owner(h):
        return remote(part.at[NH], rd2.at[me_s], d2s.at[h], d2q.at[me_s], "station", 2 * me_g + h)

    for h in range(2):

        @pl.when(2 * me_g + h != me_s)
        def _():
            diag_to_owner(h).start()

    total = part[me_s]
    for s in sp[::-1]:
        arrived(part.at[s], r2.at[s], s2s.at[s], q2.at[s], "station", s)
        total = total + r2[s]
    piece[...] = total
    for g in gp:
        send(piece, blk.at[me_g], s3.at[g], q3.at[me_g], "group", g)
    blk[me_g] = total

    def diag_to_peer(g):
        return remote(piece_e, eblk, d3s.at[g], d3q.at[0], "group", g)

    piece_e = part.at[NH + 1]

    @pl.when(diag_owner)
    def _():
        e = part[NH]
        for s in sp:
            arrived(part.at[NH], rd2.at[s], d2s.at[0], d2q.at[s], "station", s)
            e = e + rd2[s]
        e = pltpu.roll(e, lax.rem(8 - lax.rem(me_s, 8), 8), 0)
        e = pltpu.roll(e, HB * (me_s // 8), 1)
        part[NH + 1] = e
        for g in gp:
            diag_to_peer(g).start()
        eblk[...] = e

    for g in gp:
        arrived(piece, blk.at[g], s3.at[g], q3.at[g], "group", g)

    @pl.when(me_g != me_s // 2)
    def _():
        arrived(piece_e, eblk, d3s.at[0], d3q.at[0], "group", me_s // 2)

    prior = jnp.broadcast_to(prior_ref[...], (8, 128))
    full = unpack_half(jnp.concatenate([blk[g] for g in range(NG)], axis=0), eblk[...])
    mat = [full[8 * i : 8 * i + 8] + jnp.where(lane == sub + 8 * i, prior, 0.0) for i in range(16)]
    mat = invert128(mat)
    top = jnp.concatenate(mat[:8], axis=0)
    packed = pack_half(top, jnp.concatenate(mat[8:], axis=0))
    for g in range(NG):
        own[g] = packed[8 * g : 8 * g + 8]
    own[NG] = diag_tile(top)
    for s in sp:
        send(own.at[me_g], seg.at[me_s], s4.at[s], q4.at[me_s], "station", s)

    def diag_to_station(s):
        return remote(own.at[NG], dall.at[me_x, me_c, lax.rem(me_s, 2)], d4s.at[s], d4q.at[me_s], "station", s)

    @pl.when(diag_owner)
    def _():
        for s in sp:
            diag_to_station(s).start()
        dall[me_x, me_c, lax.rem(me_s, 2)] = own[NG]

    seg[me_s] = own[me_g]
    for i in range(16):
        cov_ref[8 * i : 8 * i + 8, :] = mat[i]
    um_copy.wait()
    to_stations([z.astype(F32) for z in unpack_rows(um, 0)], buf)
    zs = [station(buf, s).astype(BF16) for s in range(S)]
    for h in range(2):
        x = 2 * me_g + h

        @pl.when(x != me_s)
        def _():
            arrived(own.at[NG], dall.at[me_x, me_c, h], d4s.at[0], d4q.at[x], "station", x)

    for i, x0 in enumerate(near_first):
        for dx in range(XG):
            x = x0 + dx

            @pl.when(x != me_s)
            def _():
                arrived(own.at[me_g], seg.at[x], s4.at[0], q4.at[x], "station", x)

        xs = pl.ds(x0, XG)
        for p in xp:
            send(seg.at[xs], call.at[me_c, me_x, xs], s5.at[i, p], q5.at[i, me_x], "group", 2 * p + me_c)
        if i == 0:
            for p in xp:
                send(dall.at[me_x, me_c], dall.at[me_x, me_c], d5s.at[p], d5q.at[me_x], "group", 2 * p + me_c)
    call[me_c, me_x] = seg[...]

    def forward(i):
        xs = pl.ds(near_first[i], XG)
        for p in xp:
            arrived(seg.at[xs], call.at[me_c, p, xs], s5.at[i, p], q5.at[i, p], "group", 2 * p + me_c)
        send(call.at[me_c, :, xs], call.at[me_c, :, xs], s7.at[i], q7.at[i], "group", mate)

    for p in xp:
        arrived(dall.at[p, me_c], dall.at[p, me_c], d5s.at[p], d5q.at[p], "group", 2 * p + me_c)
    send(dall.at[:, me_c], dall.at[:, me_c], d7s, d7q, "group", mate)
    forward(0)
    arrived(dall.at[:, 1 - me_c], dall.at[:, 1 - me_c], d7s, d7q, "group", mate)
    nt = (((1,), (1,)), ((), ()))
    partial = [None] * S
    pad = jnp.zeros((HALF, 64 - A), F32)
    for i, x0 in enumerate(near_first):
        xs = pl.ds(x0, XG)
        if i + 1 < CG:
            forward(i + 1)
        arrived(call.at[1 - me_c, :, xs], call.at[1 - me_c, :, xs], s7.at[i], q7.at[i], "group", mate)
        for dx in range(XG):
            x = x0 + dx
            sg = [s2[s, slot[s, x]] for s in range(S)]
            c = unpack_half(jnp.concatenate([call[g % 2, g // 2, x] for g in range(NG)], axis=0), dall[x // 4, lax.rem(x // 2, 2), lax.rem(x, 2)])
            c2 = jnp.concatenate(split2(c), axis=1)
            c4 = jnp.concatenate([c2, c2], axis=0)
            out = jnp.dot(jnp.concatenate(sg, axis=0), c4, preferred_element_type=F32)
            hi, lo = split2(out[:, :BS] + out[:, BS:])
            n = XG * i + dx
            at = slice(BS * n, BS * n + BS)
            for s in range(S):
                sx[s, :A, at] = sg[s][:, :BS]
                sx[s, A:, at] = sg[s][:, BS:]
                lx[s, :A, at] = hi[A * s : A * s + A]
                lx[s, A:, at] = lo[A * s : A * s + A]
        for s in range(S):
            at = slice(BS * XG * i, BS * XG * (i + 1))
            out = lax.dot_general(lx[s, :, at], sx[s, :, at], nt, preferred_element_type=F32)
            out = out[:A] + out[A:]
            out = out[:, :A] + out[:, A:]
            partial[s] = out if i == 0 else partial[s] + out
            if i == CG - 1:
                mine[s] = jnp.concatenate([partial[s][:HALF], pad, partial[s][HALF:], pad], axis=1)
                if s % 4 == 3:
                    ss = pl.ds(s - 3, 4)
                    send(mine.at[ss], theirs.at[ss], s6.at[s // 4], q6.at[s // 4], "bias", 1 - me_b)
    ri = lax.broadcasted_iota(I32, (A, A), 0)
    ci = lax.broadcasted_iota(I32, (A, A), 1)
    for s in range(S):
        if s % 4 == 0:
            ss = pl.ds(s, 4)
            arrived(mine.at[ss], theirs.at[ss], s6.at[s // 4], q6.at[s // 4], "bias", 1 - me_b)
        keep = (ri < len_ref[s]) & (ci < len_ref[s])
        both = mine[s] + theirs[s]
        both = jnp.concatenate([both[:, :A], pltpu.roll(both, 64, 1)[:, :A]], axis=0)
        cov = jnp.where(keep, invs[s] + both, 0.0)
        hi, lo = split2(cov)
        t = jnp.dot(zs[s], hi, preferred_element_type=F32) + jnp.dot(zs[s], lo, preferred_element_type=F32)
        hi, lo = split2(t)
        o = lax.dot_general(hi, zs[s], nt, preferred_element_type=F32) + lax.dot_general(lo, zs[s], nt, preferred_element_type=F32)
        o = jnp.where(keep, o, 0.0)
        buf[pl.ds(s, A, stride=S), :] = jnp.concatenate([o, jnp.zeros((A, 128 - A), F32)], axis=1)
    acc = [None] * 18
    for i in range(A):
        v, o = divmod(A * i, 128)
        row = buf[8 * i : 8 * i + 8, :]
        row = pltpu.roll(row, o, 1) if o else row
        acc[v] = row if acc[v] is None else jnp.where(lane >= o, row, acc[v])
        if o + A > 128:
            acc[v + 1] = row
    for v in range(18):
        amb_ref[:, 128 * v : 128 * v + 128] = acc[v]
    for copy in sent:
        copy.wait_send()
    for s in sp:
        to_owner(s).wait_send()
    for h in range(2):

        @pl.when(2 * me_g + h != me_s)
        def _():
            diag_to_owner(h).wait_send()

    @pl.when(diag_owner)
    def _():
        for g in gp:
            diag_to_peer(g).wait_send()
        for s in sp:
            diag_to_station(s).wait_send()


def hbm(x):
    return pltpu.with_memory_space_constraint(x, pltpu.HBM)


def local(normal_mat, coupling, lengths, visible, bias_prior, unimod):
    vm = pl.BlockSpec(memory_space=pltpu.VMEM)
    sm = pl.BlockSpec(memory_space=pltpu.SMEM)
    hb = pl.BlockSpec(memory_space=pltpu.HBM)
    dma = pltpu.SemaphoreType.DMA
    vmem = pltpu.VMEM
    slots = vmem((S, VH + 1, A, 2 * BS), BF16)
    wide = vmem((S, 2 * A, NH * BS), BF16)
    rows = vmem((NH, 8, BS), F32)
    quart = vmem((4, NH, 8, BS), F32)
    half = vmem((S, HALF, BS), F32)
    cov, amb = pl.pallas_call(
        body,
        out_shape=(jax.ShapeDtypeStruct((BS, BS), F32), jax.ShapeDtypeStruct((S, A * A), F32)),
        in_specs=[sm, sm, vm, hb, hb, hb],
        out_specs=(vm, vm),
        scratch_shapes=[
            vmem((S, A * A), F32),
            vmem((S, VH, A, BS), F32),
            vmem((S, A * A), I32),
            vmem((A * S, 128), F32),
            slots, slots, slots,
            pltpu.SMEM((S, NH), I32),
            vmem((S, A, A), F32),
            vmem((2, 4, NH, 8, BS), F32),
            vmem((NH + 1, 8, BS), F32),
            quart, quart, quart,
            vmem((NG, 8, BS), F32),
            vmem((NH + 2, 8, BS), F32),
            rows, rows,
            vmem((8, BS), F32),
            vmem((NG, 8, BS), F32),
            vmem((8, BS), F32),
            vmem((NG + 1, 8, BS), F32),
            rows,
            vmem((2, 4, NH, 8, BS), F32),
            vmem((4, 2, 2, 8, BS), F32),
            wide, wide,
            half, half,
            dma((2 + S,)),
            dma((CR,)), dma((CR,)), dma((CR, 4)), dma((CR, 4)), dma((NG,)), dma((NG,)),
            dma((NST,)), dma((NST,)), dma((2,)), dma((NST,)),
            dma((NG,)), dma((NG,)), dma((NG,)), dma((1,)),
            dma((NST,)), dma((NST,)), dma((NST,)), dma((NST,)),
            dma((CG, 4)), dma((CG, 4)), dma((4,)), dma((4,)),
            dma((CG,)), dma((CG,)), dma(()), dma(()),
            dma((2,)), dma((2,)),
        ],
        compiler_params=pltpu.CompilerParams(vmem_limit_bytes=VMEM_LIMIT, collective_id=0, has_side_effects=True),
        name="epoch",
    )(
        hbm(lengths),
        hbm(visible.reshape(S, VH)),
        hbm(bias_prior.reshape(1, BS)),
        hbm(normal_mat),
        hbm(coupling.reshape(S, VH, A, BS)),
        hbm(unimod),
    )
    return (cov.reshape(1, 1, BS, BS), amb)


def solution(mesh):
    return jax.shard_map(
        local,
        mesh=mesh,
        in_specs=(
            P(("station", "group"), None),
            P(("station", "group"), "bias", None, None, None),
            P(("station", "group")),
            P(("station", "group"), "bias", None),
            P("bias", "station", None),
            P(("station", "group"), None),
        ),
        out_specs=(P("bias", "station", None, None), P(("station", "group"), None)),
        check_vma=False,
    )
```

```python
import jax
import jax.numpy as jnp
from jax import lax
from jax.experimental import pallas as pl
from jax.experimental.pallas import tpu as pltpu
from jax.sharding import PartitionSpec as P

A = 48
BS = 128
VH = 8
S = 8
NH = 16
NST = 16
NG = 8
HALF = A // 2
MESH = pl.DeviceIdType.MESH
F32 = jnp.float32
BF16 = jnp.bfloat16
I32 = jnp.int32
VMEM_LIMIT = 48 * 1024 * 1024


def lanes_of(shape=(8, 128)):
    return lax.broadcasted_iota(I32, shape, 1)


def subs_of(shape=(8, 128)):
    return lax.broadcasted_iota(I32, shape, 0)


def pick(x, idx):
    return jnp.take_along_axis(x, idx, axis=1, mode="promise_in_bounds")


def split2(x):
    hi = x.astype(BF16)
    lo = (x - hi.astype(F32)).astype(BF16)
    return hi, lo


def unpack_rows(ref, base):
    lane = lanes_of()
    vregs = [ref[:, 128 * v : 128 * (v + 1)] for v in range(18)]
    out = []
    for r in range(HALF):
        v, o = divmod(A * r, 128)

        def part(first, shift):
            head = vregs[first] if shift == 0 else pltpu.roll(vregs[first], shift, 1)
            return head

        low = part(v, (128 - o) % 128)
        high = part(v + 9, (192 - o) % 128)
        if o + A > 128:
            low = jnp.where(lane < 128 - o, low, part(v + 1, (128 - o) % 128))
            high = jnp.where(lane < 192 - o, high, part(v + 10, (192 - o) % 128))
        out.append(jnp.where(lane < 64, low, high))
    return out


def to_stations(m, buf):
    for r in range(HALF):
        buf[8 * r : 8 * r + 8, :] = m[r]
        buf[8 * (r + HALF) : 8 * (r + HALF) + 8, :] = pltpu.roll(m[r], 64, 1)


def station(buf, s):
    return buf[pl.ds(s, A, stride=S), :][:, :A]


def pivot_terms(p):
    a, b, d = p[0][0], p[0][1], p[1][1]
    det = a * d - b * b
    u = [[d * p[0][j] - b * p[1][j] for j in (2, 3)], [a * p[1][j] - b * p[0][j] for j in (2, 3)]]
    s00 = det * p[2][2] - (p[0][2] * u[0][0] + p[1][2] * u[1][0])
    s01 = det * p[2][3] - (p[0][2] * u[0][1] + p[1][2] * u[1][1])
    s11 = det * p[3][3] - (p[0][3] * u[0][1] + p[1][3] * u[1][1])
    r = 1.0 / det
    q = det * (1.0 / (s00 * s11 - s01 * s01))
    t = [[v * r for v in row] for row in u]
    return (a * r, b * r, d * r), t, (s00, s01, s11), q


def pivot_rows(terms, rows):
    (ar, br, dr), t, (s00, s01, s11), q = terms
    w = [rows[2 + j] - (t[0][j] * rows[0] + t[1][j] * rows[1]) for j in range(2)]
    y2 = [q * (s11 * w[0] - s01 * w[1]), q * (s00 * w[1] - s01 * w[0])]
    v = [dr * rows[0] - br * rows[1], ar * rows[1] - br * rows[0]]
    y1 = [v[i] - (t[i][0] * y2[0] + t[i][1] * y2[1]) for i in range(2)]
    return y1 + y2


def regroup(tiles, shifts, width):
    lane = lanes_of()
    out = None
    for h, (tile, shift) in enumerate(zip(tiles, shifts)):
        shift = shift % 128
        tile = pltpu.roll(tile, shift, 1) if shift else tile
        out = tile if out is None else jnp.where(lane >= width * h, tile, out)
    return out


def eliminate(m, order, group, row_tile, row_lanes):
    lane = lanes_of()
    sub = subs_of()
    jj = lane & (group - 1)
    base = lane - jj
    for k in range(0, order, 4):
        u0, o = row_tile(k)
        c0, j0 = divmod(k, group)
        at = [base + (j0 + q) for q in range(4)]
        inside = (jj >= j0) & (jj < j0 + 4)
        wide = [[jnp.broadcast_to(t[o + q : o + q + 1, :], (8, 128)) for t in m[u0]] for q in range(4)]
        h0 = row_lanes(k)
        own = None if h0 is None else base == h0
        p = [[None] * 4 for _ in range(4)]
        for q in range(4):
            for r in range(q, 4):
                to = at[r] if h0 is None else jnp.full((8, 128), h0 + j0 + r, I32)
                p[q][r] = p[r][q] = pick(wide[q][c0], to)
        if h0 is not None:
            wide = [[pick(t, jj + h0) for t in row] for row in wide]
        terms = pivot_terms(p)
        rh = []
        for c in range(len(m[0])):
            rows = [wide[q][c] for q in range(4)]
            if c == c0:
                rows = [jnp.where(inside, (jj == j0 + q).astype(F32), rows[q]) for q in range(4)]
            rh.append(pivot_rows(terms, rows))
        new = []
        for u in range(len(m)):
            col = [pick(m[u][c0], at[q]) for q in range(4)]
            line = []
            for c in range(len(m[0])):
                r = rh[c]
                v = jnp.where(inside, 0.0, m[u][c]) if c == c0 else m[u][c]
                v = (v - (col[2] * r[2] + col[3] * r[3])) - (col[0] * r[0] + col[1] * r[1])
                if u == u0:
                    for q in range(4):
                        hit = sub == o + q
                        v = jnp.where(hit if own is None else hit & own, r[q], v)
                line.append(v)
            new.append(line)
        m = new
    return m


def invert48(buf, len_ref):
    lane = lanes_of()
    sub = subs_of()
    lens = jnp.zeros((8, 128), I32)
    for s in range(S):
        lens = jnp.where(lane >= 16 * s, len_ref[s], lens)
    nat = [buf[pl.ds(s, A, stride=S), :] for s in range(S)]
    m = []
    for t in range(6):
        line = []
        for c in range(3):
            v = regroup([nat[s][8 * t : 8 * t + 8] for s in range(S)], [16 * s - 16 * c for s in range(S)], 16)
            row, col = sub + 8 * t, (lane & 15) + 16 * c
            line.append(jnp.where((row < lens) & (col < lens), v, (row == col).astype(F32)))
        m.append(line)
    m = eliminate(m, A, 16, lambda k: (k // 8, k % 8), lambda k: None)
    out = []
    for s in range(S):
        tiles = []
        for t in range(6):
            v = regroup(m[t], [16 * c - 16 * s for c in range(3)], 16)
            tiles.append(jnp.where(lane < A, v, 0.0))
        out.append(jnp.concatenate(tiles, axis=0))
    return out


def invert128(mat):
    m = [[regroup([mat[4 * u + h] for h in range(4)], [32 * h - 32 * c for h in range(4)], 32) for c in range(4)] for u in range(4)]
    m = eliminate(m, BS, 32, lambda k: (k // 32, k % 8), lambda k: 32 * ((k // 8) % 4))
    return [regroup(m[i // 4], [32 * c - 32 * (i % 4) for c in range(4)], 32) for i in range(16)]


def peer(axis, index):
    return {axis: index}


CR = 2
XR = NH // CR
CG = 2
XG = NH // CG
HB = BS // 2


def pack_half(top, bot):
    row = lax.broadcasted_iota(I32, (HB, BS), 0)
    lane = lax.broadcasted_iota(I32, (HB, BS), 1)
    return jnp.where((lane >= HB) | (row > lane), top, pltpu.roll(bot, HB, 1))


def diag_tile(top):
    lane = lanes_of()
    sub = subs_of()
    out = jnp.zeros((8, BS), F32)
    for t in range(8):
        out = jnp.where(lane == sub + 8 * t, top[8 * t : 8 * t + 8], out)
    return out


def unpack_half(p, e):
    row = lax.broadcasted_iota(I32, (HB, BS), 0)
    lane = lax.broadcasted_iota(I32, (HB, BS), 1)
    t = jnp.concatenate([p, jnp.zeros((HB, BS), F32)], axis=0).T
    e = jnp.concatenate([e] * 8, axis=0)
    top = jnp.where((lane >= HB) | (row > lane), p, jnp.where(row == lane, e, t[:HB]))
    low = pltpu.roll(jnp.where(row <= lane, p, t[:HB]), HB, 1)
    return jnp.concatenate([top, jnp.where(lane < HB, t[HB:], low)], axis=0)


def body(len_ref, vis_ref, prior_ref, nm_hbm, cp_hbm, um_hbm, cov_ref, amb_ref,
         nm, cp, um, buf, w2, v2, s2, slot, invs, table, ediag, rc, tsum, r1, rd1, part, r2, rd2, piece, blk, eblk, own, seg, call, dall,
         sx, lx, mine, theirs,
         loc, sa, qa, s1, q1, d1s, d1q, s2s, q2, d2s, d2q, s3, q3, d3s, d3q, s4, q4, d4s, d4q, s5, q5, d5s, d5q, s7, q7, d7s, d7q, s6, q6):
    me_g = lax.axis_index("group")
    me_s = lax.axis_index("station")
    me_b = lax.axis_index("bias")
    gp = [lax.rem(me_g + d, NG) for d in (4, 3, 5, 2, 6, 1, 7)]
    sp = [lax.rem(me_s + d, NST) for d in (8, 9, 7, 6, 10, 5, 11, 4, 12, 3, 13, 2, 14, 1, 15)]
    me_c = lax.rem(me_g, 2)
    me_x = me_g // 2
    mate = me_g + 1 - 2 * me_c
    xp = [lax.rem(me_x + d, 4) for d in (2, 1, 3)]
    nm_copy = pltpu.make_async_copy(nm_hbm, nm, loc.at[0])
    nm_copy.start()
    cp_copy = [pltpu.make_async_copy(cp_hbm.at[s], cp.at[s], loc.at[2 + s]) for s in range(S)]
    for c in cp_copy:
        c.start()
    um_copy = pltpu.make_async_copy(um_hbm, um, loc.at[1])
    um_copy.start()
    barrier = pltpu.get_barrier_semaphore()
    for s in sp:
        pl.semaphore_signal(barrier, inc=1, device_id=peer("station", s), device_id_type=MESH)
    for g in gp:
        pl.semaphore_signal(barrier, inc=1, device_id=peer("group", g), device_id_type=MESH)
    pl.semaphore_signal(barrier, inc=1, device_id=peer("bias", 1 - me_b), device_id_type=MESH)

    def remote(src, dst, ss, rs, axis, index):
        return pltpu.make_async_remote_copy(src_ref=src, dst_ref=dst, send_sem=ss, recv_sem=rs, device_id=peer(axis, index), device_id_type=MESH)

    sent = []

    def send(*args):
        copy = remote(*args)
        copy.start()
        sent.append(copy)

    def arrived(*args):
        remote(*args).wait_recv()

    lane = lanes_of()
    sub = subs_of()
    far_first = [lax.rem(XR * (me_s // XR) + XR * d, NH) for d in range(CR - 1, -1, -1)]
    near_first = [lax.rem(XG * (me_s // XG) + XG * d, NH) for d in range(CG)]
    diag_owner = me_g == me_s // 2


    nm_copy.wait()
    to_stations(unpack_rows(nm, 0), buf)
    inverses = invert48(buf, len_ref)
    zeros = jnp.zeros((A, 2 * BS), BF16)
    for s in range(S):
        inv = inverses[s][:, :A]
        invs[s] = inv
        lhs = jnp.concatenate(split2(inv), axis=0)
        keep = lax.broadcasted_iota(I32, (A, BS), 0) < len_ref[s]
        cp_copy[s].wait()
        for j in range(VH):
            w = jnp.where(keep, cp[s, j], 0.0)
            wp = jnp.concatenate(split2(w), axis=1)
            w2[s, j] = wp
            out = jnp.dot(lhs, wp, preferred_element_type=F32)
            out = out[:A] + out[A:]
            sol = out[:, :BS] + out[:, BS:]
            s2[s, j] = jnp.concatenate(split2(sol), axis=1)
            v2[s, j] = jnp.concatenate(split2(w - sol), axis=1)
        w2[s, VH] = zeros
        v2[s, VH] = zeros
        s2[s, VH] = zeros

    def pass_on(i):
        xs = pl.ds(far_first[i], XR)
        arrived(table.at[me_c, :, xs], rc.at[:, xs], sa.at[i], qa.at[i], "group", mate)
        tsum[:, xs] = table[me_c, :, xs] + rc[:, xs]
        for p in xp:
            send(tsum.at[p, xs], r1.at[me_x, xs], s1.at[i, p], q1.at[i, me_x], "group", 2 * p + me_c)

    for i, x0 in enumerate(far_first):
        for dx in range(XR):
            x = x0 + dx
            at = []
            for s in range(S):
                j = jnp.int32(VH)
                for jj in range(VH):
                    j = jnp.where(vis_ref[s, jj] == x, jj, j)
                slot[s, x] = j
                at.append(j)
            wx = jnp.concatenate([w2[s, at[s]] for s in range(S)], axis=0)
            vx = jnp.concatenate([v2[s, at[s]] for s in range(S)], axis=0)
            out = lax.dot_general(wx, vx, (((0,), (0,)), ((), ())), preferred_element_type=F32)
            out = out[:BS] + out[BS:]
            out = out[:, :BS] + out[:, BS:]
            packed = pack_half(out[:HB], out[HB:])
            for g in range(NG):
                table[g % 2, g // 2, x] = packed[8 * g : 8 * g + 8]
            ediag[x] = diag_tile(out[:HB])
        if i == 0:
            pl.semaphore_wait(barrier, NG - 1 + NST - 1 + 1)
        xs = pl.ds(x0, XR)
        send(table.at[1 - me_c, :, xs], rc.at[:, xs], sa.at[i], qa.at[i], "group", mate)
        if i > 0:
            pass_on(i - 1)
    both = jnp.zeros((8, BS), F32)
    for x in range(NH):
        e = ediag[x]
        e = pltpu.roll(e, x % 8, 0) if x % 8 else e
        both = both + (pltpu.roll(e, HB, 1) if x >= 8 else e)
    ediag[NH] = both
    for g in gp:
        send(ediag.at[NH], rd1.at[me_g], d1s.at[g], d1q.at[me_g], "group", g)
    pass_on(CR - 1)

    def to_owner(x):
        return remote(part.at[x], r2.at[me_s], s2s.at[x], q2.at[me_s], "station", x)

    for i, x0 in enumerate(far_first):
        xs = pl.ds(x0, XR)
        total = tsum[me_x, xs]
        for p in xp:
            arrived(tsum.at[p, xs], r1.at[p, xs], s1.at[i, p], q1.at[i, p], "group", 2 * p + me_c)
            total = total + r1[p, xs]
        part[xs] = total
        for dx in range(XR):
            x = x0 + dx

            @pl.when(x != me_s)
            def _():
                to_owner(x).start()

    total = both
    for g in gp:
        arrived(ediag.at[NH], rd1.at[g], d1s.at[g], d1q.at[g], "group", g)
        total = total + rd1[g]
    part[NH] = total

    def diag_to_owner(h):
        return remote(part.at[NH], rd2.at[me_s], d2s.at[h], d2q.at[me_s], "station", 2 * me_g + h)

    for h in range(2):

        @pl.when(2 * me_g + h != me_s)
        def _():
            diag_to_owner(h).start()

    total = part[me_s]
    for s in sp[::-1]:
        arrived(part.at[s], r2.at[s], s2s.at[s], q2.at[s], "station", s)
        total = total + r2[s]
    piece[...] = total
    for g in gp:
        send(piece, blk.at[me_g], s3.at[g], q3.at[me_g], "group", g)
    blk[me_g] = total

    def diag_to_peer(g):
        return remote(piece_e, eblk, d3s.at[g], d3q.at[0], "group", g)

    piece_e = part.at[NH + 1]

    @pl.when(diag_owner)
    def _():
        e = part[NH]
        for s in sp:
            arrived(part.at[NH], rd2.at[s], d2s.at[0], d2q.at[s], "station", s)
            e = e + rd2[s]
        e = pltpu.roll(e, lax.rem(8 - lax.rem(me_s, 8), 8), 0)
        e = pltpu.roll(e, HB * (me_s // 8), 1)
        part[NH + 1] = e
        for g in gp:
            diag_to_peer(g).start()
        eblk[...] = e

    for g in gp:
        arrived(piece, blk.at[g], s3.at[g], q3.at[g], "group", g)

    @pl.when(me_g != me_s // 2)
    def _():
        arrived(piece_e, eblk, d3s.at[0], d3q.at[0], "group", me_s // 2)

    prior = jnp.broadcast_to(prior_ref[...], (8, 128))
    full = unpack_half(jnp.concatenate([blk[g] for g in range(NG)], axis=0), eblk[...])
    mat = [full[8 * i : 8 * i + 8] + jnp.where(lane == sub + 8 * i, prior, 0.0) for i in range(16)]
    mat = invert128(mat)
    top = jnp.concatenate(mat[:8], axis=0)
    packed = pack_half(top, jnp.concatenate(mat[8:], axis=0))
    for g in range(NG):
        own[g] = packed[8 * g : 8 * g + 8]
    own[NG] = diag_tile(top)
    for s in sp:
        send(own.at[me_g], seg.at[me_s], s4.at[s], q4.at[me_s], "station", s)

    def diag_to_station(s):
        return remote(own.at[NG], dall.at[me_x, me_c, lax.rem(me_s, 2)], d4s.at[s], d4q.at[me_s], "station", s)

    @pl.when(diag_owner)
    def _():
        for s in sp:
            diag_to_station(s).start()
        dall[me_x, me_c, lax.rem(me_s, 2)] = own[NG]

    seg[me_s] = own[me_g]
    for i in range(16):
        cov_ref[8 * i : 8 * i + 8, :] = mat[i]
    um_copy.wait()
    to_stations([z.astype(F32) for z in unpack_rows(um, 0)], buf)
    zs = [station(buf, s).astype(BF16) for s in range(S)]
    for h in range(2):
        x = 2 * me_g + h

        @pl.when(x != me_s)
        def _():
            arrived(own.at[NG], dall.at[me_x, me_c, h], d4s.at[0], d4q.at[x], "station", x)

    for i, x0 in enumerate(near_first):
        for dx in range(XG):
            x = x0 + dx

            @pl.when(x != me_s)
            def _():
                arrived(own.at[me_g], seg.at[x], s4.at[0], q4.at[x], "station", x)

        xs = pl.ds(x0, XG)
        for p in xp:
            send(seg.at[xs], call.at[me_c, me_x, xs], s5.at[i, p], q5.at[i, me_x], "group", 2 * p + me_c)
        if i == 0:
            for p in xp:
                send(dall.at[me_x, me_c], dall.at[me_x, me_c], d5s.at[p], d5q.at[me_x], "group", 2 * p + me_c)
    call[me_c, me_x] = seg[...]

    def forward(i):
        xs = pl.ds(near_first[i], XG)
        for p in xp:
            arrived(seg.at[xs], call.at[me_c, p, xs], s5.at[i, p], q5.at[i, p], "group", 2 * p + me_c)
        send(call.at[me_c, :, xs], call.at[me_c, :, xs], s7.at[i], q7.at[i], "group", mate)

    for p in xp:
        arrived(dall.at[p, me_c], dall.at[p, me_c], d5s.at[p], d5q.at[p], "group", 2 * p + me_c)
    send(dall.at[:, me_c], dall.at[:, me_c], d7s, d7q, "group", mate)
    forward(0)
    arrived(dall.at[:, 1 - me_c], dall.at[:, 1 - me_c], d7s, d7q, "group", mate)
    for i, x0 in enumerate(near_first):
        xs = pl.ds(x0, XG)
        if i + 1 < CG:
            forward(i + 1)
        arrived(call.at[1 - me_c, :, xs], call.at[1 - me_c, :, xs], s7.at[i], q7.at[i], "group", mate)
        for dx in range(XG):
            x = x0 + dx
            sg = [s2[s, slot[s, x]] for s in range(S)]
            c = unpack_half(jnp.concatenate([call[g % 2, g // 2, x] for g in range(NG)], axis=0), dall[x // 4, lax.rem(x // 2, 2), lax.rem(x, 2)])
            c2 = jnp.concatenate(split2(c), axis=1)
            c4 = jnp.concatenate([c2, c2], axis=0)
            out = jnp.dot(jnp.concatenate(sg, axis=0), c4, preferred_element_type=F32)
            hi, lo = split2(out[:, :BS] + out[:, BS:])
            n = XG * i + dx
            at = slice(BS * n, BS * n + BS)
            for s in range(S):
                sx[s, :A, at] = sg[s][:, :BS]
                sx[s, A:, at] = sg[s][:, BS:]
                lx[s, :A, at] = hi[A * s : A * s + A]
                lx[s, A:, at] = lo[A * s : A * s + A]
    nt = (((1,), (1,)), ((), ()))
    pad = jnp.zeros((HALF, 64 - A), F32)
    for s in range(S):
        out = lax.dot_general(lx[s], sx[s], nt, preferred_element_type=F32)
        out = out[:A] + out[A:]
        out = out[:, :A] + out[:, A:]
        mine[s] = jnp.concatenate([out[:HALF], pad, out[HALF:], pad], axis=1)
        if s % 4 == 3:
            ss = pl.ds(s - 3, 4)
            send(mine.at[ss], theirs.at[ss], s6.at[s // 4], q6.at[s // 4], "bias", 1 - me_b)
    ri = lax.broadcasted_iota(I32, (A, A), 0)
    ci = lax.broadcasted_iota(I32, (A, A), 1)
    for s in range(S):
        if s % 4 == 0:
            ss = pl.ds(s, 4)
            arrived(mine.at[ss], theirs.at[ss], s6.at[s // 4], q6.at[s // 4], "bias", 1 - me_b)
        keep = (ri < len_ref[s]) & (ci < len_ref[s])
        both = mine[s] + theirs[s]
        both = jnp.concatenate([both[:, :A], pltpu.roll(both, 64, 1)[:, :A]], axis=0)
        cov = jnp.where(keep, invs[s] + both, 0.0)
        hi, lo = split2(cov)
        t = jnp.dot(zs[s], hi, preferred_element_type=F32) + jnp.dot(zs[s], lo, preferred_element_type=F32)
        hi, lo = split2(t)
        o = lax.dot_general(hi, zs[s], nt, preferred_element_type=F32) + lax.dot_general(lo, zs[s], nt, preferred_element_type=F32)
        o = jnp.where(keep, o, 0.0)
        buf[pl.ds(s, A, stride=S), :] = jnp.concatenate([o, jnp.zeros((A, 128 - A), F32)], axis=1)
    acc = [None] * 18
    for i in range(A):
        v, o = divmod(A * i, 128)
        row = buf[8 * i : 8 * i + 8, :]
        row = pltpu.roll(row, o, 1) if o else row
        acc[v] = row if acc[v] is None else jnp.where(lane >= o, row, acc[v])
        if o + A > 128:
            acc[v + 1] = row
    for v in range(18):
        amb_ref[:, 128 * v : 128 * v + 128] = acc[v]
    for copy in sent:
        copy.wait_send()
    for s in sp:
        to_owner(s).wait_send()
    for h in range(2):

        @pl.when(2 * me_g + h != me_s)
        def _():
            diag_to_owner(h).wait_send()

    @pl.when(diag_owner)
    def _():
        for g in gp:
            diag_to_peer(g).wait_send()
        for s in sp:
            diag_to_station(s).wait_send()


def hbm(x):
    return pltpu.with_memory_space_constraint(x, pltpu.HBM)


def local(normal_mat, coupling, lengths, visible, bias_prior, unimod):
    vm = pl.BlockSpec(memory_space=pltpu.VMEM)
    sm = pl.BlockSpec(memory_space=pltpu.SMEM)
    hb = pl.BlockSpec(memory_space=pltpu.HBM)
    dma = pltpu.SemaphoreType.DMA
    vmem = pltpu.VMEM
    slots = vmem((S, VH + 1, A, 2 * BS), BF16)
    wide = vmem((S, 2 * A, NH * BS), BF16)
    rows = vmem((NH, 8, BS), F32)
    quart = vmem((4, NH, 8, BS), F32)
    half = vmem((S, HALF, BS), F32)
    cov, amb = pl.pallas_call(
        body,
        out_shape=(jax.ShapeDtypeStruct((BS, BS), F32), jax.ShapeDtypeStruct((S, A * A), F32)),
        in_specs=[sm, sm, vm, hb, hb, hb],
        out_specs=(vm, vm),
        scratch_shapes=[
            vmem((S, A * A), F32),
            vmem((S, VH, A, BS), F32),
            vmem((S, A * A), I32),
            vmem((A * S, 128), F32),
            slots, slots, slots,
            pltpu.SMEM((S, NH), I32),
            vmem((S, A, A), F32),
            vmem((2, 4, NH, 8, BS), F32),
            vmem((NH + 1, 8, BS), F32),
            quart, quart, quart,
            vmem((NG, 8, BS), F32),
            vmem((NH + 2, 8, BS), F32),
            rows, rows,
            vmem((8, BS), F32),
            vmem((NG, 8, BS), F32),
            vmem((8, BS), F32),
            vmem((NG + 1, 8, BS), F32),
            rows,
            vmem((2, 4, NH, 8, BS), F32),
            vmem((4, 2, 2, 8, BS), F32),
            wide, wide,
            half, half,
            dma((2 + S,)),
            dma((CR,)), dma((CR,)), dma((CR, 4)), dma((CR, 4)), dma((NG,)), dma((NG,)),
            dma((NST,)), dma((NST,)), dma((2,)), dma((NST,)),
            dma((NG,)), dma((NG,)), dma((NG,)), dma((1,)),
            dma((NST,)), dma((NST,)), dma((NST,)), dma((NST,)),
            dma((CG, 4)), dma((CG, 4)), dma((4,)), dma((4,)),
            dma((CG,)), dma((CG,)), dma(()), dma(()),
            dma((2,)), dma((2,)),
        ],
        compiler_params=pltpu.CompilerParams(vmem_limit_bytes=VMEM_LIMIT, collective_id=0, has_side_effects=True),
        name="epoch",
    )(
        hbm(lengths),
        hbm(visible.reshape(S, VH)),
        hbm(bias_prior.reshape(1, BS)),
        hbm(normal_mat),
        hbm(coupling.reshape(S, VH, A, BS)),
        hbm(unimod),
    )
    return (cov.reshape(1, 1, BS, BS), amb)


def solution(mesh):
    return jax.shard_map(
        local,
        mesh=mesh,
        in_specs=(
            P(("station", "group"), None),
            P(("station", "group"), "bias", None, None, None),
            P(("station", "group")),
            P(("station", "group"), "bias", None),
            P("bias", "station", None),
            P(("station", "group"), None),
        ),
        out_specs=(P("bias", "station", None, None), P(("station", "group"), None)),
        check_vma=False,
    )
```
